32 devices in a mesh: narrow: 4 (over y, x), wide: 4 (over z), seq: 2 (over core).
Axes of the slice: x: 2, y: 2, z: 4, core: 2. Of those that a mesh axis runs over, the one named last changes fastest.
Arguments:
- inputs: bfloat16 [8192, 1536], P(('narrow', 'wide', 'seq')), may hold values from -6 to 6
- doc_start: int32 [8192], P(('narrow', 'wide', 'seq')), may hold values from 0 to 8191, as said below
- norm_gain: float32 [1536], replicated, may hold values from 0.5 to 1.5
- qkv_weight: bfloat16 [1536, 4608], P('wide'), may hold values from -0.15625 to 0.15625
- logit_kernel: float32 [16, 6, 11], replicated, may hold values from -1 to 1
- head_mix: float32 [16, 2], replicated, may hold values from 0.2 to 1
- group_gain: float32 [1536], replicated, may hold values from 0.5 to 1.5
- out_weight: bfloat16 [1536, 1536], P('wide'), may hold values from -0.15625 to 0.15625
- feed_gain: float32 [1536], replicated, may hold values from 0.5 to 1.5
- gate_up: bfloat16 [1536, 8192], P('wide'), may hold values from -0.15625 to 0.15625
- down_weight: bfloat16 [4096, 1536], P('wide'), may hold values from -0.09375 to 0.09375
- cotangent: bfloat16 [8192, 1536], P(('narrow', 'wide', 'seq')), may hold values from -6 to 6
Outputs:
- block_out: bfloat16 [8192, 1536], P(('narrow', 'wide', 'seq'))
- grad_input: float32 [8192, 1536], P(('narrow', 'wide', 'seq'))
- grad_norm: float32 [1536], replicated
- grad_qkv: float32 [1536, 4608], P('wide')
- grad_kernel: float32 [16, 6, 11], replicated
- grad_mix: float32 [16, 2], replicated
- grad_group: float32 [1536], replicated
- grad_out: float32 [1536, 1536], P('wide')
- grad_feed: float32 [1536], replicated
- grad_gate: float32 [1536, 8192], P('wide')
- grad_down: float32 [4096, 1536], P('wide')
The draws below stay inside these ranges and needn't reach their ends.
Inputs may be any that keep to these rules, and one draw needn't show every extreme that they name: `doc_start`: each token holds the global index of the first token of its document; documents lie inside aligned rows of 512 tokens, the first starting at the row's first token and the last being the row's last token alone, and in every row one document covers the 17 positions around the row's middle.
All inputs are finite; a program needn't handle non-finite values.
Results may differ from the reference program's by a relative error of at most 0.02.
Values may be sent and summed in bfloat16 or wider, within the bound.
No kernel may reach another device: no remote copies, remote signals or barrier semaphores. Data moves between devices by JAX's collectives and lax.ppermute only.
A program may use at most 320 MiB of HBM per device.

```python
import jax
import jax.numpy as jnp
from jax import lax

D = 1536
HEADS = 16
HEAD_DIM = 96
FF = 4096
QCONV = 6
KCONV = 11
SEQLEN = 512
TOKENS = 8192


def draw_doc_start(key, part):
    key = jax.random.fold_in(key, 7)
    row_total = TOKENS // SEQLEN
    coin_flip = jax.random.randint(key, (row_total, SEQLEN), 0, SEQLEN // 4)
    within = jnp.arange(SEQLEN, dtype=jnp.int32)
    middle = SEQLEN // 2
    quiet_zone = (within >= middle - 8) & (within <= middle + 8)
    is_start = (coin_flip == 0) & jnp.logical_not(quiet_zone)[None, :] | (within == 0)[None, :] | (within == SEQLEN - 1)[None, :]
    global_index = within[None, :] + (jnp.arange(row_total, dtype=jnp.int32) * SEQLEN)[:, None]
    marked = jnp.where(is_start, global_index, 0)
    return lax.cummax(marked, axis=1).reshape(TOKENS).astype(jnp.int32)


def block_levels(key, shape, pieces, least, high):
    loudness = 1.0
    for position, shards_of in pieces:
        steps = jax.random.uniform(jax.random.fold_in(jax.random.fold_in(key, 6), position), (shards_of,), jnp.float32, least / len(pieces), high / len(pieces))
        loudness = loudness * jnp.repeat(jnp.exp(steps), shape[position] // shards_of).reshape((-1,) + (1,) * (len(shape) - 1 - position))
    return loudness


def bell_draw(own_key, extent, scale, limit, cuts=(), kind=jnp.bfloat16):
    entries = jax.random.normal(own_key, extent, jnp.float32) * scale
    if len(cuts) > 0:
        entries = block_levels(own_key, extent, cuts, -0.22, 0.18) * entries
    return jnp.clip(entries, min=-limit, max=limit).astype(kind)


def setup_inputs(seed: int = 0) -> dict:
    seeds = jax.random.split(jax.random.key(seed), 13)
    inputs = bell_draw(seeds[0], (TOKENS, D), 1.0, 6.0, ((0, 32),))
    doc_start = draw_doc_start(jax.random.fold_in(seeds[12], 71), 0)
    norm_gain = jnp.clip(1.0 + 0.1 * jax.random.normal(seeds[2], (D,), jnp.float32), 0.5, 1.5)
    qkv_weight = bell_draw(seeds[3], (D, 3 * D), D ** -0.5, 0.15625, ((0, 4),))
    logit_kernel = bell_draw(seeds[4], (HEADS, QCONV, KCONV), 0.25, 1.0, (), jnp.float32)
    head_mix = jnp.clip(jax.random.uniform(seeds[5], (HEADS, 2), jnp.float32, 0.2, 1.0), 0.2, 1.0)
    group_gain = jnp.clip(1.0 + 0.1 * jax.random.normal(seeds[6], (D,), jnp.float32), 0.5, 1.5)
    out_weight = bell_draw(seeds[7], (D, D), D ** -0.5, 0.15625, ((0, 4),))
    feed_gain = jnp.clip(1.0 + 0.1 * jax.random.normal(seeds[8], (D,), jnp.float32), 0.5, 1.5)
    gate_up = bell_draw(seeds[9], (D, 2 * FF), D ** -0.5, 0.15625, ((0, 4),))
    down_weight = bell_draw(seeds[10], (FF, D), FF ** -0.5, 0.09375, ((0, 4),))
    cotangent = bell_draw(seeds[11], (TOKENS, D), 1.0, 6.0, ((0, 32),))
    return {"inputs": inputs, "doc_start": doc_start, "norm_gain": norm_gain, "qkv_weight": qkv_weight, "logit_kernel": logit_kernel, "head_mix": head_mix, "group_gain": group_gain, "out_weight": out_weight, "feed_gain": feed_gain, "gate_up": gate_up, "down_weight": down_weight, "cotangent": cotangent}


@jax.custom_vjp
def low(v):
    return lax.optimization_barrier(v.astype(jnp.bfloat16)).astype(jnp.float32)

@jax.custom_vjp
def low_back(v):
    return v

def low_keep(v):
    return (low(v), None)

def low_pass(kept, grad):
    return (grad,)

def back_keep(v):
    return (v, None)

def back_low(kept, grad):
    return (low(grad),)
low.defvjp(low_keep, low_pass)
low_back.defvjp(back_keep, back_low)

def rms_norm(values, scale_row):
    return values * lax.rsqrt(lax.optimization_barrier(jnp.mean(values * values, axis=-1, keepdims=True)) + 1e-06) * scale_row

def group_norm(values, scale_row):
    centered = values - lax.optimization_barrier(jnp.mean(values, axis=-1, keepdims=True))
    spread = lax.optimization_barrier(jnp.mean(centered * centered, axis=-1, keepdims=True))
    normal = centered * lax.rsqrt(spread + 1e-05)
    return normal.reshape(values.shape[0], -1) * scale_row

def swiglu(joined):
    half_cols = joined.shape[1] // 2
    gating = joined[:, :half_cols]
    upward = joined[:, half_cols:]
    return gating / (1.0 + jnp.exp(-gating)) * upward

def shift_keys(slab_in, offset):
    length = slab_in.shape[-1]
    if offset > 0:
        return jnp.pad(slab_in[..., :length - offset], ((0, 0), (0, 0), (offset, 0)))
    if offset < 0:
        return jnp.pad(slab_in[..., -offset:], ((0, 0), (0, 0), (0, -offset)))
    return slab_in

def convolve(scores, kernel, out_pos, out_start, key_pos):
    query_taps = kernel.shape[1]
    key_taps = kernel.shape[2]
    margin = query_taps - 1
    half_taps = (key_taps - 1) // 2
    out_count = out_pos.shape[0]
    summed = jnp.zeros((scores.shape[0], out_count, scores.shape[2]), jnp.float32)
    for tap_q in range(query_taps):
        rows_at = scores[:, margin - tap_q:margin - tap_q + out_count, :]
        source = out_pos - tap_q
        inside = (source >= out_start)[:, None] & (key_pos[None, :] >= out_start[:, None]) & (key_pos[None, :] <= source[:, None])
        masked = jnp.where(inside[None], rows_at, 0.0)
        for tap_k in range(key_taps):
            shifted = shift_keys(masked, tap_k - half_taps)
            summed = summed + kernel[:, tap_q, tap_k][:, None, None] * shifted
    return summed

def combine_heads(mix_group, weights):
    return jnp.stack([mix_group[0, 0] * weights[0] + mix_group[0, 1] * weights[1], mix_group[1, 0] * weights[0] + mix_group[1, 1] * weights[1]])

def ref_attend(q_group, k_group, v_group, kernel, mix_group, out_pos, out_start, key_pos):
    highest_p = lax.Precision.HIGHEST
    scores = low_back(jnp.einsum('qhd,khd->hqk', q_group, k_group, precision=highest_p) * HEAD_DIM ** (-0.5))
    convolved = convolve(scores, kernel, out_pos, out_start, key_pos)
    allowed = (key_pos[None, :] >= out_start[:, None]) & (key_pos[None, :] <= out_pos[:, None])
    logits = jnp.where(allowed[None], convolved, -1e+30)
    highest = lax.optimization_barrier(jnp.max(logits, axis=-1, keepdims=True))
    raised = jnp.exp(logits - highest)
    weights = raised / lax.optimization_barrier(jnp.sum(raised, axis=-1, keepdims=True))
    mixed_low = low(combine_heads(mix_group, weights))
    return jnp.einsum('hqk,khd->qhd', mixed_low, v_group, precision=highest_p)

def reference(inputs, doc_start, norm_gain, qkv_weight, logit_kernel, head_mix, group_gain, out_weight, feed_gain, gate_up, down_weight, cotangent):
    highest_p = lax.Precision.HIGHEST
    floats = tuple((tensor.astype(jnp.float32) for tensor in (inputs, norm_gain, qkv_weight, logit_kernel, head_mix, group_gain, out_weight, feed_gain, gate_up, down_weight)))
    row_total = TOKENS // SEQLEN
    group_total = HEADS // 2

    def forward(inputs_f, norm_gain, qkv_weight, logit_kernel, head_mix, group_gain, out_weight, feed_gain, gate_up, down_weight):
        normed = low(rms_norm(inputs_f, norm_gain))
        projected = low(low_back(jnp.dot(normed, qkv_weight, precision=highest_p)))

        def to_groups(matrix):
            return jnp.moveaxis(matrix.reshape(row_total, SEQLEN, group_total, 2, HEAD_DIM), 2, 1)
        row_queries = to_groups(projected[:, :D])
        row_keys = to_groups(projected[:, D:2 * D])
        row_values = to_groups(projected[:, 2 * D:])
        kernels = logit_kernel.reshape(group_total, 2, QCONV, KCONV)
        mix_groups = head_mix.reshape(group_total, 2, 2)
        starts = doc_start.reshape(row_total, SEQLEN)

        def one_row(row_items):
            queries_r, keys_r, values_r, start_r, row_number = row_items
            positions = row_number * SEQLEN + jnp.arange(SEQLEN, dtype=jnp.int32)

            def one_group(group_items):
                q_group, k_group, v_group, kernel, mix_group = group_items
                padded = jnp.concatenate([jnp.zeros((QCONV - 1, 2, HEAD_DIM), jnp.float32), q_group], 0)
                return ref_attend(padded, k_group, v_group, kernel, mix_group, positions, start_r, positions)
            return lax.map(jax.checkpoint(one_group), (queries_r, keys_r, values_r, kernels, mix_groups))
        attended = lax.map(one_row, (row_queries, row_keys, row_values, starts, jnp.arange(row_total, dtype=jnp.int32)))
        attended = low_back(jnp.moveaxis(attended, 1, 2).reshape(TOKENS, HEADS, HEAD_DIM))
        grouped = low(group_norm(attended, group_gain))
        branch = low_back(jnp.dot(grouped, out_weight, precision=highest_p))
        residual = inputs_f + branch
        normed_ffn = low(rms_norm(residual, feed_gain))
        gate_vals = low_back(jnp.dot(normed_ffn, gate_up, precision=highest_p))
        hidden = low(swiglu(gate_vals))
        branch_ffn = low_back(jnp.dot(hidden, down_weight, precision=highest_p))
        return residual + branch_ffn
    outputs, pullback = jax.vjp(forward, *floats)
    gradients = pullback(cotangent.astype(jnp.float32))
    return (outputs.astype(jnp.bfloat16), gradients[0], gradients[1], gradients[2], gradients[3], gradients[4], gradients[5], gradients[6], gradients[7], gradients[8], gradients[9])
```

```python
import functools
import jax
import jax.numpy as jnp
from jax import lax
from jax.experimental import pallas as pl
from jax.experimental.pallas import tpu as pltpu

LANES = 128
EDGE = 64
TOP = 16


def tap_bands(kernel, scaling):
    heads, taps_q, taps_k = kernel.shape
    half = (taps_k - 1) // 2
    row = jnp.arange(2 * LANES)[:, None]
    col = jnp.arange(LANES)[None, :]
    forth = col - row + EDGE + half
    back = row - col - EDGE + half
    spread = jnp.zeros((heads, 2 * LANES, taps_q, LANES), jnp.float32)
    spread_back = jnp.zeros((heads, taps_q, 2 * LANES, LANES), jnp.float32)
    for tap in range(taps_k):
        spread = spread + jnp.where((forth == tap)[None, :, None, :], kernel[:, None, :, tap, None], 0.0)
        spread_back = spread_back + jnp.where(
            (back == tap)[None, None, :, :], kernel[:, :, tap, None, None], 0.0
        )
    spread = spread.reshape(heads, 2 * LANES, taps_q * LANES) * scaling
    high = spread.astype(jnp.bfloat16)
    low = (spread - high.astype(jnp.float32)).astype(jnp.bfloat16)
    forward = jnp.concatenate([high, high, low], 1)
    backward = spread_back.reshape(heads, taps_q * 2 * LANES, LANES).astype(jnp.bfloat16)
    return forward, backward


def masked_scores(q_blk, keys, since, first_row):
    scores = lax.dot_general(q_blk, keys, (((1,), (1,)), ((), ())), preferred_element_type=jnp.float32)
    rows = first_row + lax.broadcasted_iota(jnp.int32, scores.shape, 0)
    back = rows + EDGE - lax.broadcasted_iota(jnp.int32, scores.shape, 1)
    limit = jnp.concatenate([since] * (scores.shape[1] // LANES), 1)
    return jnp.where((back >= 0) & (back <= limit), scores, 0.0)


def forward_kernel(
    taps_q, head_size, mix_ref, proj_ref, since_ref, taps_ref, gain_ref,
    att_ref, grouped_ref, weights_ref, keys_pad, s_high, s_low, spread,
):
    seq_len = proj_ref.shape[0]
    blocks = seq_len // LANES
    keys_pad[...] = jnp.zeros_like(keys_pad)
    s_high[...] = jnp.zeros_like(s_high)
    s_low[...] = jnp.zeros_like(s_low)

    def one_head(head, carry):
        lane = pl.multiple_of(head * LANES, LANES)
        lane_k = pl.multiple_of((head + 2) * LANES, LANES)
        keys_pad[EDGE : EDGE + seq_len, :] = proj_ref[:, pl.ds(lane_k, LANES)]
        for qi in range(blocks):
            first = qi * LANES
            width = (qi + 2) * LANES
            scores = masked_scores(
                proj_ref[first : first + LANES, pl.ds(lane, LANES)],
                keys_pad[:width, :],
                since_ref[first : first + LANES, :],
                first,
            )
            high = scores.astype(jnp.bfloat16)
            s_high[TOP + first : TOP + first + LANES, :width] = high
            s_low[TOP + first : TOP + first + LANES, :width] = (scores - high.astype(jnp.float32)).astype(jnp.bfloat16)
        for m in range(blocks):
            first = m * LANES
            count = seq_len - first
            high = s_high[first:, first : first + 2 * LANES]
            left = jnp.concatenate([high, s_low[first:, first : first + 2 * LANES], high], 1)
            spread[first:, :] = jnp.dot(left, taps_ref[head], preferred_element_type=jnp.float32)
            since = since_ref[first:, :]
            logits = spread[TOP + first :, :LANES]
            for tap in range(1, taps_q):
                moved = spread[TOP + first - tap : TOP + seq_len - tap, tap * LANES : (tap + 1) * LANES]
                logits = logits + jnp.where(since >= tap, moved, 0.0)
            weights_ref[head, first:, first : first + LANES] = logits
        for qi in range(blocks):
            first = qi * LANES
            width = (qi + 1) * LANES
            logits = weights_ref[head, first : first + LANES, :width]
            rows = first + lax.broadcasted_iota(jnp.int32, logits.shape, 0)
            back = rows - lax.broadcasted_iota(jnp.int32, logits.shape, 1)
            limit = jnp.concatenate([since_ref[first : first + LANES, :]] * (qi + 1), 1)
            logits = jnp.where((back >= 0) & (back <= limit), logits, -1e30)
            raised = jnp.exp(logits - jnp.max(logits, axis=1, keepdims=True))
            weights_ref[head, first : first + LANES, :width] = raised / jnp.sum(raised, axis=1, keepdims=True)
        return carry

    lax.fori_loop(0, 2, one_head, 0)
    real = lax.broadcasted_iota(jnp.int32, (LANES, LANES), 1) < head_size
    for qi in range(blocks):
        first = qi * LANES
        width = (qi + 1) * LANES
        low = weights_ref[0, first : first + LANES, :width]
        upp = weights_ref[1, first : first + LANES, :width]
        for head in range(2):
            mixed = (mix_ref[head, 0] * low + mix_ref[head, 1] * upp).astype(jnp.bfloat16)
            cols = slice(head * LANES, (head + 1) * LANES)
            att = jnp.dot(
                mixed, proj_ref[:width, (4 + head) * LANES : (5 + head) * LANES], preferred_element_type=jnp.float32
            )
            att_ref[first : first + LANES, cols] = att
            normal, _ = normalize(att, real, head_size)
            grouped_ref[first : first + LANES, cols] = (normal * gain_ref[:, cols]).astype(jnp.bfloat16)


def normalize(att, real, head_size):
    mean = jnp.sum(att, axis=1, keepdims=True) * (1.0 / head_size)
    centered = jnp.where(real, att - mean, 0.0)
    spread = jnp.sum(centered * centered, axis=1, keepdims=True) * (1.0 / head_size)
    scale = lax.rsqrt(spread + 1e-05)
    return centered * scale, scale


def attend_row(proj, since, mix, taps_forward, gain_pad, taps_q, head_size):
    seq_len = proj.shape[0]
    full = seq_len + 2 * EDGE
    return pl.pallas_call(
        functools.partial(forward_kernel, taps_q, head_size),
        out_shape=(
            jax.ShapeDtypeStruct((seq_len, 2 * LANES), jnp.float32),
            jax.ShapeDtypeStruct((seq_len, 2 * LANES), jnp.bfloat16),
            jax.ShapeDtypeStruct((2, seq_len, seq_len), jnp.float32),
        ),
        in_specs=[pl.BlockSpec(memory_space=pltpu.SMEM)] + [pl.BlockSpec(memory_space=pltpu.VMEM)] * 4,
        out_specs=(pl.BlockSpec(memory_space=pltpu.VMEM),) * 3,
        scratch_shapes=[
            pltpu.VMEM((full, LANES), jnp.bfloat16),
            pltpu.VMEM((TOP + seq_len, full), jnp.bfloat16),
            pltpu.VMEM((TOP + seq_len, full), jnp.bfloat16),
            pltpu.VMEM((TOP + seq_len, taps_q * LANES), jnp.float32),
        ],
        compiler_params=pltpu.CompilerParams(vmem_limit_bytes=40 * 1024 * 1024),
        cost_estimate=pl.CostEstimate(flops=10_000_000_000, bytes_accessed=8_000_000, transcendentals=600_000),
        name="attend_row",
    )(mix, proj, since, taps_forward, gain_pad)


def backward_kernel(
    taps_q, taps_k, head_size, scaling, mix_ref, proj_ref, since_ref, taps_ref, gain_ref, att_ref, weights_ref, grad_ref,
    out_ref, small_ref, tap_ref,
    keys_pad, grad_att, conv_grad, shifted, s_low, s_grad, since_pad,
):
    seq_len = proj_ref.shape[0]
    blocks = seq_len // LANES
    half = (taps_k - 1) // 2
    full = seq_len + 2 * EDGE
    keys_pad[...] = jnp.zeros_like(keys_pad)
    s_low[...] = jnp.zeros_like(s_low)
    s_grad[...] = jnp.zeros_like(s_grad)
    shifted[...] = jnp.zeros_like(shifted)
    conv_grad[...] = jnp.zeros_like(conv_grad)
    since_pad[:seq_len, :] = since_ref[...]
    since_pad[seq_len:, :] = jnp.zeros((8, LANES), jnp.int32)
    small_ref[...] = jnp.zeros_like(small_ref)

    real = lax.broadcasted_iota(jnp.int32, (LANES, LANES), 1) < head_size
    for head in range(2):
        cols = slice(head * LANES, (head + 1) * LANES)
        group_sum = jnp.zeros((1, LANES), jnp.float32)
        for qi in range(blocks):
            rows = slice(qi * LANES, (qi + 1) * LANES)
            normal, scale = normalize(att_ref[rows, cols], real, head_size)
            grad = grad_ref[rows, cols]
            group_sum = group_sum + jnp.sum(grad * normal, axis=0, keepdims=True)
            lift = grad * gain_ref[:, cols]
            mean = jnp.sum(lift, axis=1, keepdims=True) * (1.0 / head_size)
            along = jnp.sum(lift * normal, axis=1, keepdims=True) * (1.0 / head_size)
            grad_att[rows, cols] = jnp.where(real, scale * (lift - mean - normal * along), 0.0).astype(jnp.bfloat16)
        small_ref[head : head + 1, :] = group_sum

    sums = [[jnp.zeros((1, LANES), jnp.float32) for _ in range(2)] for _ in range(2)]
    grad_v = [[], []]
    for qi in range(blocks):
        first = qi * LANES
        width = (qi + 1) * LANES
        rows = slice(first, first + LANES)
        maps = [weights_ref[k, rows, :width] for k in range(2)]
        grad_mixed = []
        for head in range(2):
            cols = slice(head * LANES, (head + 1) * LANES)
            values = proj_ref[:width, (4 + head) * LANES : (5 + head) * LANES]
            gm = lax.dot_general(
                grad_att[rows, cols], values, (((1,), (1,)), ((), ())), preferred_element_type=jnp.float32
            )
            grad_mixed.append(gm)
        for head in range(2):
            for k in range(2):
                part = jnp.sum(grad_mixed[head] * maps[k], axis=0, keepdims=True)
                for b in range(qi + 1):
                    sums[head][k] = sums[head][k] + part[:, b * LANES : (b + 1) * LANES]
        for k in range(2):
            grad_w = mix_ref[0, k] * grad_mixed[0] + mix_ref[1, k] * grad_mixed[1]
            inner = jnp.sum(grad_w * maps[k], axis=1, keepdims=True)
            conv_grad[k, rows, :width] = maps[k] * (grad_w - inner)
    for head in range(2):
        for k in range(2):
            small_ref[2 + 2 * head + k : 3 + 2 * head + k, :] = sums[head][k]
        cols = slice(head * LANES, (head + 1) * LANES)
        for kb in range(blocks):
            first = kb * LANES
            mixed = (
                mix_ref[head, 0] * weights_ref[0, first:, first : first + LANES]
                + mix_ref[head, 1] * weights_ref[1, first:, first : first + LANES]
            ).astype(jnp.bfloat16)
            out_ref[first : first + LANES, (4 + head) * LANES : (5 + head) * LANES] = lax.dot_general(
                mixed, grad_att[first:, cols], (((0,), (0,)), ((), ())), preferred_element_type=jnp.float32
            ).astype(jnp.bfloat16)

    def one_head(head, carry):
        lane = pl.multiple_of(head * LANES, LANES)
        lane_k = pl.multiple_of((head + 2) * LANES, LANES)
        keys_pad[EDGE : EDGE + seq_len, :] = proj_ref[:, pl.ds(lane_k, LANES)]
        for qi in range(blocks):
            first = qi * LANES
            width = (qi + 2) * LANES
            scores = masked_scores(
                proj_ref[first : first + LANES, pl.ds(lane, LANES)],
                keys_pad[:width, :],
                since_ref[first : first + LANES, :],
                first,
            )
            s_low[TOP + first : TOP + first + LANES, :width] = scores.astype(jnp.bfloat16)
            reach = min(width, seq_len)
            for tap in range(taps_q):
                moved = conv_grad[head, first + tap : first + tap + LANES, :reach]
                if tap > 0:
                    limit = since_pad[first + tap : first + tap + LANES, :]
                    limit = jnp.concatenate([limit] * (reach // LANES), 1)
                    moved = jnp.where(limit >= tap, moved, 0.0)
                shifted[tap, TOP + first : TOP + first + LANES, LANES : LANES + reach] = moved.astype(jnp.bfloat16)
        for m in range(blocks + 1):
            first = max(m - 1, 0) * LANES
            left = jnp.concatenate(
                [shifted[tap, TOP + first :, m * LANES : (m + 2) * LANES] for tap in range(taps_q)], 1
            )
            grad = jnp.dot(left, taps_ref[head], preferred_element_type=jnp.float32)
            rows = first + lax.broadcasted_iota(jnp.int32, grad.shape, 0)
            back = rows + EDGE - m * LANES - lax.broadcasted_iota(jnp.int32, grad.shape, 1)
            keep = (back >= 0) & (back <= since_ref[first:, :])
            s_grad[first:, m * LANES : (m + 1) * LANES] = jnp.where(keep, grad, 0.0).astype(jnp.bfloat16)
        total = jnp.zeros((2 * LANES, taps_q * LANES), jnp.float32)
        for m in range(blocks):
            first = m * LANES
            right = jnp.concatenate(
                [shifted[tap, first:, (m + 1) * LANES : (m + 2) * LANES] for tap in range(taps_q)], 1
            )
            total = total + lax.dot_general(
                s_low[first:, first : first + 2 * LANES], right, (((0,), (0,)), ((), ())),
                preferred_element_type=jnp.float32,
            )
        ridge = lax.broadcasted_iota(jnp.int32, (2 * LANES, LANES), 1) - lax.broadcasted_iota(
            jnp.int32, (2 * LANES, LANES), 0
        )
        for tap_k in range(taps_k):
            on = ridge == tap_k - EDGE - half
            for tap in range(taps_q):
                line = jnp.where(on, total[:, tap * LANES : (tap + 1) * LANES], 0.0)
                tap_ref[head, tap * taps_k + tap_k : tap * taps_k + tap_k + 1, :] = jnp.sum(line, axis=0, keepdims=True)
        for qi in range(blocks):
            first = qi * LANES
            width = (qi + 2) * LANES
            grad_q = jnp.dot(
                s_grad[first : first + LANES, :width], keys_pad[:width, :], preferred_element_type=jnp.float32
            )
            out_ref[first : first + LANES, pl.ds(lane, LANES)] = (grad_q * scaling).astype(jnp.bfloat16)
        for kb in range(blocks):
            first = kb * LANES
            grad_k = lax.dot_general(
                s_grad[first:, first + EDGE : first + EDGE + LANES],
                proj_ref[first:, pl.ds(lane, LANES)],
                (((0,), (0,)), ((), ())),
                preferred_element_type=jnp.float32,
            )
            out_ref[first : first + LANES, pl.ds(lane_k, LANES)] = (grad_k * scaling).astype(jnp.bfloat16)
        return carry

    lax.fori_loop(0, 2, one_head, 0)


def attend_row_back(proj, since, mix, taps_backward, gain_pad, att, weights, grad_grouped, taps_q, taps_k, head_size):
    seq_len = proj.shape[0]
    full = seq_len + 2 * EDGE
    return pl.pallas_call(
        functools.partial(backward_kernel, taps_q, taps_k, head_size, head_size ** (-0.5)),
        out_shape=(
            jax.ShapeDtypeStruct((seq_len, 6 * LANES), jnp.bfloat16),
            jax.ShapeDtypeStruct((8, LANES), jnp.float32),
            jax.ShapeDtypeStruct((2, taps_q * taps_k, LANES), jnp.float32),
        ),
        in_specs=[pl.BlockSpec(memory_space=pltpu.SMEM)] + [pl.BlockSpec(memory_space=pltpu.VMEM)] * 7,
        out_specs=(pl.BlockSpec(memory_space=pltpu.VMEM),) * 3,
        scratch_shapes=[
            pltpu.VMEM((full, LANES), jnp.bfloat16),
            pltpu.VMEM((seq_len, 2 * LANES), jnp.bfloat16),
            pltpu.VMEM((2, seq_len + 8, seq_len), jnp.float32),
            pltpu.VMEM((taps_q, TOP + seq_len, seq_len + 2 * LANES), jnp.bfloat16),
            pltpu.VMEM((TOP + seq_len, full), jnp.bfloat16),
            pltpu.VMEM((seq_len, full), jnp.bfloat16),
            pltpu.VMEM((seq_len + 8, LANES), jnp.int32),
        ],
        compiler_params=pltpu.CompilerParams(vmem_limit_bytes=48 * 1024 * 1024),
        cost_estimate=pl.CostEstimate(flops=15_000_000_000, bytes_accessed=8_000_000, transcendentals=0),
        name="attend_row_back",
    )(mix, proj, since, taps_backward, gain_pad, att, weights, grad_grouped)


from jax.sharding import PartitionSpec as P

PLANE = ("narrow", "seq")
SWAP = [(0, 1), (1, 0)]


def seq_swap(array):
    return lax.ppermute(array, "seq", SWAP)


def x_swap(array):
    return lax.ppermute(array, "narrow", [(0, 1), (1, 0), (2, 3), (3, 2)])


def y_swap(array):
    return lax.ppermute(array, "narrow", [(0, 2), (2, 0), (1, 3), (3, 1)])


def joint_move(array, pairs):
    wide = lax.axis_size("wide")
    return lax.ppermute(array, ("narrow", "wide"), [(a * wide + b, c * wide + d) for (a, b), (c, d) in pairs])


def ordered(own, other):
    first = lax.axis_index("seq") == 0
    return jnp.concatenate([jnp.where(first, own, other), jnp.where(first, other, own)], 0)


def gather_plane(own):
    half = own.shape[0] // 2
    from_x = x_swap(own)
    from_y = y_swap(own)
    own_pair = ordered(own, seq_swap(own))
    corner = jnp.concatenate([y_swap(from_x[:half]), x_swap(from_y[half:])], 0)
    x_pair = ordered(from_x, seq_swap(from_x))
    y_pair = ordered(from_y, seq_swap(from_y))
    return [own_pair, x_pair, y_pair, ordered(corner, seq_swap(corner))]


def scatter_plane(parts):
    count = parts[0].shape[0] // 2
    core = lax.axis_index("seq")

    def pair(part):
        mine = lax.dynamic_slice_in_dim(part, core * count, count, 0)
        theirs = lax.dynamic_slice_in_dim(part, (1 - core) * count, count, 0)
        return mine.astype(jnp.float32) + seq_swap(theirs.astype(jnp.bfloat16)).astype(jnp.float32)

    cut = count // 2
    corner = pair(parts[3])
    to_y = x_swap(corner[:cut].astype(jnp.bfloat16)).astype(jnp.float32)
    to_x = y_swap(corner[cut:].astype(jnp.bfloat16)).astype(jnp.float32)
    at_x = pair(parts[1])
    at_y = pair(parts[2])
    at_x = jnp.concatenate([at_x[:cut], at_x[cut:] + to_x], 0).astype(jnp.bfloat16)
    at_y = jnp.concatenate([at_y[:cut] + to_y, at_y[cut:]], 0).astype(jnp.bfloat16)
    return pair(parts[0]) + x_swap(at_x).astype(jnp.float32) + y_swap(at_y).astype(jnp.float32)


def ring_next(array):
    count = lax.axis_size("wide")
    return lax.ppermute(array, "wide", [(i, (i + 1) % count) for i in range(count)])


def gather_wide(piece, shape_piece=lambda a: a):
    count = lax.axis_size("wide")
    place = lax.axis_index("wide")
    if count > 4:
        return shape_piece(lax.all_gather(piece, "wide", axis=0, tiled=True))
    rows = piece.shape[0]
    current = piece
    whole = None
    for step in range(count):
        shaped = shape_piece(current)
        if whole is None:
            whole = jnp.zeros((count * rows,) + shaped.shape[1:], shaped.dtype)
        whole = lax.dynamic_update_slice_in_dim(whole, shaped, ((place - step) % count) * rows, 0)
        if step < count - 1:
            current = ring_next(current)
    return whole


def scatter_wide(whole):
    count = lax.axis_size("wide")
    place = lax.axis_index("wide")
    if count > 4:
        return lax.psum_scatter(whole.astype(jnp.bfloat16), "wide", scatter_dimension=0, tiled=True).astype(jnp.float32)
    rows = whole.shape[0] // count

    def block(step):
        return lax.dynamic_slice_in_dim(whole, ((place - step) % count) * rows, rows, 0)

    total = block(1)
    for step in range(2, count + 1):
        total = ring_next(total.astype(jnp.bfloat16)).astype(jnp.float32) + block(step)
    return total


def gather_out(out_weight, group_rows):
    wide = lax.axis_size("wide")
    core = lax.axis_index("seq")
    line = lax.axis_index("narrow")
    place = lax.axis_index("wide")
    if wide != 4:
        whole = lax.all_gather(out_weight, "wide", axis=0, tiled=True)
        return lax.dynamic_slice_in_dim(whole, (2 * line + core) * group_rows, group_rows, 0)
    held = lax.dynamic_slice_in_dim(out_weight, core * group_rows, group_rows, 0)
    came = joint_move(held, [((n, n), (n, n ^ 2)) for n in range(4)])
    held = jnp.where(place == line, held, came)
    came = joint_move(held, [((n, n ^ k), (n, n ^ k ^ 1)) for n in range(4) for k in (0, 2)])
    return jnp.where((place ^ line) & 1 == 0, held, came)


def scatter_out(term):
    wide = lax.axis_size("wide")
    place = lax.axis_index("wide")
    line = lax.axis_index("narrow")
    if wide != 4:
        whole = lax.all_gather(term.astype(jnp.bfloat16), PLANE, axis=0, tiled=True)
        return lax.psum_scatter(whole, "wide", scatter_dimension=0, tiled=True).astype(jnp.float32)
    low = term.astype(jnp.bfloat16)
    came = joint_move(low, [((n, n ^ k ^ 1), (n, n ^ k)) for n in range(4) for k in (0, 2)])
    term = term + came.astype(jnp.float32)
    came = joint_move(term.astype(jnp.bfloat16), [((n, n ^ 2), (n, n)) for n in range(4)])
    held = (term + came.astype(jnp.float32)).astype(jnp.bfloat16)
    came = joint_move(held, [((z, z), (z ^ 1, z)) for z in range(4)])
    held = jnp.where(place == line, held, came)
    came = joint_move(held, [((z ^ k, z), (z ^ k ^ 2, z)) for z in range(4) for k in (0, 1)])
    held = jnp.where((place ^ line) & 2 == 0, held, came)
    return ordered(held, seq_swap(held)).astype(jnp.float32)


def pad_heads(array, head_size):
    heads = array.shape[1] // head_size
    split = array.reshape(array.shape[0], heads, head_size)
    return jnp.pad(split, ((0, 0), (0, 0), (0, LANES - head_size))).reshape(array.shape[0], heads * LANES)


def unpad_heads(array, head_size):
    heads = array.shape[1] // LANES
    return array.reshape(array.shape[0], heads, LANES)[:, :, :head_size].reshape(array.shape[0], heads * head_size)


def times(left, right):
    return jnp.dot(left, right, preferred_element_type=jnp.float32)


def times_back(left, right):
    return lax.dot_general(left, right, (((1,), (1,)), ((), ())), preferred_element_type=jnp.float32)


def row_product(left, right):
    return lax.dot_general(left, right, (((0,), (0,)), ((), ())), preferred_element_type=jnp.float32)


def norm_scale(values):
    return lax.rsqrt(jnp.mean(values * values, axis=-1, keepdims=True) + 1e-06)


def norm_back(values, scale, gain, grad):
    lift = grad * gain
    along = jnp.mean(lift * values, axis=-1, keepdims=True)
    return scale * lift - values * (scale * scale * scale * along), jnp.sum(grad * values * scale, axis=0)


def on_device(
    inputs,
    doc_start,
    norm_gain,
    qkv_weight,
    logit_kernel,
    head_mix,
    group_gain,
    out_weight,
    feed_gain,
    gate_up,
    down_weight,
    cotangent,
):
    tokens_dev, width = inputs.shape
    head_count, taps_q, taps_k = logit_kernel.shape
    head_size = width // head_count
    group_cols = 2 * head_size
    cores = lax.axis_size(PLANE)
    wide = lax.axis_size("wide")
    line = lax.axis_index("narrow")
    part = lax.axis_index(PLANE)
    hidden_size = gate_up.shape[1] // 2
    chunk = hidden_size // (wide * cores)
    scaling = head_size ** (-0.5)

    first_pos = lax.axis_index(("narrow", "wide", "seq")) * tokens_dev
    since_own = first_pos + jnp.arange(tokens_dev, dtype=jnp.int32) - doc_start
    since_all = lax.all_gather(since_own, PLANE, axis=0, tiled=True).reshape(cores // 2, 2 * tokens_dev)

    inputs_f = inputs.astype(jnp.float32)
    scale_in = norm_scale(inputs_f)
    normed = (inputs_f * scale_in * norm_gain).astype(jnp.bfloat16)
    normed_rows = gather_plane(normed)

    qkv_piece = lax.dynamic_index_in_dim(
        qkv_weight.reshape(qkv_weight.shape[0], 3, cores, group_cols), part, 2, keepdims=False
    ).reshape(qkv_weight.shape[0], 3 * group_cols)
    qkv_own = gather_wide(qkv_piece, lambda a: pad_heads(a, head_size))
    out_own = gather_out(out_weight, group_cols)
    out_own = jnp.pad(
        out_own.reshape(2, head_size, width), ((0, 0), (0, LANES - head_size), (0, 0))
    ).reshape(2 * LANES, width)
    gate_piece = lax.dynamic_index_in_dim(
        gate_up.reshape(gate_up.shape[0], 2, wide, cores, chunk), part, 3, keepdims=False
    ).reshape(gate_up.shape[0], 2 * wide * chunk)
    gate_own = gather_wide(gate_piece)
    down_own = gather_wide(lax.dynamic_slice_in_dim(down_weight, part * chunk, chunk, 0))
    cotangent_rows = gather_plane(cotangent)

    kernels = lax.dynamic_slice_in_dim(logit_kernel, 2 * part, 2, 0)
    mix = lax.dynamic_slice_in_dim(head_mix, 2 * part, 2, 0)
    taps_forward, taps_backward = tap_bands(kernels, scaling)
    gain_pad = pad_heads(lax.dynamic_slice_in_dim(group_gain, part * group_cols, group_cols, 0)[None], head_size)

    rows = []
    branch_parts = []
    for k in range(4):
        since = jnp.broadcast_to(
            lax.dynamic_index_in_dim(since_all, line ^ k, 0, keepdims=False)[:, None], (2 * tokens_dev, LANES)
        )
        projected = times(normed_rows[k], qkv_own).astype(jnp.bfloat16)
        attended, grouped, weights = attend_row(projected, since, mix, taps_forward, gain_pad, taps_q, head_size)
        branch_parts.append(times(grouped, out_own))
        rows.append((projected, since, attended, grouped, weights))
    residual = inputs_f + scatter_plane(branch_parts)
    scale_mid = norm_scale(residual)
    normed_ffn = (residual * scale_mid * feed_gain).astype(jnp.bfloat16)
    ffn_rows = gather_plane(normed_ffn)

    gate_cols = wide * chunk
    gate_w, up_w = gate_own[:, :gate_cols], gate_own[:, gate_cols:]
    hidden_rows, gate_grad_rows, up_grad_rows, back_parts, ffn_parts = [], [], [], [], []
    for k in range(4):
        gating = times(ffn_rows[k], gate_w)
        upward = times(ffn_rows[k], up_w)
        grad_hidden = times_back(cotangent_rows[k], down_own)
        sig = 1.0 / (1.0 + jnp.exp(-gating))
        hidden = (gating * sig * upward).astype(jnp.bfloat16)
        grad_gate = (grad_hidden * upward * sig * (1.0 + gating * (1.0 - sig))).astype(jnp.bfloat16)
        grad_up = (grad_hidden * gating * sig).astype(jnp.bfloat16)
        back_parts.append(times_back(grad_gate, gate_w) + times_back(grad_up, up_w))
        ffn_parts.append(times(hidden, down_own))
        hidden_rows.append(hidden)
        gate_grad_rows.append(grad_gate)
        up_grad_rows.append(grad_up)
    grad_ffn = scatter_plane(back_parts)
    norm_part, grad_feed = norm_back(residual, scale_mid, feed_gain, grad_ffn)
    grad_residual = norm_part + cotangent.astype(jnp.float32)
    grad_branch = grad_residual.astype(jnp.bfloat16)
    branch_rows = gather_plane(grad_branch)

    block_out = (residual + scatter_plane(ffn_parts)).astype(jnp.bfloat16)

    ffn_all = jnp.concatenate(ffn_rows, 0)
    grad_gate_own = jnp.concatenate(
        [row_product(ffn_all, jnp.concatenate(gate_grad_rows, 0)), row_product(ffn_all, jnp.concatenate(up_grad_rows, 0))],
        1,
    )
    shard_gate = scatter_wide(grad_gate_own).astype(jnp.bfloat16)
    grad_down_own = row_product(jnp.concatenate(hidden_rows, 0), jnp.concatenate(cotangent_rows, 0))
    shard_down = scatter_wide(grad_down_own).astype(jnp.bfloat16)

    grad_proj_rows, normed_parts, smalls, tap_sums = [], [], [], []
    for k in range(4):
        projected, since, attended, grouped, weights = rows[k]
        grad_grouped = times_back(branch_rows[k], out_own)
        grad_proj, small, tap_sum = attend_row_back(
            projected, since, mix, taps_backward, gain_pad, attended, weights, grad_grouped, taps_q, taps_k, head_size
        )
        normed_parts.append(times_back(grad_proj, qkv_own))
        grad_proj_rows.append(grad_proj)
        smalls.append(small)
        tap_sums.append(tap_sum)
    grad_qkv_own = row_product(jnp.concatenate(normed_rows, 0), jnp.concatenate(grad_proj_rows, 0))
    shard_qkv = scatter_wide(unpad_heads(grad_qkv_own, head_size)).astype(jnp.bfloat16)
    grad_out_own = row_product(jnp.concatenate([r[3] for r in rows], 0), jnp.concatenate(branch_rows, 0))
    grad_out = scatter_out(
        grad_out_own.reshape(2, LANES, width)[:, :head_size].reshape(2 * head_size, width)
    )
    grad_normed = scatter_plane(normed_parts)
    norm_part, grad_norm = norm_back(inputs_f, scale_in, norm_gain, grad_normed)
    grad_input = norm_part + grad_residual

    small = smalls[0] + smalls[1] + smalls[2] + smalls[3]
    taps = jnp.sum(tap_sums[0] + tap_sums[1] + tap_sums[2] + tap_sums[3], axis=2) * scaling

    def placed(array, total):
        array = array.reshape(-1)
        return lax.dynamic_update_slice(jnp.zeros((total,), jnp.float32), array, (part * array.shape[0],))

    grad_norm, grad_feed, grad_group, grad_kernel, grad_mix = lax.psum(
        (
            grad_norm,
            grad_feed,
            placed(small[:2, :head_size], width),
            placed(taps, head_count * taps_q * taps_k),
            placed(jnp.sum(small[2:6], axis=1), 2 * head_count),
        ),
        ("narrow", "wide", "seq"),
    )

    def columns(shard, sections):
        rows_here = shard.shape[0]
        every = lax.all_gather(shard, PLANE, axis=0).reshape(cores, rows_here, sections, -1)
        return jnp.moveaxis(every, 0, 2).reshape(rows_here, -1).astype(jnp.float32)

    grad_qkv = columns(shard_qkv, 3)
    grad_gate = columns(shard_gate, 2 * wide)
    grad_down = lax.all_gather(shard_down, PLANE, axis=0, tiled=True).astype(jnp.float32)
    return (
        block_out,
        grad_input,
        grad_norm,
        grad_qkv,
        grad_kernel.reshape(head_count, taps_q, taps_k),
        grad_mix.reshape(head_count, 2),
        grad_group,
        grad_out,
        grad_feed,
        grad_gate,
        grad_down,
    )


def solution(mesh):
    tokens = P(("narrow", "wide", "seq"), None)
    rows = P("wide", None)
    return jax.shard_map(
        on_device,
        mesh=mesh,
        in_specs=(tokens, P(("narrow", "wide", "seq")), P(), rows, P(), P(), P(), rows, P(), rows, rows, tokens),
        out_specs=(tokens, tokens, P(), rows, P(), P(), P(), rows, P(), rows, rows),
        check_vma=False,
    )
```

```python
import functools
import jax
import jax.numpy as jnp
from jax import lax
from jax.experimental import pallas as pl
from jax.experimental.pallas import tpu as pltpu

LANES = 128
EDGE = 64
TOP = 16
LIGHT = pl.CostEstimate(flops=1_000_000, bytes_accessed=1_000_000, transcendentals=0)


def taps_kernel(taps_q, taps_k, scaling, kernel_ref, forward_ref, backward_ref):
    half = (taps_k - 1) // 2
    row = lax.broadcasted_iota(jnp.int32, (2 * LANES, LANES), 0)
    col = lax.broadcasted_iota(jnp.int32, (2 * LANES, LANES), 1)
    forth = col - row + EDGE + half
    back = row - col - EDGE + half
    for head in range(2):
        for tap in range(taps_q):
            ahead = jnp.zeros((2 * LANES, LANES), jnp.float32)
            behind = jnp.zeros((2 * LANES, LANES), jnp.float32)
            for tap_k in range(taps_k):
                value = kernel_ref[head, tap, tap_k]
                ahead = jnp.where(forth == tap_k, value, ahead)
                behind = jnp.where(back == tap_k, value, behind)
            ahead = ahead * scaling
            high = ahead.astype(jnp.bfloat16)
            cols = slice(tap * LANES, (tap + 1) * LANES)
            forward_ref[head, : 2 * LANES, cols] = high
            forward_ref[head, 2 * LANES : 4 * LANES, cols] = high
            forward_ref[head, 4 * LANES :, cols] = (ahead - high.astype(jnp.float32)).astype(jnp.bfloat16)
            backward_ref[head, tap * 2 * LANES : (tap + 1) * 2 * LANES, :] = behind.astype(jnp.bfloat16)


def tap_bands(kernels, scaling):
    heads, taps_q, taps_k = kernels.shape
    return pl.pallas_call(
        functools.partial(taps_kernel, taps_q, taps_k, scaling),
        out_shape=(
            jax.ShapeDtypeStruct((heads, 6 * LANES, taps_q * LANES), jnp.bfloat16),
            jax.ShapeDtypeStruct((heads, taps_q * 2 * LANES, LANES), jnp.bfloat16),
        ),
        in_specs=[pl.BlockSpec(memory_space=pltpu.SMEM)],
        out_specs=(pl.BlockSpec(memory_space=pltpu.VMEM),) * 2,
        compiler_params=pltpu.CompilerParams(vmem_limit_bytes=32 * 1024 * 1024),
        cost_estimate=LIGHT,
        name="tap_bands",
    )(kernels)


def place_columns_kernel(sections, chunk, where_ref, *refs):
    ins, out_ref = refs[:-1], refs[-1]
    line, core = where_ref[0], where_ref[1]
    width = 2 * chunk
    chips = len(ins) // 2
    for k in range(chips):
        own = ins[2 * k][...].astype(jnp.float32)
        other = ins[2 * k + 1][...].astype(jnp.float32)
        first = jnp.where(core == 0, own, other)
        second = jnp.where(core == 0, other, own)
        for s in range(sections):
            both = jnp.concatenate([first[:, s * chunk : (s + 1) * chunk], second[:, s * chunk : (s + 1) * chunk]], 1)
            at = pl.multiple_of(s * chips * width + (line ^ k) * width, LANES)
            out_ref[:, pl.ds(at, width)] = both


def place_columns(place, pieces, sections, chunk):
    rows, cols = pieces[0].shape
    cols_out = sections * chunk * len(pieces)
    steps = 4 if rows % 64 == 0 else 1
    spec = pl.BlockSpec((rows // steps, cols), lambda s, place: (s, 0))
    return pl.pallas_call(
        functools.partial(place_columns_kernel, sections, chunk),
        out_shape=jax.ShapeDtypeStruct((rows, cols_out), jnp.float32),
        grid_spec=pltpu.PrefetchScalarGridSpec(
            num_scalar_prefetch=1,
            grid=(steps,),
            in_specs=[spec] * len(pieces),
            out_specs=pl.BlockSpec((rows // steps, cols_out), lambda s, place: (s, 0)),
        ),
        compiler_params=pltpu.CompilerParams(vmem_limit_bytes=40 * 1024 * 1024),
        cost_estimate=LIGHT,
        name="place_columns",
    )(place, *pieces)


def place_feed_kernel(sections, chunk, pieces, where_ref, *refs):
    ins, extras = refs[:pieces], refs[pieces : 2 * pieces]
    gate_ref, down_ref, out_ref = refs[2 * pieces :]
    line, core = where_ref[0], where_ref[1]
    width = 2 * chunk
    chips = pieces // 2
    gate_cols = sections * chunk
    for k in range(chips):
        own = ins[2 * k][...].astype(jnp.float32)
        other = ins[2 * k + 1][...].astype(jnp.float32)
        first = jnp.where(core == 0, own, other)
        second = jnp.where(core == 0, other, own)
        for s in range(sections):
            both = jnp.concatenate([first[:, s * chunk : (s + 1) * chunk], second[:, s * chunk : (s + 1) * chunk]], 1)
            at = pl.multiple_of(s * chips * width + (line ^ k) * width, LANES)
            gate_ref[:, pl.ds(at, width)] = both
        at = pl.multiple_of((line ^ k) * width, width)
        down_ref[pl.ds(at, chunk), :] = first[:, gate_cols:]
        down_ref[pl.ds(at + chunk, chunk), :] = second[:, gate_cols:]

    @pl.when(pl.program_id(0) == 0)
    def _():
        rows = extras[0].shape[0]
        for k in range(chips):
            for e in range(2):
                at = pl.multiple_of(((core ^ e) * chips + (line ^ k)) * rows, rows)
                out_ref[pl.ds(at, rows), :] = extras[2 * k + e][...].astype(jnp.float32)


def place_feed(place, pieces, chunk, blocks):
    rows, cols = pieces[0].shape
    extra = rows - blocks * chunk
    sections = (cols // chunk) * 2 // 3
    hidden = cols - sections * chunk
    gate_cols = sections * chunk * len(pieces)
    last = blocks * chunk // extra
    return pl.pallas_call(
        functools.partial(place_feed_kernel, sections, chunk, len(pieces)),
        out_shape=(
            jax.ShapeDtypeStruct((blocks * chunk, gate_cols), jnp.float32),
            jax.ShapeDtypeStruct((chunk * len(pieces), hidden * blocks), jnp.float32),
            jax.ShapeDtypeStruct((extra * len(pieces), cols), jnp.float32),
        ),
        grid_spec=pltpu.PrefetchScalarGridSpec(
            num_scalar_prefetch=1,
            grid=(blocks,),
            in_specs=[pl.BlockSpec((chunk, cols), lambda s, place: (s, 0))] * len(pieces)
            + [pl.BlockSpec((extra, cols), lambda s, place: (last, 0))] * len(pieces),
            out_specs=(
                pl.BlockSpec((chunk, gate_cols), lambda s, place: (s, 0)),
                pl.BlockSpec((chunk * len(pieces), hidden), lambda s, place: (0, s)),
                pl.BlockSpec((extra * len(pieces), cols), lambda s, place: (0, 0)),
            ),
        ),
        compiler_params=pltpu.CompilerParams(vmem_limit_bytes=48 * 1024 * 1024),
        cost_estimate=LIGHT,
        name="place_feed",
    )(place, *pieces, *pieces)


def masked_scores(q_blk, keys, since, first_row):
    scores = lax.dot_general(q_blk, keys, (((1,), (1,)), ((), ())), preferred_element_type=jnp.float32)
    rows = first_row + lax.broadcasted_iota(jnp.int32, scores.shape, 0)
    back = rows + EDGE - lax.broadcasted_iota(jnp.int32, scores.shape, 1)
    limit = jnp.concatenate([since] * (scores.shape[1] // LANES), 1)
    return jnp.where((back >= 0) & (back <= limit), scores, 0.0)


def head_places(heads, head_size):
    return [((head * head_size) // LANES, (head * head_size) % LANES) for head in range(heads)]


def split_heads(joined, heads, head_size):
    real = lax.broadcasted_iota(jnp.int32, (joined.shape[0], LANES), 1) < head_size
    out = []
    for tile, shift in head_places(heads, head_size):
        if shift:
            both = joined[:, tile * LANES : (tile + 2) * LANES]
            piece = pltpu.roll(both, 2 * LANES - shift, 1)[:, :LANES]
        else:
            piece = joined[:, tile * LANES : (tile + 1) * LANES]
        out.append(jnp.where(real, piece, 0.0))
    return out


def join_heads(pieces, head_size):
    count = pieces[0].shape[0]
    nothing = jnp.zeros((count, LANES), jnp.float32)
    tiles = [nothing] * 5
    for piece, (tile, shift) in zip(pieces, head_places(len(pieces), head_size)):
        if shift:
            both = pltpu.roll(jnp.concatenate([piece, nothing], 1), shift, 1)
            tiles[tile] = tiles[tile] + both[:, :LANES]
            tiles[tile + 1] = tiles[tile + 1] + both[:, LANES:]
        else:
            tiles[tile] = tiles[tile] + piece
    return jnp.concatenate(tiles, 1)


def forward_kernel(
    taps_q, head_size, core_ref, mix_ref, own_ref, other_ref, since_ref, joined_ref, taps_ref, gain_ref,
    proj_ref, att_ref, grouped_ref, weights_ref, keys_pad, s_high, s_low, spread, grouped_row,
):
    seq_len = proj_ref.shape[0]
    half_len = seq_len // 2
    blocks = seq_len // LANES
    own_at = pl.multiple_of(core_ref[0] * half_len, half_len)
    other_at = pl.multiple_of((1 - core_ref[0]) * half_len, half_len)
    keys_pad[...] = jnp.zeros_like(keys_pad)
    s_high[...] = jnp.zeros_like(s_high)
    s_low[...] = jnp.zeros_like(s_low)
    for ref, at in ((own_ref, own_at), (other_ref, other_at)):
        joined = jnp.dot(ref[...], joined_ref[...], preferred_element_type=jnp.float32)
        for head, piece in enumerate(split_heads(joined, 6, head_size)):
            proj_ref[pl.ds(at, half_len), head * LANES : (head + 1) * LANES] = piece.astype(jnp.bfloat16)

    def one_head(head, carry):
        lane = pl.multiple_of(head * LANES, LANES)
        lane_k = pl.multiple_of((head + 2) * LANES, LANES)
        keys_pad[EDGE : EDGE + seq_len, :] = proj_ref[:, pl.ds(lane_k, LANES)]
        for qi in range(blocks):
            first = qi * LANES
            width = (qi + 2) * LANES
            scores = masked_scores(
                proj_ref[first : first + LANES, pl.ds(lane, LANES)],
                keys_pad[:width, :],
                since_ref[first : first + LANES, :],
                first,
            )
            high = scores.astype(jnp.bfloat16)
            s_high[TOP + first : TOP + first + LANES, :width] = high
            s_low[TOP + first : TOP + first + LANES, :width] = (scores - high.astype(jnp.float32)).astype(jnp.bfloat16)
        for m in range(blocks):
            first = m * LANES
            count = seq_len - first
            high = s_high[first:, first : first + 2 * LANES]
            left = jnp.concatenate([high, s_low[first:, first : first + 2 * LANES], high], 1)
            spread[first:, :] = jnp.dot(left, taps_ref[head], preferred_element_type=jnp.float32)
            since = since_ref[first:, :]
            logits = spread[TOP + first :, :LANES]
            for tap in range(1, taps_q):
                moved = spread[TOP + first - tap : TOP + seq_len - tap, tap * LANES : (tap + 1) * LANES]
                logits = logits + jnp.where(since >= tap, moved, 0.0)
            weights_ref[head, first:, first : first + LANES] = logits
        for qi in range(blocks):
            first = qi * LANES
            width = (qi + 1) * LANES
            logits = weights_ref[head, first : first + LANES, :width]
            rows = first + lax.broadcasted_iota(jnp.int32, logits.shape, 0)
            back = rows - lax.broadcasted_iota(jnp.int32, logits.shape, 1)
            limit = jnp.concatenate([since_ref[first : first + LANES, :]] * (qi + 1), 1)
            logits = jnp.where((back >= 0) & (back <= limit), logits, -1e30)
            raised = jnp.exp(logits - jnp.max(logits, axis=1, keepdims=True))
            weights_ref[head, first : first + LANES, :width] = raised / jnp.sum(raised, axis=1, keepdims=True)
        return carry

    lax.fori_loop(0, 2, one_head, 0)
    real = lax.broadcasted_iota(jnp.int32, (LANES, LANES), 1) < head_size
    for qi in range(blocks):
        first = qi * LANES
        width = (qi + 1) * LANES
        low = weights_ref[0, first : first + LANES, :width]
        upp = weights_ref[1, first : first + LANES, :width]
        for head in range(2):
            mixed = (mix_ref[head, 0] * low + mix_ref[head, 1] * upp).astype(jnp.bfloat16)
            cols = slice(head * LANES, (head + 1) * LANES)
            att = jnp.dot(
                mixed, proj_ref[:width, (4 + head) * LANES : (5 + head) * LANES], preferred_element_type=jnp.float32
            )
            att_ref[first : first + LANES, cols] = att
            normal, _ = normalize(att, real, head_size)
            grouped_row[first : first + LANES, cols] = (normal * gain_ref[:, cols]).astype(jnp.bfloat16)
    grouped_ref[:half_len, :] = grouped_row[pl.ds(own_at, half_len), :]
    grouped_ref[half_len:, :] = grouped_row[pl.ds(other_at, half_len), :]


def normalize(att, real, head_size):
    mean = jnp.sum(att, axis=1, keepdims=True) * (1.0 / head_size)
    centered = jnp.where(real, att - mean, 0.0)
    spread = jnp.sum(centered * centered, axis=1, keepdims=True) * (1.0 / head_size)
    scale = lax.rsqrt(spread + 1e-05)
    return centered * scale, scale


def attend_row(core, own, other, since, mix, joined, taps_forward, gain_pad, taps_q, head_size):
    seq_len = 2 * own.shape[0]
    full = seq_len + 2 * EDGE
    vmem = pl.BlockSpec(memory_space=pltpu.VMEM)
    smem = pl.BlockSpec(memory_space=pltpu.SMEM)
    return pl.pallas_call(
        functools.partial(forward_kernel, taps_q, head_size),
        out_shape=(
            jax.ShapeDtypeStruct((seq_len, 6 * LANES), jnp.bfloat16),
            jax.ShapeDtypeStruct((seq_len, 2 * LANES), jnp.float32),
            jax.ShapeDtypeStruct((seq_len, 2 * LANES), jnp.bfloat16),
            jax.ShapeDtypeStruct((2, seq_len, seq_len), jnp.float32),
        ),
        in_specs=[smem, smem] + [vmem] * 6,
        out_specs=(vmem,) * 4,
        scratch_shapes=[
            pltpu.VMEM((full, LANES), jnp.bfloat16),
            pltpu.VMEM((TOP + seq_len, full), jnp.bfloat16),
            pltpu.VMEM((TOP + seq_len, full), jnp.bfloat16),
            pltpu.VMEM((TOP + seq_len, taps_q * LANES), jnp.float32),
            pltpu.VMEM((seq_len, 2 * LANES), jnp.bfloat16),
        ],
        compiler_params=pltpu.CompilerParams(vmem_limit_bytes=40 * 1024 * 1024),
        cost_estimate=LIGHT,
        name="attend_row",
    )(core, mix, own, other, since, joined, taps_forward, gain_pad)


def backward_kernel(
    taps_q, taps_k, head_size, scaling, core_ref, mix_ref, own_ref, other_ref, out_weight_ref, joined_ref,
    proj_ref, since_ref, taps_ref, gain_ref, att_ref, weights_ref,
    joined_grad_ref, mine_ref, theirs_ref, small_ref, tap_ref,
    keys_pad, grad_att, conv_grad, shifted, s_low, s_grad, since_pad, grad_ref, out_ref,
):
    seq_len = proj_ref.shape[0]
    half_len = seq_len // 2
    own_at = pl.multiple_of(core_ref[0] * half_len, half_len)
    other_at = pl.multiple_of((1 - core_ref[0]) * half_len, half_len)
    for ref, at in ((own_ref, own_at), (other_ref, other_at)):
        grad_ref[pl.ds(at, half_len), :] = lax.dot_general(
            ref[...], out_weight_ref[...], (((1,), (1,)), ((), ())), preferred_element_type=jnp.float32
        )
    blocks = seq_len // LANES
    half = (taps_k - 1) // 2
    full = seq_len + 2 * EDGE
    keys_pad[...] = jnp.zeros_like(keys_pad)
    s_low[...] = jnp.zeros_like(s_low)
    s_grad[...] = jnp.zeros_like(s_grad)
    shifted[...] = jnp.zeros_like(shifted)
    conv_grad[...] = jnp.zeros_like(conv_grad)
    since_pad[:seq_len, :] = since_ref[...]
    since_pad[seq_len:, :] = jnp.zeros((8, LANES), jnp.int32)
    small_ref[...] = jnp.zeros_like(small_ref)

    real = lax.broadcasted_iota(jnp.int32, (LANES, LANES), 1) < head_size
    for head in range(2):
        cols = slice(head * LANES, (head + 1) * LANES)
        group_sum = jnp.zeros((1, LANES), jnp.float32)
        for qi in range(blocks):
            rows = slice(qi * LANES, (qi + 1) * LANES)
            normal, scale = normalize(att_ref[rows, cols], real, head_size)
            grad = grad_ref[rows, cols]
            group_sum = group_sum + jnp.sum(grad * normal, axis=0, keepdims=True)
            lift = grad * gain_ref[:, cols]
            mean = jnp.sum(lift, axis=1, keepdims=True) * (1.0 / head_size)
            along = jnp.sum(lift * normal, axis=1, keepdims=True) * (1.0 / head_size)
            grad_att[rows, cols] = jnp.where(real, scale * (lift - mean - normal * along), 0.0).astype(jnp.bfloat16)
        small_ref[head : head + 1, :] = group_sum

    sums = [[jnp.zeros((1, LANES), jnp.float32) for _ in range(2)] for _ in range(2)]
    grad_v = [[], []]
    for qi in range(blocks):
        first = qi * LANES
        width = (qi + 1) * LANES
        rows = slice(first, first + LANES)
        maps = [weights_ref[k, rows, :width] for k in range(2)]
        grad_mixed = []
        for head in range(2):
            cols = slice(head * LANES, (head + 1) * LANES)
            values = proj_ref[:width, (4 + head) * LANES : (5 + head) * LANES]
            gm = lax.dot_general(
                grad_att[rows, cols], values, (((1,), (1,)), ((), ())), preferred_element_type=jnp.float32
            )
            grad_mixed.append(gm)
        for head in range(2):
            for k in range(2):
                part = jnp.sum(grad_mixed[head] * maps[k], axis=0, keepdims=True)
                for b in range(qi + 1):
                    sums[head][k] = sums[head][k] + part[:, b * LANES : (b + 1) * LANES]
        for k in range(2):
            grad_w = mix_ref[0, k] * grad_mixed[0] + mix_ref[1, k] * grad_mixed[1]
            inner = jnp.sum(grad_w * maps[k], axis=1, keepdims=True)
            conv_grad[k, rows, :width] = maps[k] * (grad_w - inner)
    for head in range(2):
        for k in range(2):
            small_ref[2 + 2 * head + k : 3 + 2 * head + k, :] = sums[head][k]
        cols = slice(head * LANES, (head + 1) * LANES)
        for kb in range(blocks):
            first = kb * LANES
            mixed = (
                mix_ref[head, 0] * weights_ref[0, first:, first : first + LANES]
                + mix_ref[head, 1] * weights_ref[1, first:, first : first + LANES]
            ).astype(jnp.bfloat16)
            out_ref[first : first + LANES, (4 + head) * LANES : (5 + head) * LANES] = lax.dot_general(
                mixed, grad_att[first:, cols], (((0,), (0,)), ((), ())), preferred_element_type=jnp.float32
            )

    def one_head(head, carry):
        lane = pl.multiple_of(head * LANES, LANES)
        lane_k = pl.multiple_of((head + 2) * LANES, LANES)
        keys_pad[EDGE : EDGE + seq_len, :] = proj_ref[:, pl.ds(lane_k, LANES)]
        for qi in range(blocks):
            first = qi * LANES
            width = (qi + 2) * LANES
            scores = masked_scores(
                proj_ref[first : first + LANES, pl.ds(lane, LANES)],
                keys_pad[:width, :],
                since_ref[first : first + LANES, :],
                first,
            )
            s_low[TOP + first : TOP + first + LANES, :width] = scores.astype(jnp.bfloat16)
            reach = min(width, seq_len)
            for tap in range(taps_q):
                moved = conv_grad[head, first + tap : first + tap + LANES, :reach]
                if tap > 0:
                    limit = since_pad[first + tap : first + tap + LANES, :]
                    limit = jnp.concatenate([limit] * (reach // LANES), 1)
                    moved = jnp.where(limit >= tap, moved, 0.0)
                shifted[tap, TOP + first : TOP + first + LANES, LANES : LANES + reach] = moved.astype(jnp.bfloat16)
        for m in range(blocks + 1):
            first = max(m - 1, 0) * LANES
            left = jnp.concatenate(
                [shifted[tap, TOP + first :, m * LANES : (m + 2) * LANES] for tap in range(taps_q)], 1
            )
            grad = jnp.dot(left, taps_ref[head], preferred_element_type=jnp.float32)
            rows = first + lax.broadcasted_iota(jnp.int32, grad.shape, 0)
            back = rows + EDGE - m * LANES - lax.broadcasted_iota(jnp.int32, grad.shape, 1)
            keep = (back >= 0) & (back <= since_ref[first:, :])
            s_grad[first:, m * LANES : (m + 1) * LANES] = jnp.where(keep, grad, 0.0).astype(jnp.bfloat16)
        total = jnp.zeros((2 * LANES, taps_q * LANES), jnp.float32)
        for m in range(blocks):
            first = m * LANES
            right = jnp.concatenate(
                [shifted[tap, first:, (m + 1) * LANES : (m + 2) * LANES] for tap in range(taps_q)], 1
            )
            total = total + lax.dot_general(
                s_low[first:, first : first + 2 * LANES], right, (((0,), (0,)), ((), ())),
                preferred_element_type=jnp.float32,
            )
        ridge = lax.broadcasted_iota(jnp.int32, (2 * LANES, LANES), 1) - lax.broadcasted_iota(
            jnp.int32, (2 * LANES, LANES), 0
        )
        for tap_k in range(taps_k):
            on = ridge == tap_k - EDGE - half
            for tap in range(taps_q):
                line = jnp.where(on, total[:, tap * LANES : (tap + 1) * LANES], 0.0)
                tap_ref[head, tap * taps_k + tap_k : tap * taps_k + tap_k + 1, :] = jnp.sum(line, axis=0, keepdims=True)
        for qi in range(blocks):
            first = qi * LANES
            width = (qi + 2) * LANES
            grad_q = jnp.dot(
                s_grad[first : first + LANES, :width], keys_pad[:width, :], preferred_element_type=jnp.float32
            )
            out_ref[first : first + LANES, pl.ds(lane, LANES)] = grad_q * scaling
        for kb in range(blocks):
            first = kb * LANES
            grad_k = lax.dot_general(
                s_grad[first:, first + EDGE : first + EDGE + LANES],
                proj_ref[first:, pl.ds(lane, LANES)],
                (((0,), (0,)), ((), ())),
                preferred_element_type=jnp.float32,
            )
            out_ref[first : first + LANES, pl.ds(lane_k, LANES)] = grad_k * scaling
        return carry

    lax.fori_loop(0, 2, one_head, 0)
    for at, first in ((own_at, 0), (other_at, half_len)):
        pieces = [out_ref[pl.ds(at, half_len), head * LANES : (head + 1) * LANES] for head in range(6)]
        joined = join_heads(pieces, head_size).astype(jnp.bfloat16)
        joined_grad_ref[first : first + half_len, :] = joined
        grad_in = lax.dot_general(
            joined, joined_ref[...], (((1,), (1,)), ((), ())), preferred_element_type=jnp.float32
        )
        if first:
            theirs_ref[...] = grad_in.astype(jnp.bfloat16)
        else:
            mine_ref[...] = grad_in


def attend_row_back(
    core, own, other, out_weight, joined, saved, since, mix, taps_backward, gain_pad, taps_q, taps_k, head_size
):
    projected, att, weights = saved
    seq_len = projected.shape[0]
    width = own.shape[1]
    full = seq_len + 2 * EDGE
    vmem = pl.BlockSpec(memory_space=pltpu.VMEM)
    smem = pl.BlockSpec(memory_space=pltpu.SMEM)
    return pl.pallas_call(
        functools.partial(backward_kernel, taps_q, taps_k, head_size, head_size ** (-0.5)),
        out_shape=(
            jax.ShapeDtypeStruct((seq_len, joined.shape[1]), jnp.bfloat16),
            jax.ShapeDtypeStruct((seq_len // 2, width), jnp.float32),
            jax.ShapeDtypeStruct((seq_len // 2, width), jnp.bfloat16),
            jax.ShapeDtypeStruct((8, LANES), jnp.float32),
            jax.ShapeDtypeStruct((2, taps_q * taps_k, LANES), jnp.float32),
        ),
        in_specs=[smem, smem] + [vmem] * 10,
        out_specs=(vmem,) * 5,
        scratch_shapes=[
            pltpu.VMEM((full, LANES), jnp.bfloat16),
            pltpu.VMEM((seq_len, 2 * LANES), jnp.bfloat16),
            pltpu.VMEM((2, seq_len + 8, seq_len), jnp.float32),
            pltpu.VMEM((taps_q, TOP + seq_len, seq_len + 2 * LANES), jnp.bfloat16),
            pltpu.VMEM((TOP + seq_len, full), jnp.bfloat16),
            pltpu.VMEM((seq_len, full), jnp.bfloat16),
            pltpu.VMEM((seq_len + 8, LANES), jnp.int32),
            pltpu.VMEM((seq_len, 2 * LANES), jnp.float32),
            pltpu.VMEM((seq_len, 6 * LANES), jnp.float32),
        ],
        compiler_params=pltpu.CompilerParams(vmem_limit_bytes=48 * 1024 * 1024),
        cost_estimate=LIGHT,
        name="attend_row_back",
    )(core, mix, own, other, out_weight, joined, projected, since, taps_backward, gain_pad, att, weights)


def feed_kernel(wide, own_ref, other_ref, cot_own_ref, cot_other_ref, gate_ref, cut_ref,
                hidden_ref, grads_ref, ffn_mine_ref, ffn_theirs_ref, back_mine_ref, back_theirs_ref, down_ref):
    half_len = own_ref.shape[0]
    cols = down_ref.shape[0]
    chunk = cols // wide
    blocks = down_ref.shape[1] // cols
    for z in range(wide):
        for b in range(blocks):
            first = (z * blocks + b) * chunk
            down_ref[z * chunk : (z + 1) * chunk, b * cols : (b + 1) * cols] = cut_ref[first : first + chunk, :]
    for first, ref, cot_ref in ((0, own_ref, cot_own_ref), (half_len, other_ref, cot_other_ref)):
        rows = slice(first, first + half_len)
        both = jnp.dot(ref[...], gate_ref[...], preferred_element_type=jnp.float32)
        gating, upward = both[:, :cols], both[:, cols:]
        grad = lax.dot_general(
            cot_ref[...], down_ref[...], (((1,), (1,)), ((), ())), preferred_element_type=jnp.float32
        )
        sig = 1.0 / (1.0 + jnp.exp(-gating))
        silu = gating * sig
        hidden = (silu * upward).astype(jnp.bfloat16)
        hidden_ref[rows, :] = hidden
        grads_ref[rows, :cols] = (grad * upward * (sig * (1.0 + gating * (1.0 - sig)))).astype(jnp.bfloat16)
        grads_ref[rows, cols:] = (grad * silu).astype(jnp.bfloat16)
        back = lax.dot_general(
            grads_ref[rows, :], gate_ref[...], (((1,), (1,)), ((), ())), preferred_element_type=jnp.float32
        )
        ffn = jnp.dot(hidden, down_ref[...], preferred_element_type=jnp.float32)
        if first:
            back_theirs_ref[...] = back.astype(jnp.bfloat16)
            ffn_theirs_ref[...] = ffn.astype(jnp.bfloat16)
        else:
            back_mine_ref[...] = back
            ffn_mine_ref[...] = ffn


def feed_row(own, other, cot_own, cot_other, weights, wide):
    half_len, width = own.shape
    cols = weights[1].shape[1]
    vmem = pl.BlockSpec(memory_space=pltpu.VMEM)
    return pl.pallas_call(
        functools.partial(feed_kernel, wide),
        out_shape=(
            jax.ShapeDtypeStruct((2 * half_len, cols), jnp.bfloat16),
            jax.ShapeDtypeStruct((2 * half_len, 2 * cols), jnp.bfloat16),
            jax.ShapeDtypeStruct((half_len, width), jnp.float32),
            jax.ShapeDtypeStruct((half_len, width), jnp.bfloat16),
            jax.ShapeDtypeStruct((half_len, width), jnp.float32),
            jax.ShapeDtypeStruct((half_len, width), jnp.bfloat16),
        ),
        in_specs=[vmem] * 6,
        out_specs=(vmem,) * 6,
        scratch_shapes=[pltpu.VMEM((cols, width), jnp.bfloat16)],
        compiler_params=pltpu.CompilerParams(vmem_limit_bytes=48 * 1024 * 1024),
        cost_estimate=LIGHT,
        name="feed_row",
    )(own, other, cot_own, cot_other, *weights)


def feed_grad_kernel(counts, *refs):
    lefts, grads, hiddens, cots = (
        jnp.concatenate([ref[...] for ref in refs[sum(counts[:i]) : sum(counts[: i + 1])]], 0) for i in range(4)
    )
    out_ref = refs[-1]
    chunk = hiddens.shape[1]
    cols = out_ref.shape[1] - grads.shape[1]
    out_ref[:, : grads.shape[1]] = lax.dot_general(
        lefts, grads, (((0,), (0,)), ((), ())), preferred_element_type=jnp.float32
    ).astype(jnp.bfloat16)
    down = lax.dot_general(hiddens, cots, (((0,), (0,)), ((), ())), preferred_element_type=jnp.float32)
    for b in range(down.shape[1] // cols):
        out_ref[b * chunk : (b + 1) * chunk, grads.shape[1] :] = down[:, b * cols : (b + 1) * cols].astype(jnp.bfloat16)


def feed_grad(lefts, grads, hiddens, cots, wide):
    width = lefts[0].shape[1]
    cols = hiddens[0].shape[1]
    block, chunk = width // wide, cols // wide
    if block % LANES or chunk % LANES:
        gate = lax.dot_general(
            jnp.concatenate(lefts, 0), jnp.concatenate(grads, 0), (((0,), (0,)), ((), ())),
            preferred_element_type=jnp.float32,
        )
        down = lax.dot_general(
            jnp.concatenate(hiddens, 0), jnp.concatenate(cots, 0), (((0,), (0,)), ((), ())),
            preferred_element_type=jnp.float32,
        )
        down = jnp.swapaxes(down.reshape(wide, chunk, width // cols, cols), 1, 2).reshape(width, cols)
        return jnp.concatenate([gate, down], 1).astype(jnp.bfloat16)
    count = sum(a.shape[0] for a in lefts)
    cols_out = grads[0].shape[1] + cols
    return pl.pallas_call(
        functools.partial(feed_grad_kernel, (len(lefts), len(grads), len(hiddens), len(cots))),
        out_shape=jax.ShapeDtypeStruct((width, cols_out), jnp.bfloat16),
        grid=(wide,),
        in_specs=[pl.BlockSpec((a.shape[0], block), lambda s: (0, s)) for a in lefts]
        + [pl.BlockSpec(a.shape, lambda s: (0, 0)) for a in grads]
        + [pl.BlockSpec((a.shape[0], chunk), lambda s: (0, s)) for a in hiddens]
        + [pl.BlockSpec(a.shape, lambda s: (0, 0)) for a in cots],
        out_specs=pl.BlockSpec((block, cols_out), lambda s: (s, 0)),
        compiler_params=pltpu.CompilerParams(vmem_limit_bytes=56 * 1024 * 1024),
        cost_estimate=LIGHT,
        name="feed_grad",
    )(*lefts, *grads, *hiddens, *cots)


def weight_kernel(lefts, *refs):
    left = jnp.concatenate([ref[...] for ref in refs[:lefts]], 0)
    right = jnp.concatenate([ref[...] for ref in refs[lefts:-1]], 0)
    refs[-1][...] = lax.dot_general(
        left, right, (((0,), (0,)), ((), ())), preferred_element_type=jnp.float32
    ).astype(jnp.bfloat16)


def weight_grad(lefts, rights, block, name):
    rows_out, cols_out = lefts[0].shape[1], rights[0].shape[1]
    count = sum(a.shape[0] for a in lefts)
    return pl.pallas_call(
        functools.partial(weight_kernel, len(lefts)),
        out_shape=jax.ShapeDtypeStruct((rows_out, cols_out), jnp.bfloat16),
        grid=(rows_out // block,),
        in_specs=[pl.BlockSpec((a.shape[0], block), lambda s: (0, s)) for a in lefts]
        + [pl.BlockSpec(a.shape, lambda s: (0, 0)) for a in rights],
        out_specs=pl.BlockSpec((block, cols_out), lambda s: (s, 0)),
        compiler_params=pltpu.CompilerParams(vmem_limit_bytes=48 * 1024 * 1024),
        cost_estimate=LIGHT,
        name=name,
    )(*lefts, *rights)


def halves_kernel(mine_ref, came_ref, low_ref, high_ref):
    cut = low_ref.shape[0]
    low_ref[...] = (mine_ref[:cut, :] + came_ref[:cut, :].astype(jnp.float32)).astype(jnp.bfloat16)
    high_ref[...] = (mine_ref[cut:, :] + came_ref[cut:, :].astype(jnp.float32)).astype(jnp.bfloat16)


def sum_halves(mine, came):
    half = jax.ShapeDtypeStruct((mine.shape[0] // 2, mine.shape[1]), jnp.bfloat16)
    vmem = pl.BlockSpec(memory_space=pltpu.VMEM)
    return pl.pallas_call(
        halves_kernel, out_shape=(half, half), in_specs=[vmem] * 2, out_specs=(vmem,) * 2,
        compiler_params=pltpu.CompilerParams(vmem_limit_bytes=16 * 1024 * 1024), cost_estimate=LIGHT, name="sum_halves",
    )(mine, came)


def sum_kernel(second, mine_ref, came_ref, extra_ref, out_ref):
    cut = extra_ref.shape[0]
    rows, rest = (slice(cut, 2 * cut), slice(0, cut)) if second else (slice(0, cut), slice(cut, 2 * cut))
    total = mine_ref[rows, :] + came_ref[rows, :].astype(jnp.float32) + extra_ref[...].astype(jnp.float32)
    out_ref[rows, :] = total.astype(jnp.bfloat16)
    out_ref[rest, :] = (mine_ref[rest, :] + came_ref[rest, :].astype(jnp.float32)).astype(jnp.bfloat16)


def low_sum(mine, came, extra, second):
    vmem = pl.BlockSpec(memory_space=pltpu.VMEM)
    return pl.pallas_call(
        functools.partial(sum_kernel, second), out_shape=jax.ShapeDtypeStruct(mine.shape, jnp.bfloat16),
        in_specs=[vmem] * 3, out_specs=vmem,
        compiler_params=pltpu.CompilerParams(vmem_limit_bytes=16 * 1024 * 1024), cost_estimate=LIGHT, name="low_sum",
    )(mine, came, extra)


def pair_kernel(mine_ref, came_ref, out_ref):
    out_ref[...] = (mine_ref[...] + came_ref[...].astype(jnp.float32)).astype(jnp.bfloat16)


def pair_sum(mine, came):
    vmem = pl.BlockSpec(memory_space=pltpu.VMEM)
    return pl.pallas_call(
        pair_kernel, out_shape=jax.ShapeDtypeStruct(mine.shape, jnp.bfloat16), in_specs=[vmem] * 2, out_specs=vmem,
        compiler_params=pltpu.CompilerParams(vmem_limit_bytes=16 * 1024 * 1024), cost_estimate=LIGHT, name="pair_sum",
    )(mine, came)


from jax.sharding import PartitionSpec as P

PLANE = ("narrow", "seq")
SWAP = [(0, 1), (1, 0)]


def seq_swap(array):
    return lax.ppermute(array, "seq", SWAP)


def x_swap(array):
    return lax.ppermute(array, "narrow", [(0, 1), (1, 0), (2, 3), (3, 2)])


def y_swap(array):
    return lax.ppermute(array, "narrow", [(0, 2), (2, 0), (1, 3), (3, 1)])


def diagonal_swap(array):
    return lax.ppermute(array, "narrow", [(i, i ^ 3) for i in range(4)])


def gather_plane(own):
    half = own.shape[0] // 2
    from_x = x_swap(own)
    from_y = y_swap(own)
    corner = jnp.concatenate([y_swap(from_x[:half]), x_swap(from_y[half:])], 0)
    return [(a, seq_swap(a)) for a in (own, from_x, from_y, corner)]


def after(array, *others):
    return lax.optimization_barrier((array, *others))[0] if others else array


class Steps:
    def __init__(self):
        self.ended = ()

    def hold(self, array):
        return after(array, *self.ended)

    def end(self, *arrays):
        self.ended = arrays


def half_rows(array, second):
    cut = array.shape[0] // 2
    return array[cut:] if second else array[:cut]


def whole_sum(mine, came, from_x, from_y):
    return mine + came.astype(jnp.float32) + from_x.astype(jnp.float32) + from_y.astype(jnp.float32)


def wide_shift(array, by):
    count = lax.axis_size("wide")
    return lax.ppermute(array, "wide", [(i, (i + by) % count) for i in range(count)])


def wide_block(blocks, step):
    count = lax.axis_size("wide")
    at = (lax.axis_index("wide") - step) % count
    return lax.dynamic_index_in_dim(blocks, at, 0, keepdims=False)


def wide_stack(pieces):
    whole = jnp.zeros((len(pieces),) + pieces[0].shape, pieces[0].dtype)
    for step, piece in enumerate(pieces):
        whole = lax.dynamic_update_index_in_dim(whole, piece, (lax.axis_index("wide") - step) % len(pieces), 0)
    return whole


def gather_wide(piece):
    return lax.all_gather(piece, "wide", axis=0, tiled=True)


def scatter_wide(whole):
    return lax.psum_scatter(whole, "wide", scatter_dimension=0, tiled=True)


def exchange_plane(blocks):
    line = lax.axis_index("narrow")

    def block(k):
        return lax.dynamic_index_in_dim(blocks, line ^ k, 0, keepdims=False)

    came = [block(0), x_swap(block(1)), y_swap(block(2)), diagonal_swap(block(3))]
    whole = jnp.zeros_like(blocks)
    for k in range(4):
        whole = lax.dynamic_update_index_in_dim(whole, came[k], line ^ k, 0)
    return whole


def pad_heads(array, head_size):
    heads = array.shape[1] // head_size
    split = array.reshape(array.shape[0], heads, head_size)
    return jnp.pad(split, ((0, 0), (0, 0), (0, LANES - head_size))).reshape(array.shape[0], heads * LANES)


def times(left, right):
    return jnp.dot(left, right, preferred_element_type=jnp.float32)


def norm_scale(values):
    return lax.rsqrt(jnp.mean(values * values, axis=-1, keepdims=True) + 1e-06)


def norm_back(values, scale, gain, grad):
    lift = grad * gain
    along = jnp.mean(lift * values, axis=-1, keepdims=True)
    return scale * lift - values * (scale * scale * scale * along), jnp.sum(grad * values * scale, axis=0)


def on_device(
    inputs,
    doc_start,
    norm_gain,
    qkv_weight,
    logit_kernel,
    head_mix,
    group_gain,
    out_weight,
    feed_gain,
    gate_up,
    down_weight,
    cotangent,
):
    tokens_dev, width = inputs.shape
    head_count, taps_q, taps_k = logit_kernel.shape
    head_size = width // head_count
    group_cols = 2 * head_size
    cores = lax.axis_size(PLANE)
    wide = lax.axis_size("wide")
    line = lax.axis_index("narrow")
    part = lax.axis_index(PLANE)
    chunk = gate_up.shape[1] // (2 * wide * cores)
    scaling = head_size ** (-0.5)

    core = lax.axis_index("seq").astype(jnp.int32).reshape(1)
    place = jnp.stack([line, lax.axis_index("seq"), lax.axis_index("wide")]).astype(jnp.int32)

    joined_piece = jnp.concatenate(
        [
            lax.dynamic_slice_in_dim(qkv_weight, s * width + part * group_cols, group_cols, 1)
            for s in range(3)
        ]
        + [jnp.zeros((qkv_weight.shape[0], -3 * group_cols % LANES), qkv_weight.dtype)],
        1,
    )
    joined = gather_wide(joined_piece)
    inputs, doc_start, out_weight = lax.optimization_barrier((inputs, doc_start, out_weight, joined_piece))[:3]

    flow = Steps()
    hold = flow.hold
    feed_cols = wide * chunk
    first_pos = lax.axis_index(("narrow", "wide", "seq")) * tokens_dev

    out_rows = group_cols // 4
    ring = wide == 4

    inputs_f = inputs.astype(jnp.float32)
    scale_in = norm_scale(inputs_f)
    normed = (inputs_f * scale_in * norm_gain).astype(jnp.bfloat16)
    since = first_pos + jnp.arange(tokens_dev, dtype=jnp.int32) - doc_start
    since_x, since_y, since_d = x_swap(since), y_swap(since), diagonal_swap(since)
    out_pieces = [lax.dynamic_slice_in_dim(out_weight, (lax.axis_index("seq") * 4 + line) * out_rows, out_rows, 0)]
    if ring:
        out_pieces += [wide_shift(out_pieces[0], 1), wide_shift(out_pieces[0], 2)]
    flow.end(normed, since_x, since_y, since_d, out_pieces[-1])

    normed_x, normed_y, normed_o = x_swap(hold(normed)), y_swap(hold(normed)), seq_swap(hold(normed))
    if ring:
        out_pieces.append(wide_shift(hold(out_pieces[0]), 3))
    kernels = lax.dynamic_slice_in_dim(logit_kernel, 2 * part, 2, 0)
    mix = lax.dynamic_slice_in_dim(head_mix, 2 * part, 2, 0)
    taps_forward, taps_backward = tap_bands(hold(kernels), scaling)
    gain_pad = pad_heads(lax.dynamic_slice_in_dim(group_gain, part * group_cols, group_cols, 0)[None], head_size)
    gate_piece = jnp.concatenate(
        [
            lax.dynamic_slice_in_dim(hold(gate_up), (s * cores + part) * chunk, chunk, 1)
            for s in range(2 * wide)
        ],
        1,
    )
    down_piece = lax.dynamic_slice_in_dim(hold(down_weight), part * chunk, chunk, 0)
    down_piece = jnp.concatenate(
        [down_piece[:, at : at + feed_cols] for at in range(0, width, feed_cols)], 0
    )
    since_same = jnp.stack([since, since_x, since_y, since_d])
    since_other = seq_swap(hold(since_same))
    flow.end(normed_x, normed_y, normed_o, taps_forward, gate_piece, down_piece, out_pieces[-1], since_other)

    corner_low, corner_high = y_swap(hold(half_rows(normed_x, False))), x_swap(hold(half_rows(normed_y, True)))
    normed_xo, normed_yo = seq_swap(hold(normed_x)), seq_swap(hold(normed_y))
    first = lax.axis_index("seq") == 0
    since_all = hold(
        jnp.concatenate([jnp.where(first, since_same, since_other), jnp.where(first, since_other, since_same)], 1)
    )
    since_rows = [jnp.broadcast_to(since_all[k][:, None], (2 * tokens_dev, LANES)) for k in range(4)]
    flow.end(corner_low, corner_high, normed_xo, normed_yo, *since_rows)

    normed_c = jnp.concatenate([corner_low, corner_high], 0)
    normed_co = seq_swap(hold(normed_c))
    if ring:
        out_own = exchange_plane(hold(wide_stack(out_pieces)))
    else:
        out_own = lax.dynamic_slice_in_dim(gather_wide(hold(out_weight)), part * group_cols, group_cols, 0)
    normed_rows = [(normed, normed_o), (normed_x, normed_xo), (normed_y, normed_yo), (normed_c, normed_co)]
    flow.end(normed_co, joined, out_own)

    saved, grouped_rows = [None] * 4, [None] * 4

    def attend(k):
        projected, attended, grouped_rows[k], weights = attend_row(
            hold(core), *normed_rows[k], since_rows[k], mix, joined, taps_forward, gain_pad, taps_q, head_size
        )
        saved[k] = (projected, attended, weights)

    feed_own = [gather_wide(hold(gate_piece)), gather_wide(hold(down_piece))]
    out_own = jnp.pad(
        hold(out_own).reshape(2, head_size, width), ((0, 0), (0, LANES - head_size), (0, 0))
    ).reshape(2 * LANES, width)
    branch_mine, branch_theirs = [None] * 4, [None] * 4

    def branch(k):
        branch_theirs[k] = times(hold(grouped_rows[k])[tokens_dev:], out_own).astype(jnp.bfloat16)
        branch_mine[k] = times(hold(grouped_rows[k])[:tokens_dev], out_own)

    cot_x, cot_y = x_swap(hold(cotangent)), y_swap(hold(cotangent))
    attend(3)
    flow.end(grouped_rows[3], out_own)
    branch(3)
    flow.end(branch_theirs[3], branch_mine[3])
    came_3 = seq_swap(hold(branch_theirs[3]))
    cot_o = seq_swap(hold(cotangent))
    attend(1)
    flow.end(grouped_rows[1], cot_x, cot_y, came_3, cot_o)
    low, high = sum_halves(branch_mine[3], hold(came_3))
    branch(1)
    flow.end(low, high, branch_theirs[1], branch_mine[1])
    to_y, to_x = x_swap(hold(low)), y_swap(hold(high))
    came_1, cot_xo = seq_swap(hold(branch_theirs[1])), seq_swap(hold(cot_x))
    attend(2)
    flow.end(grouped_rows[2], came_1, cot_xo, to_x, to_y)
    branch(2)
    low_x = low_sum(branch_mine[1], hold(came_1), to_x, True)
    flow.end(branch_theirs[2], branch_mine[2], low_x)
    came_2, cot_yo = seq_swap(hold(branch_theirs[2])), seq_swap(hold(cot_y))
    flow.end(came_2, cot_yo)
    low_y = low_sum(branch_mine[2], hold(came_2), to_y, False)
    flow.end(low_x, low_y)
    branch_x, branch_y = x_swap(hold(low_x)), y_swap(hold(low_y))
    attend(0)
    flow.end(grouped_rows[0], branch_x, branch_y)
    branch(0)
    flow.end(branch_theirs[0], branch_mine[0])
    came_0 = seq_swap(hold(branch_theirs[0]))
    flow.end(came_0)
    residual = inputs_f + whole_sum(branch_mine[0], hold(came_0), branch_x, branch_y)
    scale_mid = norm_scale(residual)
    normed_ffn = (residual * scale_mid * feed_gain).astype(jnp.bfloat16)
    flow.end(normed_ffn)

    ffn_x, ffn_y, ffn_o = x_swap(hold(normed_ffn)), y_swap(hold(normed_ffn)), seq_swap(hold(normed_ffn))
    flow.end(ffn_o, ffn_x, ffn_y)
    corner_low, corner_high = y_swap(hold(half_rows(ffn_x, False))), x_swap(hold(half_rows(ffn_y, True)))
    ffn_xo, ffn_yo = seq_swap(hold(ffn_x)), seq_swap(hold(ffn_y))
    flow.end(corner_low, corner_high, ffn_xo, ffn_yo)
    cot_low, cot_high = y_swap(hold(half_rows(cot_x, False))), x_swap(hold(half_rows(cot_y, True)))
    ffn_c = jnp.concatenate([corner_low, corner_high], 0)
    ffn_co = seq_swap(hold(ffn_c))
    hidden_rows, gate_grads, feed_out = [None] * 4, [None] * 4, [None] * 4
    ffn_rows = [(normed_ffn, ffn_o), (ffn_x, ffn_xo), (ffn_y, ffn_yo), (ffn_c, ffn_co)]
    cotangent_rows = [(cotangent, cot_o), (cot_x, cot_xo), (cot_y, cot_yo), None]

    def feed(k):
        hidden_rows[k], gate_grads[k], *feed_out[k] = feed_row(
            hold(ffn_rows[k][0]), ffn_rows[k][1], *cotangent_rows[k], feed_own, wide
        )

    feed(0)
    flow.end(hidden_rows[0], ffn_co, cot_low, cot_high)
    cot_c = jnp.concatenate([cot_low, cot_high], 0)
    cot_co = seq_swap(hold(cot_c))
    cotangent_rows[3] = (cot_c, cot_co)
    back_came = [None] * 4
    back_came[0] = seq_swap(hold(feed_out[0][3]))
    feed(1)
    flow.end(hidden_rows[1], cot_co, back_came[0])
    back_came[1] = seq_swap(hold(feed_out[1][3]))
    feed_came = [seq_swap(hold(feed_out[0][1])), seq_swap(hold(feed_out[1][1]))]
    feed(3)
    flow.end(hidden_rows[3], back_came[1], *feed_came)
    back_came[3] = seq_swap(hold(feed_out[3][3]))
    flow.end(back_came[3])
    low, high = sum_halves(feed_out[3][2], hold(back_came[3]))
    flow.end(low, high)
    to_y, to_x = x_swap(hold(low)), y_swap(hold(high))
    feed(2)
    flow.end(hidden_rows[2], to_x, to_y)
    back_came[2] = seq_swap(hold(feed_out[2][3]))
    feed_came.append(seq_swap(hold(feed_out[2][1])))
    low_x = low_sum(feed_out[1][2], back_came[1], hold(to_x), True)
    flow.end(back_came[2], feed_came[2], low_x)
    low_y = low_sum(feed_out[2][2], hold(back_came[2]), to_y, False)
    flow.end(low_x, low_y)
    back_x, back_y = x_swap(hold(low_x)), y_swap(hold(low_y))
    feed_grad_own = feed_grad(
        [hold(a) for k in ffn_rows for a in k], gate_grads, hidden_rows, [a for k in cotangent_rows for a in k], wide
    )
    flow.end(back_x, back_y, feed_grad_own)
    shard_feed = scatter_wide(hold(feed_grad_own))
    feed_came.append(seq_swap(hold(feed_out[3][1])))
    grad_ffn = whole_sum(feed_out[0][2], hold(back_came[0]), back_x, back_y)
    norm_part, grad_feed = norm_back(residual, scale_mid, feed_gain, grad_ffn)
    grad_residual = norm_part + cotangent.astype(jnp.float32)
    grad_branch = grad_residual.astype(jnp.bfloat16)
    flow.end(grad_branch, feed_came[3])

    gb_x, gb_y, gb_o = x_swap(hold(grad_branch)), y_swap(hold(grad_branch)), seq_swap(hold(grad_branch))
    low, high = sum_halves(feed_out[3][0], hold(feed_came[3]))
    flow.end(gb_o, low, high)
    branch_rows = [(grad_branch, gb_o), None, None, None]
    grad_joined, normed_mine, normed_theirs, smalls, tap_sums = ([None] * 4 for _ in range(5))

    def attend_back(k):
        grad_joined[k], normed_mine[k], normed_theirs[k], smalls[k], tap_sums[k] = attend_row_back(
            hold(core), *branch_rows[k], out_own, joined, saved[k], since_rows[k], mix, taps_backward, gain_pad,
            taps_q, taps_k, head_size,
        )

    attend_back(0)
    flow.end(grad_joined[0], gb_x, gb_y)
    gb_xo, gb_yo = seq_swap(hold(gb_x)), seq_swap(hold(gb_y))
    branch_rows[1], branch_rows[2] = (gb_x, gb_xo), (gb_y, gb_yo)
    flow.end(gb_xo, gb_yo)
    corner_low, corner_high = y_swap(hold(half_rows(gb_x, False))), x_swap(hold(half_rows(gb_y, True)))
    to_y, to_x = x_swap(hold(low)), y_swap(hold(high))
    attend_back(1)
    flow.end(grad_joined[1], corner_low, corner_high, to_x, to_y)
    low_x = low_sum(feed_out[1][0], feed_came[1], hold(to_x), True)
    low_y = low_sum(feed_out[2][0], feed_came[2], hold(to_y), False)
    gb_c = jnp.concatenate([corner_low, corner_high], 0)
    flow.end(low_x, low_y, gb_c)
    feed_x, feed_y = x_swap(hold(low_x)), y_swap(hold(low_y))
    gb_co = seq_swap(hold(gb_c))
    branch_rows[3] = (gb_c, gb_co)
    normed_came = [None] * 4
    normed_came[1] = seq_swap(hold(normed_theirs[1]))
    attend_back(2)
    flow.end(grad_joined[2], gb_co, normed_came[1], feed_x, feed_y)
    block_out = (residual + whole_sum(feed_out[0][0], hold(feed_came[0]), feed_x, feed_y)).astype(jnp.bfloat16)
    normed_came[2] = seq_swap(hold(normed_theirs[2]))
    grad_out_own = weight_grad(grouped_rows, [hold(a) for k in branch_rows for a in k], LANES, "out_grad")
    grad_out_own = grad_out_own.reshape(2, LANES, width)[:, :head_size].reshape(2 * head_size, width)
    low_x = pair_sum(normed_mine[1], hold(normed_came[1]))
    flow.end(normed_came[2], grad_out_own, low_x)
    low_y = pair_sum(normed_mine[2], hold(normed_came[2]))
    flow.end(low_x, low_y)
    grad_x, grad_y = x_swap(hold(low_x)), y_swap(hold(low_y))
    out_terms = hold(grad_out_own)
    if ring:
        out_terms = exchange_plane(out_terms.reshape(4, out_rows, width))
    attend_back(3)
    flow.end(grad_joined[3], grad_x, grad_y, out_terms)

    normed_came[3], normed_came[0] = seq_swap(hold(normed_theirs[3])), seq_swap(hold(normed_theirs[0]))
    flow.end(normed_came[3], normed_came[0])
    low = pair_sum(normed_mine[3], hold(normed_came[3]))
    flow.end(low)
    grad_d = diagonal_swap(hold(low))
    out_came = [out_terms]
    if ring:
        out_came = [wide_shift(hold(wide_block(out_terms, -step)), step) for step in range(1, 4)]
    joined_grad_own = weight_grad(
        [hold(a) for k in normed_rows for a in k], grad_joined, 2 * LANES, "joined_grad"
    )
    flow.end(grad_d, joined_grad_own, *out_came)
    shard_joined = scatter_wide(hold(joined_grad_own))
    if ring:
        out_sum = wide_block(out_terms, 0).astype(jnp.float32)
        for came in out_came:
            out_sum = out_sum + hold(came).astype(jnp.float32)
        shard_feed = jnp.concatenate([shard_feed, out_sum.astype(jnp.bfloat16)], 0)
    flow.end(shard_feed)
    feed_x, feed_y, feed_o = x_swap(hold(shard_feed)), y_swap(hold(shard_feed)), seq_swap(hold(shard_feed))
    grad_normed = whole_sum(normed_mine[0], normed_came[0], grad_x, grad_y) + hold(grad_d).astype(jnp.float32)
    norm_part, grad_norm = norm_back(inputs_f, scale_in, norm_gain, grad_normed)
    grad_input = norm_part + grad_residual
    small = hold(smalls[0] + smalls[1] + smalls[2] + smalls[3])
    taps = jnp.sum(tap_sums[0] + tap_sums[1] + tap_sums[2] + tap_sums[3], axis=2) * scaling

    def placed(array, total):
        array = array.reshape(-1)
        return lax.dynamic_update_slice(jnp.zeros((total,), jnp.float32), array, (part * array.shape[0],))

    pieces = [
        grad_feed,
        placed(small[:2, :head_size], width),
        placed(hold(taps), head_count * taps_q * taps_k),
        placed(jnp.sum(small[2:6], axis=1), 2 * head_count),
    ]
    lengths = [a.shape[0] for a in pieces]
    fill = -(sum(lengths) + width) % (8 * LANES)
    packed = jnp.concatenate(pieces + [jnp.zeros((fill,), jnp.float32)]).reshape(-1, LANES)
    packed = jnp.concatenate([packed, grad_norm.reshape(-1, LANES)], 0)
    flow.end(packed, feed_x, feed_y, feed_o)
    packed = packed + seq_swap(hold(packed))
    feed_low, feed_high = y_swap(hold(half_rows(feed_x, False))), x_swap(hold(half_rows(feed_y, True)))
    feed_xo, feed_yo = seq_swap(hold(feed_x)), seq_swap(hold(feed_y))
    flow.end(feed_low, feed_high, feed_xo, feed_yo, packed, shard_joined)

    def columns(rows_of, sections, size):
        if 2 * size % LANES == 0:
            return place_columns(place, [a for k in rows_of for a in k], sections, size)
        every = lax.all_gather(rows_of[0][0], PLANE, axis=0)[:, :, : sections * size]
        split = every.reshape(cores, rows_of[0][0].shape[0], sections, size)
        return jnp.moveaxis(split, 0, 2).reshape(rows_of[0][0].shape[0], -1).astype(jnp.float32)

    def wide_sums(array, hops):
        if wide & (wide - 1):
            return lax.psum(array, "wide") if 1 in hops else array
        for hop in hops:
            array = array + lax.ppermute(array, "wide", [(i, i ^ hop) for i in range(wide)])
        return array

    joined_x, joined_y, joined_o = x_swap(hold(shard_joined)), y_swap(hold(shard_joined)), seq_swap(hold(shard_joined))
    feed_c = jnp.concatenate([feed_low, feed_high], 0)
    feed_co = seq_swap(hold(feed_c))
    packed = wide_sums(hold(packed), [1])
    flow.end(joined_x, joined_y, joined_o, feed_co, packed)
    joined_low, joined_high = y_swap(hold(half_rows(joined_x, False))), x_swap(hold(half_rows(joined_y, True)))
    joined_xo, joined_yo = seq_swap(hold(joined_x)), seq_swap(hold(joined_y))
    packed = wide_sums(hold(packed), [2 << i for i in range(16) if 2 << i < wide])
    if ring:
        grad_gate, grad_down, grad_out = place_feed(
            place, [hold(shard_feed), feed_o, feed_x, feed_xo, feed_y, feed_yo, feed_c, feed_co], chunk,
            width // feed_cols,
        )
    else:
        every = lax.all_gather(shard_feed, PLANE, axis=0)
        split = every[:, :, : 2 * feed_cols].reshape(cores, shard_feed.shape[0], 2 * wide, chunk)
        grad_gate = jnp.moveaxis(split, 0, 2).reshape(shard_feed.shape[0], -1).astype(jnp.float32)
        split = every[:, :, 2 * feed_cols :].reshape(cores, width // feed_cols, chunk, feed_cols)
        grad_down = jnp.swapaxes(split, 1, 2).reshape(cores * chunk, width).astype(jnp.float32)
        grad_out = scatter_wide(lax.all_gather(out_terms, PLANE, axis=0, tiled=True)).astype(jnp.float32)
    flow.end(joined_low, joined_high, joined_xo, joined_yo, packed, grad_gate)
    joined_c = jnp.concatenate([joined_low, joined_high], 0)
    joined_co = seq_swap(hold(joined_c))
    packed = packed + x_swap(hold(packed))
    packed = packed + y_swap(packed)
    joined_rows = [(shard_joined, joined_o), (joined_x, joined_xo), (joined_y, joined_yo), (joined_c, joined_co)]
    grad_qkv = columns(joined_rows, 3, group_cols)
    packed = packed.reshape(-1)
    grad_norm = packed[-width:]
    parts = []
    for length in lengths:
        parts.append(packed[:length])
        packed = packed[length:]
    grad_feed, grad_group, grad_kernel, grad_mix = parts
    return (
        block_out,
        grad_input,
        grad_norm,
        grad_qkv,
        grad_kernel.reshape(head_count, taps_q, taps_k),
        grad_mix.reshape(head_count, 2),
        grad_group,
        grad_out,
        grad_feed,
        grad_gate,
        grad_down,
    )


def solution(mesh):
    tokens = P(("narrow", "wide", "seq"), None)
    rows = P("wide", None)
    return jax.shard_map(
        on_device,
        mesh=mesh,
        in_specs=(tokens, P(("narrow", "wide", "seq")), P(), rows, P(), P(), P(), rows, P(), rows, rows, tokens),
        out_specs=(tokens, tokens, P(), rows, P(), P(), P(), rows, P(), rows, rows),
        check_vma=False,
    )
```

```python
import functools
import jax
import jax.numpy as jnp
from jax import lax
from jax.experimental import pallas as pl
from jax.experimental.pallas import tpu as pltpu

LANES = 128
EDGE = 64
TOP = 16
ROOM = 60 * 1024 * 1024
LIGHT = pl.CostEstimate(flops=1_000_000, bytes_accessed=1_000_000, transcendentals=0)


def cost(micros):
    return pl.CostEstimate(flops=0, bytes_accessed=3_600_000 * micros, transcendentals=0)


def taps_kernel(taps_q, taps_k, scaling, kernel_ref, forward_ref, backward_ref):
    half = (taps_k - 1) // 2
    row = lax.broadcasted_iota(jnp.int32, (2 * LANES, LANES), 0)
    col = lax.broadcasted_iota(jnp.int32, (2 * LANES, LANES), 1)
    forth = col - row + EDGE + half
    back = row - col - EDGE + half
    for head in range(2):
        for tap in range(taps_q):
            ahead = jnp.zeros((2 * LANES, LANES), jnp.float32)
            behind = jnp.zeros((2 * LANES, LANES), jnp.float32)
            for tap_k in range(taps_k):
                value = kernel_ref[head, tap, tap_k]
                ahead = jnp.where(forth == tap_k, value, ahead)
                behind = jnp.where(back == tap_k, value, behind)
            ahead = ahead * scaling
            high = ahead.astype(jnp.bfloat16)
            cols = slice(tap * LANES, (tap + 1) * LANES)
            forward_ref[head, : 2 * LANES, cols] = high
            forward_ref[head, 2 * LANES : 4 * LANES, cols] = high
            forward_ref[head, 4 * LANES :, cols] = (ahead - high.astype(jnp.float32)).astype(jnp.bfloat16)
            backward_ref[head, tap * 2 * LANES : (tap + 1) * 2 * LANES, :] = behind.astype(jnp.bfloat16)


def tap_bands(kernels, scaling):
    heads, taps_q, taps_k = kernels.shape
    return pl.pallas_call(
        functools.partial(taps_kernel, taps_q, taps_k, scaling),
        out_shape=(
            jax.ShapeDtypeStruct((heads, 6 * LANES, taps_q * LANES), jnp.bfloat16),
            jax.ShapeDtypeStruct((heads, taps_q * 2 * LANES, LANES), jnp.bfloat16),
        ),
        in_specs=[pl.BlockSpec(memory_space=pltpu.SMEM)],
        out_specs=(pl.BlockSpec(memory_space=pltpu.VMEM),) * 2,
        compiler_params=pltpu.CompilerParams(vmem_limit_bytes=32 * 1024 * 1024),
        cost_estimate=LIGHT,
        name="tap_bands",
    )(kernels)


def place_columns_kernel(sections, chunk, where_ref, *refs):
    ins, out_ref = refs[:-1], refs[-1]
    line, core = where_ref[0], where_ref[1]
    width = 2 * chunk
    chips = len(ins) // 2
    for k in range(chips):
        own = ins[2 * k][...].astype(jnp.float32)
        other = ins[2 * k + 1][...].astype(jnp.float32)
        first = jnp.where(core == 0, own, other)
        second = jnp.where(core == 0, other, own)
        for s in range(sections):
            both = jnp.concatenate([first[:, s * chunk : (s + 1) * chunk], second[:, s * chunk : (s + 1) * chunk]], 1)
            at = pl.multiple_of(s * chips * width + (line ^ k) * width, LANES)
            out_ref[:, pl.ds(at, width)] = both


def place_columns(place, pieces, sections, chunk):
    rows, cols = pieces[0].shape
    cols_out = sections * chunk * len(pieces)
    steps = 4 if rows % 64 == 0 else 1
    spec = pl.BlockSpec((rows // steps, cols), lambda s, place: (s, 0))
    return pl.pallas_call(
        functools.partial(place_columns_kernel, sections, chunk),
        out_shape=jax.ShapeDtypeStruct((rows, cols_out), jnp.float32),
        grid_spec=pltpu.PrefetchScalarGridSpec(
            num_scalar_prefetch=1,
            grid=(steps,),
            in_specs=[spec] * len(pieces),
            out_specs=pl.BlockSpec((rows // steps, cols_out), lambda s, place: (s, 0)),
        ),
        compiler_params=pltpu.CompilerParams(vmem_limit_bytes=ROOM),
        cost_estimate=cost(5),
        name="place_columns",
    )(place, *pieces)


def place_feed_kernel(sections, chunk, pieces, where_ref, *refs):
    ins, extras = refs[:pieces], refs[pieces : 2 * pieces]
    gate_ref, down_ref, out_ref = refs[2 * pieces :]
    line, core = where_ref[0], where_ref[1]
    width = 2 * chunk
    chips = pieces // 2
    gate_cols = sections * chunk
    for k in range(chips):
        own = ins[2 * k][...].astype(jnp.float32)
        other = ins[2 * k + 1][...].astype(jnp.float32)
        first = jnp.where(core == 0, own, other)
        second = jnp.where(core == 0, other, own)
        for s in range(sections):
            both = jnp.concatenate([first[:, s * chunk : (s + 1) * chunk], second[:, s * chunk : (s + 1) * chunk]], 1)
            at = pl.multiple_of(s * chips * width + (line ^ k) * width, LANES)
            gate_ref[:, pl.ds(at, width)] = both
        at = pl.multiple_of((line ^ k) * width, width)
        down_ref[pl.ds(at, chunk), :] = first[:, gate_cols:]
        down_ref[pl.ds(at + chunk, chunk), :] = second[:, gate_cols:]

    @pl.when(pl.program_id(0) == 0)
    def _():
        rows = extras[0].shape[0]
        for k in range(chips):
            for e in range(2):
                at = pl.multiple_of(((core ^ e) * chips + (line ^ k)) * rows, rows)
                out_ref[pl.ds(at, rows), :] = extras[2 * k + e][...].astype(jnp.float32)


def place_feed(place, pieces, chunk, blocks):
    rows, cols = pieces[0].shape
    extra = rows - blocks * chunk
    sections = (cols // chunk) * 2 // 3
    hidden = cols - sections * chunk
    gate_cols = sections * chunk * len(pieces)
    last = blocks * chunk // extra
    return pl.pallas_call(
        functools.partial(place_feed_kernel, sections, chunk, len(pieces)),
        out_shape=(
            jax.ShapeDtypeStruct((blocks * chunk, gate_cols), jnp.float32),
            jax.ShapeDtypeStruct((chunk * len(pieces), hidden * blocks), jnp.float32),
            jax.ShapeDtypeStruct((extra * len(pieces), cols), jnp.float32),
        ),
        grid_spec=pltpu.PrefetchScalarGridSpec(
            num_scalar_prefetch=1,
            grid=(blocks,),
            in_specs=[pl.BlockSpec((chunk, cols), lambda s, place: (s, 0))] * len(pieces)
            + [pl.BlockSpec((extra, cols), lambda s, place: (last, 0))] * len(pieces),
            out_specs=(
                pl.BlockSpec((chunk, gate_cols), lambda s, place: (s, 0)),
                pl.BlockSpec((chunk * len(pieces), hidden), lambda s, place: (0, s)),
                pl.BlockSpec((extra * len(pieces), cols), lambda s, place: (0, 0)),
            ),
        ),
        compiler_params=pltpu.CompilerParams(vmem_limit_bytes=ROOM),
        cost_estimate=cost(11),
        name="place_feed",
    )(place, *pieces, *pieces)


def masked_scores(q_blk, keys, since, first_row):
    scores = lax.dot_general(q_blk, keys, (((1,), (1,)), ((), ())), preferred_element_type=jnp.float32)
    rows = first_row + lax.broadcasted_iota(jnp.int32, scores.shape, 0)
    back = rows + EDGE - lax.broadcasted_iota(jnp.int32, scores.shape, 1)
    limit = jnp.concatenate([since] * (scores.shape[1] // LANES), 1)
    return jnp.where((back >= 0) & (back <= limit), scores, 0.0)


def head_places(heads, head_size):
    return [((head * head_size) // LANES, (head * head_size) % LANES) for head in range(heads)]


def split_heads(joined, heads, head_size):
    real = lax.broadcasted_iota(jnp.int32, (joined.shape[0], LANES), 1) < head_size
    out = []
    for tile, shift in head_places(heads, head_size):
        if shift:
            both = joined[:, tile * LANES : (tile + 2) * LANES]
            piece = pltpu.roll(both, 2 * LANES - shift, 1)[:, :LANES]
        else:
            piece = joined[:, tile * LANES : (tile + 1) * LANES]
        out.append(jnp.where(real, piece, 0.0))
    return out


def join_heads(pieces, head_size):
    count = pieces[0].shape[0]
    nothing = jnp.zeros((count, LANES), jnp.float32)
    tiles = [nothing] * 5
    for piece, (tile, shift) in zip(pieces, head_places(len(pieces), head_size)):
        if shift:
            both = pltpu.roll(jnp.concatenate([piece, nothing], 1), shift, 1)
            tiles[tile] = tiles[tile] + both[:, :LANES]
            tiles[tile + 1] = tiles[tile + 1] + both[:, LANES:]
        else:
            tiles[tile] = tiles[tile] + piece
    return jnp.concatenate(tiles, 1)


def forward_kernel(taps_q, head_size, rows, core_ref, mix_ref, since_all, joined_ref, taps_ref, gain_ref, *refs):
    halves, outs = refs[: 2 * rows], refs[2 * rows : 2 * rows + 4]
    pieces, proj, att, grouped, maps, keys_pad, s_high, s_low, spread, grouped_row, in_sems, out_sems = refs[2 * rows + 4 :]
    arrivals = [pltpu.make_async_copy(ref, pieces.at[i], in_sems.at[i]) for i, ref in enumerate(halves)]
    for arrival in arrivals:
        arrival.start()
    seq_len = proj.shape[1]
    half_len = seq_len // 2
    blocks = seq_len // LANES
    core = core_ref[0]
    keys_pad[...] = jnp.zeros_like(keys_pad)
    s_high[...] = jnp.zeros_like(s_high)
    s_low[...] = jnp.zeros_like(s_low)
    for arrival in arrivals:
        arrival.wait()

    def project(step, carry):
        row, part = lax.div(step, 2), lax.rem(step, 2)
        at = pl.multiple_of(jnp.bitwise_xor(core, part) * half_len, half_len)
        joined = jnp.dot(pieces[step], joined_ref[...], preferred_element_type=jnp.float32)
        for head, piece in enumerate(split_heads(joined, 6, head_size)):
            proj[row, pl.ds(at, half_len), head * LANES : (head + 1) * LANES] = piece.astype(jnp.bfloat16)
        return carry

    lax.fori_loop(0, 2 * rows, project, 0)
    real = lax.broadcasted_iota(jnp.int32, (LANES, LANES), 1) < head_size

    def mix_row(row):
        for qi in range(blocks):
            first = qi * LANES
            width = (qi + 1) * LANES
            low = maps[row, 0, first : first + LANES, :width]
            upp = maps[row, 1, first : first + LANES, :width]
            for head in range(2):
                mixed = (mix_ref[head, 0] * low + mix_ref[head, 1] * upp).astype(jnp.bfloat16)
                cols = slice(head * LANES, (head + 1) * LANES)
                attended = jnp.dot(
                    mixed, proj[row, :width, (4 + head) * LANES : (5 + head) * LANES],
                    preferred_element_type=jnp.float32,
                )
                att[row, first : first + LANES, cols] = attended
                normal, _ = normalize(attended, real, head_size)
                grouped_row[first : first + LANES, cols] = (normal * gain_ref[:, cols]).astype(jnp.bfloat16)
        for part in range(2):
            at = pl.multiple_of(jnp.bitwise_xor(core, part) * half_len, half_len)
            grouped[row, part * half_len : (part + 1) * half_len, :] = grouped_row[pl.ds(at, half_len), :]
        for copy in copies_out(row):
            copy.start()

    def copies_out(row):
        return [
            pltpu.make_async_copy(here.at[row], there.at[row], out_sems.at[kind, row])
            for kind, (here, there) in enumerate(zip((proj, att, grouped, maps), outs))
        ]

    def one_head(step, carry):
        row, head = lax.div(step, 2), lax.rem(step, 2)
        proj_ref, since_ref, weights_ref = proj.at[row], since_all.at[row], maps.at[row]
        lane = pl.multiple_of(head * LANES, LANES)
        lane_k = pl.multiple_of((head + 2) * LANES, LANES)
        keys_pad[EDGE : EDGE + seq_len, :] = proj_ref[:, pl.ds(lane_k, LANES)]
        for qi in range(blocks):
            first = qi * LANES
            width = (qi + 2) * LANES
            scores = masked_scores(
                proj_ref[first : first + LANES, pl.ds(lane, LANES)],
                keys_pad[:width, :],
                since_ref[first : first + LANES, :],
                first,
            )
            high = scores.astype(jnp.bfloat16)
            s_high[TOP + first : TOP + first + LANES, :width] = high
            s_low[TOP + first : TOP + first + LANES, :width] = (scores - high.astype(jnp.float32)).astype(jnp.bfloat16)
        for m in range(blocks):
            first = m * LANES
            count = seq_len - first
            high = s_high[first:, first : first + 2 * LANES]
            left = jnp.concatenate([high, s_low[first:, first : first + 2 * LANES], high], 1)
            spread[first:, :] = jnp.dot(left, taps_ref[head], preferred_element_type=jnp.float32)
            since = since_ref[first:, :]
            logits = spread[TOP + first :, :LANES]
            for tap in range(1, taps_q):
                moved = spread[TOP + first - tap : TOP + seq_len - tap, tap * LANES : (tap + 1) * LANES]
                logits = logits + jnp.where(since >= tap, moved, 0.0)
            weights_ref[head, first:, first : first + LANES] = logits
        for qi in range(blocks):
            first = qi * LANES
            width = (qi + 1) * LANES
            logits = weights_ref[head, first : first + LANES, :width]
            rows = first + lax.broadcasted_iota(jnp.int32, logits.shape, 0)
            back = rows - lax.broadcasted_iota(jnp.int32, logits.shape, 1)
            limit = jnp.concatenate([since_ref[first : first + LANES, :]] * (qi + 1), 1)
            logits = jnp.where((back >= 0) & (back <= limit), logits, -1e30)
            raised = jnp.exp(logits - jnp.max(logits, axis=1, keepdims=True))
            weights_ref[head, first : first + LANES, :width] = raised / jnp.sum(raised, axis=1, keepdims=True)

        @pl.when(head == 1)
        def _():
            mix_row(row)

        return carry

    lax.fori_loop(0, 2 * rows, one_head, 0)
    for row in range(rows):
        for copy in copies_out(row):
            copy.wait()


def normalize(att, real, head_size):
    mean = jnp.sum(att, axis=1, keepdims=True) * (1.0 / head_size)
    centered = jnp.where(real, att - mean, 0.0)
    spread = jnp.sum(centered * centered, axis=1, keepdims=True) * (1.0 / head_size)
    scale = lax.rsqrt(spread + 1e-05)
    return centered * scale, scale


def attend_rows(core, halves, since, mix, joined, taps_forward, gain_pad, taps_q, head_size):
    rows, seq_len = since.shape[:2]
    full = seq_len + 2 * EDGE
    vmem = pl.BlockSpec(memory_space=pltpu.VMEM)
    smem = pl.BlockSpec(memory_space=pltpu.SMEM)
    anywhere = pl.BlockSpec(memory_space=pl.ANY)
    shapes = (
        ((rows, seq_len, 6 * LANES), jnp.bfloat16),
        ((rows, seq_len, 2 * LANES), jnp.float32),
        ((rows, seq_len, 2 * LANES), jnp.bfloat16),
        ((rows, 2, seq_len, seq_len), jnp.float32),
    )
    return pl.pallas_call(
        functools.partial(forward_kernel, taps_q, head_size, rows),
        out_shape=tuple(jax.ShapeDtypeStruct(*a) for a in shapes),
        in_specs=[smem, smem] + [vmem] * 4 + [anywhere] * len(halves),
        out_specs=(anywhere,) * 4,
        scratch_shapes=[pltpu.VMEM((len(halves),) + halves[0].shape, jnp.bfloat16)]
        + [pltpu.VMEM(*a) for a in shapes]
        + [
            pltpu.VMEM((full, LANES), jnp.bfloat16),
            pltpu.VMEM((TOP + seq_len, full), jnp.bfloat16),
            pltpu.VMEM((TOP + seq_len, full), jnp.bfloat16),
            pltpu.VMEM((TOP + seq_len, taps_q * LANES), jnp.float32),
            pltpu.VMEM((seq_len, 2 * LANES), jnp.bfloat16),
            pltpu.SemaphoreType.DMA((len(halves),)),
            pltpu.SemaphoreType.DMA((4, rows)),
        ],
        compiler_params=pltpu.CompilerParams(vmem_limit_bytes=52 * 1024 * 1024),
        cost_estimate=LIGHT,
        name="attend_rows",
    )(core, mix, since, joined, taps_forward, gain_pad, *halves)


def backward_kernel(
    taps_q, taps_k, head_size, scaling, row, core_ref, mix_ref, own_ref, other_ref, out_weight_ref, joined_ref,
    taps_ref, gain_ref, proj_all, since_all, att_all, weights_all,
    joined_grad_ref, mine_ref, theirs_ref, small_ref, tap_ref,
    keys_pad, grad_att, conv_grad, shifted, s_low, s_grad, since_pad, grad_ref, out_ref,
    proj_ref, since_ref, att_ref, weights_ref, sems,
):
    arrivals = [
        pltpu.make_async_copy(source.at[row], here, sems.at[i])
        for i, (source, here) in enumerate(
            ((since_all, since_ref), (att_all, att_ref), (proj_all, proj_ref), (weights_all, weights_ref))
        )
    ]
    for arrival in arrivals:
        arrival.start()
    seq_len = proj_ref.shape[0]
    half_len = seq_len // 2
    own_at = pl.multiple_of(core_ref[0] * half_len, half_len)
    other_at = pl.multiple_of((1 - core_ref[0]) * half_len, half_len)
    for ref, at in ((own_ref, own_at), (other_ref, other_at)):
        grad_ref[pl.ds(at, half_len), :] = lax.dot_general(
            ref[...], out_weight_ref[...], (((1,), (1,)), ((), ())), preferred_element_type=jnp.float32
        )
    blocks = seq_len // LANES
    half = (taps_k - 1) // 2
    full = seq_len + 2 * EDGE
    keys_pad[...] = jnp.zeros_like(keys_pad)
    s_low[...] = jnp.zeros_like(s_low)
    s_grad[...] = jnp.zeros_like(s_grad)
    shifted[...] = jnp.zeros_like(shifted)
    conv_grad[...] = jnp.zeros_like(conv_grad)
    for arrival in arrivals:
        arrival.wait()
    since_pad[:seq_len, :] = since_ref[...]
    since_pad[seq_len:, :] = jnp.zeros((8, LANES), jnp.int32)
    small_ref[...] = jnp.zeros_like(small_ref)

    real = lax.broadcasted_iota(jnp.int32, (LANES, LANES), 1) < head_size
    for head in range(2):
        cols = slice(head * LANES, (head + 1) * LANES)
        group_sum = jnp.zeros((1, LANES), jnp.float32)
        for qi in range(blocks):
            rows = slice(qi * LANES, (qi + 1) * LANES)
            normal, scale = normalize(att_ref[rows, cols], real, head_size)
            grad = grad_ref[rows, cols]
            group_sum = group_sum + jnp.sum(grad * normal, axis=0, keepdims=True)
            lift = grad * gain_ref[:, cols]
            mean = jnp.sum(lift, axis=1, keepdims=True) * (1.0 / head_size)
            along = jnp.sum(lift * normal, axis=1, keepdims=True) * (1.0 / head_size)
            grad_att[rows, cols] = jnp.where(real, scale * (lift - mean - normal * along), 0.0).astype(jnp.bfloat16)
        small_ref[head : head + 1, :] = group_sum

    sums = [[jnp.zeros((1, LANES), jnp.float32) for _ in range(2)] for _ in range(2)]
    grad_v = [[], []]
    for qi in range(blocks):
        first = qi * LANES
        width = (qi + 1) * LANES
        rows = slice(first, first + LANES)
        maps = [weights_ref[k, rows, :width] for k in range(2)]
        grad_mixed = []
        for head in range(2):
            cols = slice(head * LANES, (head + 1) * LANES)
            values = proj_ref[:width, (4 + head) * LANES : (5 + head) * LANES]
            gm = lax.dot_general(
                grad_att[rows, cols], values, (((1,), (1,)), ((), ())), preferred_element_type=jnp.float32
            )
            grad_mixed.append(gm)
        for head in range(2):
            for k in range(2):
                part = jnp.sum(grad_mixed[head] * maps[k], axis=0, keepdims=True)
                for b in range(qi + 1):
                    sums[head][k] = sums[head][k] + part[:, b * LANES : (b + 1) * LANES]
        for k in range(2):
            grad_w = mix_ref[0, k] * grad_mixed[0] + mix_ref[1, k] * grad_mixed[1]
            inner = jnp.sum(grad_w * maps[k], axis=1, keepdims=True)
            conv_grad[k, rows, :width] = maps[k] * (grad_w - inner)
    for head in range(2):
        for k in range(2):
            small_ref[2 + 2 * head + k : 3 + 2 * head + k, :] = sums[head][k]
        cols = slice(head * LANES, (head + 1) * LANES)
        for kb in range(blocks):
            first = kb * LANES
            mixed = (
                mix_ref[head, 0] * weights_ref[0, first:, first : first + LANES]
                + mix_ref[head, 1] * weights_ref[1, first:, first : first + LANES]
            ).astype(jnp.bfloat16)
            out_ref[first : first + LANES, (4 + head) * LANES : (5 + head) * LANES] = lax.dot_general(
                mixed, grad_att[first:, cols], (((0,), (0,)), ((), ())), preferred_element_type=jnp.float32
            )

    def one_head(head, carry):
        lane = pl.multiple_of(head * LANES, LANES)
        lane_k = pl.multiple_of((head + 2) * LANES, LANES)
        keys_pad[EDGE : EDGE + seq_len, :] = proj_ref[:, pl.ds(lane_k, LANES)]
        for qi in range(blocks):
            first = qi * LANES
            width = (qi + 2) * LANES
            scores = masked_scores(
                proj_ref[first : first + LANES, pl.ds(lane, LANES)],
                keys_pad[:width, :],
                since_ref[first : first + LANES, :],
                first,
            )
            s_low[TOP + first : TOP + first + LANES, :width] = scores.astype(jnp.bfloat16)
            reach = min(width, seq_len)
            for tap in range(taps_q):
                moved = conv_grad[head, first + tap : first + tap + LANES, :reach]
                if tap > 0:
                    limit = since_pad[first + tap : first + tap + LANES, :]
                    limit = jnp.concatenate([limit] * (reach // LANES), 1)
                    moved = jnp.where(limit >= tap, moved, 0.0)
                shifted[tap, TOP + first : TOP + first + LANES, LANES : LANES + reach] = moved.astype(jnp.bfloat16)
        for m in range(blocks + 1):
            first = max(m - 1, 0) * LANES
            left = jnp.concatenate(
                [shifted[tap, TOP + first :, m * LANES : (m + 2) * LANES] for tap in range(taps_q)], 1
            )
            grad = jnp.dot(left, taps_ref[head], preferred_element_type=jnp.float32)
            rows = first + lax.broadcasted_iota(jnp.int32, grad.shape, 0)
            back = rows + EDGE - m * LANES - lax.broadcasted_iota(jnp.int32, grad.shape, 1)
            keep = (back >= 0) & (back <= since_ref[first:, :])
            s_grad[first:, m * LANES : (m + 1) * LANES] = jnp.where(keep, grad, 0.0).astype(jnp.bfloat16)
        total = jnp.zeros((2 * LANES, taps_q * LANES), jnp.float32)
        for m in range(blocks):
            first = m * LANES
            right = jnp.concatenate(
                [shifted[tap, first:, (m + 1) * LANES : (m + 2) * LANES] for tap in range(taps_q)], 1
            )
            total = total + lax.dot_general(
                s_low[first:, first : first + 2 * LANES], right, (((0,), (0,)), ((), ())),
                preferred_element_type=jnp.float32,
            )
        ridge = lax.broadcasted_iota(jnp.int32, (2 * LANES, LANES), 1) - lax.broadcasted_iota(
            jnp.int32, (2 * LANES, LANES), 0
        )
        for tap_k in range(taps_k):
            on = ridge == tap_k - EDGE - half
            for tap in range(taps_q):
                line = jnp.where(on, total[:, tap * LANES : (tap + 1) * LANES], 0.0)
                tap_ref[head, tap * taps_k + tap_k : tap * taps_k + tap_k + 1, :] = jnp.sum(line, axis=0, keepdims=True)
        for qi in range(blocks):
            first = qi * LANES
            width = (qi + 2) * LANES
            grad_q = jnp.dot(
                s_grad[first : first + LANES, :width], keys_pad[:width, :], preferred_element_type=jnp.float32
            )
            out_ref[first : first + LANES, pl.ds(lane, LANES)] = grad_q * scaling
        for kb in range(blocks):
            first = kb * LANES
            grad_k = lax.dot_general(
                s_grad[first:, first + EDGE : first + EDGE + LANES],
                proj_ref[first:, pl.ds(lane, LANES)],
                (((0,), (0,)), ((), ())),
                preferred_element_type=jnp.float32,
            )
            out_ref[first : first + LANES, pl.ds(lane_k, LANES)] = grad_k * scaling
        return carry

    lax.fori_loop(0, 2, one_head, 0)
    for at, first in ((own_at, 0), (other_at, half_len)):
        pieces = [out_ref[pl.ds(at, half_len), head * LANES : (head + 1) * LANES] for head in range(6)]
        joined = join_heads(pieces, head_size).astype(jnp.bfloat16)
        joined_grad_ref[first : first + half_len, :] = joined
        grad_in = lax.dot_general(
            joined, joined_ref[...], (((1,), (1,)), ((), ())), preferred_element_type=jnp.float32
        )
        if first:
            theirs_ref[...] = grad_in.astype(jnp.bfloat16)
        else:
            mine_ref[...] = grad_in.astype(jnp.bfloat16)


def attend_row_back(
    row, core, own, other, out_weight, joined, saved, since, mix, taps_backward, gain_pad, taps_q, taps_k, head_size
):
    projected, att, weights = saved
    seq_len = projected.shape[1]
    width = own.shape[1]
    full = seq_len + 2 * EDGE
    vmem = pl.BlockSpec(memory_space=pltpu.VMEM)
    smem = pl.BlockSpec(memory_space=pltpu.SMEM)
    anywhere = pl.BlockSpec(memory_space=pl.ANY)
    return pl.pallas_call(
        functools.partial(backward_kernel, taps_q, taps_k, head_size, head_size ** (-0.5), row),
        out_shape=(
            jax.ShapeDtypeStruct((seq_len, joined.shape[1]), jnp.bfloat16),
            jax.ShapeDtypeStruct((seq_len // 2, width), jnp.bfloat16),
            jax.ShapeDtypeStruct((seq_len // 2, width), jnp.bfloat16),
            jax.ShapeDtypeStruct((8, LANES), jnp.float32),
            jax.ShapeDtypeStruct((2, taps_q * taps_k, LANES), jnp.float32),
        ),
        in_specs=[smem, smem] + [vmem] * 6 + [anywhere] * 4,
        out_specs=(vmem,) * 5,
        scratch_shapes=[
            pltpu.VMEM((full, LANES), jnp.bfloat16),
            pltpu.VMEM((seq_len, 2 * LANES), jnp.bfloat16),
            pltpu.VMEM((2, seq_len + 8, seq_len), jnp.float32),
            pltpu.VMEM((taps_q, TOP + seq_len, seq_len + 2 * LANES), jnp.bfloat16),
            pltpu.VMEM((TOP + seq_len, full), jnp.bfloat16),
            pltpu.VMEM((seq_len, full), jnp.bfloat16),
            pltpu.VMEM((seq_len + 8, LANES), jnp.int32),
            pltpu.VMEM((seq_len, 2 * LANES), jnp.float32),
            pltpu.VMEM((seq_len, 6 * LANES), jnp.float32),
            pltpu.VMEM(projected.shape[1:], jnp.bfloat16),
            pltpu.VMEM(since.shape[1:], jnp.int32),
            pltpu.VMEM(att.shape[1:], jnp.float32),
            pltpu.VMEM(weights.shape[1:], jnp.float32),
            pltpu.SemaphoreType.DMA((4,)),
        ],
        compiler_params=pltpu.CompilerParams(vmem_limit_bytes=48 * 1024 * 1024),
        cost_estimate=cost(14),
        name="attend_row_back",
    )(core, mix, own, other, out_weight, joined, taps_backward, gain_pad, projected, since, att, weights)


def split_kernel(wide, feed_ref, gate_ref, down_ref):
    cols = down_ref.shape[0]
    chunk = cols // wide
    blocks = down_ref.shape[1] // cols
    gate_ref[...] = feed_ref[:, : 2 * cols]
    for z in range(wide):
        for b in range(blocks):
            first = (z * blocks + b) * chunk
            down_ref[z * chunk : (z + 1) * chunk, b * cols : (b + 1) * cols] = feed_ref[first : first + chunk, 2 * cols :]


def split_feed(feed, wide):
    vmem = pl.BlockSpec(memory_space=pltpu.VMEM)
    rows, cols = feed.shape[0], feed.shape[1] // 3
    return pl.pallas_call(
        functools.partial(split_kernel, wide),
        out_shape=(
            jax.ShapeDtypeStruct((rows, 2 * cols), jnp.bfloat16), jax.ShapeDtypeStruct((cols, rows), jnp.bfloat16),
        ),
        in_specs=[vmem],
        out_specs=(vmem,) * 2,
        compiler_params=pltpu.CompilerParams(vmem_limit_bytes=24 * 1024 * 1024),
        cost_estimate=LIGHT,
        name="split_feed",
    )(feed)


def feed_kernel(own_ref, other_ref, cot_own_ref, cot_other_ref, gate_ref, down_ref,
                hidden_ref, grads_ref, ffn_mine_ref, ffn_theirs_ref, back_mine_ref, back_theirs_ref):
    half_len = own_ref.shape[0]
    cols = down_ref.shape[0]
    for first, ref, cot_ref in ((0, own_ref, cot_own_ref), (half_len, other_ref, cot_other_ref)):
        rows = slice(first, first + half_len)
        both = jnp.dot(ref[...], gate_ref[...], preferred_element_type=jnp.float32)
        gating, upward = both[:, :cols], both[:, cols:]
        grad = lax.dot_general(
            cot_ref[...], down_ref[...], (((1,), (1,)), ((), ())), preferred_element_type=jnp.float32
        )
        sig = 1.0 / (1.0 + jnp.exp(-gating))
        silu = gating * sig
        hidden = (silu * upward).astype(jnp.bfloat16)
        hidden_ref[rows, :] = hidden
        grads_ref[rows, :cols] = (grad * upward * (sig * (1.0 + gating * (1.0 - sig)))).astype(jnp.bfloat16)
        grads_ref[rows, cols:] = (grad * silu).astype(jnp.bfloat16)
        back = lax.dot_general(
            grads_ref[rows, :], gate_ref[...], (((1,), (1,)), ((), ())), preferred_element_type=jnp.float32
        )
        ffn = jnp.dot(hidden, down_ref[...], preferred_element_type=jnp.float32)
        if first:
            back_theirs_ref[...] = back.astype(jnp.bfloat16)
            ffn_theirs_ref[...] = ffn.astype(jnp.bfloat16)
        else:
            back_mine_ref[...] = back.astype(jnp.bfloat16)
            ffn_mine_ref[...] = ffn.astype(jnp.bfloat16)


def feed_row(own, other, cot_own, cot_other, gate, down):
    half_len, width = own.shape
    cols = down.shape[0]
    vmem = pl.BlockSpec(memory_space=pltpu.VMEM)
    return pl.pallas_call(
        feed_kernel,
        out_shape=(
            jax.ShapeDtypeStruct((2 * half_len, cols), jnp.bfloat16),
            jax.ShapeDtypeStruct((2 * half_len, 2 * cols), jnp.bfloat16),
            jax.ShapeDtypeStruct((half_len, width), jnp.bfloat16),
            jax.ShapeDtypeStruct((half_len, width), jnp.bfloat16),
            jax.ShapeDtypeStruct((half_len, width), jnp.bfloat16),
            jax.ShapeDtypeStruct((half_len, width), jnp.bfloat16),
        ),
        in_specs=[vmem] * 6,
        out_specs=(vmem,) * 6,
        compiler_params=pltpu.CompilerParams(vmem_limit_bytes=48 * 1024 * 1024),
        cost_estimate=cost(8),
        name="feed_row",
    )(own, other, cot_own, cot_other, gate, down)


def feed_grad_kernel(counts, *refs):
    lefts, grads, hiddens, cots = (
        jnp.concatenate([ref[...] for ref in refs[sum(counts[:i]) : sum(counts[: i + 1])]], 0) for i in range(4)
    )
    out_ref = refs[-1]
    chunk = hiddens.shape[1]
    cols = out_ref.shape[1] - grads.shape[1]
    out_ref[:, : grads.shape[1]] = lax.dot_general(
        lefts, grads, (((0,), (0,)), ((), ())), preferred_element_type=jnp.float32
    ).astype(jnp.bfloat16)
    down = lax.dot_general(hiddens, cots, (((0,), (0,)), ((), ())), preferred_element_type=jnp.float32)
    for b in range(down.shape[1] // cols):
        out_ref[b * chunk : (b + 1) * chunk, grads.shape[1] :] = down[:, b * cols : (b + 1) * cols].astype(jnp.bfloat16)


def feed_grad(lefts, grads, hiddens, cots, wide):
    width = lefts[0].shape[1]
    cols = hiddens[0].shape[1]
    block, chunk = width // wide, cols // wide
    if block % LANES or chunk % LANES:
        gate = lax.dot_general(
            jnp.concatenate(lefts, 0), jnp.concatenate(grads, 0), (((0,), (0,)), ((), ())),
            preferred_element_type=jnp.float32,
        )
        down = lax.dot_general(
            jnp.concatenate(hiddens, 0), jnp.concatenate(cots, 0), (((0,), (0,)), ((), ())),
            preferred_element_type=jnp.float32,
        )
        down = jnp.swapaxes(down.reshape(wide, chunk, width // cols, cols), 1, 2).reshape(width, cols)
        return jnp.concatenate([gate, down], 1).astype(jnp.bfloat16)
    count = sum(a.shape[0] for a in lefts)
    cols_out = grads[0].shape[1] + cols
    return pl.pallas_call(
        functools.partial(feed_grad_kernel, (len(lefts), len(grads), len(hiddens), len(cots))),
        out_shape=jax.ShapeDtypeStruct((width, cols_out), jnp.bfloat16),
        grid=(wide,),
        in_specs=[pl.BlockSpec((a.shape[0], block), lambda s: (0, s)) for a in lefts]
        + [pl.BlockSpec(a.shape, lambda s: (0, 0)) for a in grads]
        + [pl.BlockSpec((a.shape[0], chunk), lambda s: (0, s)) for a in hiddens]
        + [pl.BlockSpec(a.shape, lambda s: (0, 0)) for a in cots],
        out_specs=pl.BlockSpec((block, cols_out), lambda s: (s, 0)),
        compiler_params=pltpu.CompilerParams(vmem_limit_bytes=ROOM),
        cost_estimate=cost(17),
        name="feed_grad",
    )(*lefts, *grads, *hiddens, *cots)


def weight_kernel(lefts, *refs):
    left = jnp.concatenate([ref[...] for ref in refs[:lefts]], 0)
    right = jnp.concatenate([ref[...] for ref in refs[lefts:-1]], 0)
    refs[-1][...] = lax.dot_general(
        left, right, (((0,), (0,)), ((), ())), preferred_element_type=jnp.float32
    ).astype(jnp.bfloat16)


def small_weight_grad(lefts, rights, name):
    vmem = pl.BlockSpec(memory_space=pltpu.VMEM)
    return pl.pallas_call(
        functools.partial(weight_kernel, len(lefts)),
        out_shape=jax.ShapeDtypeStruct((lefts[0].shape[1], rights[0].shape[1]), jnp.bfloat16),
        in_specs=[vmem] * (len(lefts) + len(rights)),
        out_specs=vmem,
        compiler_params=pltpu.CompilerParams(vmem_limit_bytes=32 * 1024 * 1024),
        cost_estimate=cost(3),
        name=name,
    )(*lefts, *rights)


def weight_grad(lefts, rights, block, name):
    rows_out, cols_out = lefts[0].shape[1], rights[0].shape[1]
    count = sum(a.shape[0] for a in lefts)
    return pl.pallas_call(
        functools.partial(weight_kernel, len(lefts)),
        out_shape=jax.ShapeDtypeStruct((rows_out, cols_out), jnp.bfloat16),
        grid=(rows_out // block,),
        in_specs=[pl.BlockSpec((a.shape[0], block), lambda s: (0, s)) for a in lefts]
        + [pl.BlockSpec(a.shape, lambda s: (0, 0)) for a in rights],
        out_specs=pl.BlockSpec((block, cols_out), lambda s: (s, 0)),
        compiler_params=pltpu.CompilerParams(vmem_limit_bytes=ROOM),
        cost_estimate=cost(8),
        name=name,
    )(*lefts, *rights)


def halves_kernel(mine_ref, came_ref, low_ref, high_ref):
    cut = low_ref.shape[0]
    low_ref[...] = (mine_ref[:cut, :].astype(jnp.float32) + came_ref[:cut, :].astype(jnp.float32)).astype(jnp.bfloat16)
    high_ref[...] = (mine_ref[cut:, :].astype(jnp.float32) + came_ref[cut:, :].astype(jnp.float32)).astype(jnp.bfloat16)


def sum_halves(mine, came):
    half = jax.ShapeDtypeStruct((mine.shape[0] // 2, mine.shape[1]), jnp.bfloat16)
    vmem = pl.BlockSpec(memory_space=pltpu.VMEM)
    return pl.pallas_call(
        halves_kernel, out_shape=(half, half), in_specs=[vmem] * 2, out_specs=(vmem,) * 2,
        compiler_params=pltpu.CompilerParams(vmem_limit_bytes=16 * 1024 * 1024), cost_estimate=LIGHT, name="sum_halves",
    )(mine, came)


def sum_kernel(second, mine_ref, came_ref, extra_ref, out_ref):
    cut = extra_ref.shape[0]
    rows, rest = (slice(cut, 2 * cut), slice(0, cut)) if second else (slice(0, cut), slice(cut, 2 * cut))
    total = mine_ref[rows, :].astype(jnp.float32) + came_ref[rows, :].astype(jnp.float32) + extra_ref[...].astype(jnp.float32)
    out_ref[rows, :] = total.astype(jnp.bfloat16)
    out_ref[rest, :] = (mine_ref[rest, :].astype(jnp.float32) + came_ref[rest, :].astype(jnp.float32)).astype(jnp.bfloat16)


def low_sum(mine, came, extra, second):
    vmem = pl.BlockSpec(memory_space=pltpu.VMEM)
    return pl.pallas_call(
        functools.partial(sum_kernel, second), out_shape=jax.ShapeDtypeStruct(mine.shape, jnp.bfloat16),
        in_specs=[vmem] * 3, out_specs=vmem,
        compiler_params=pltpu.CompilerParams(vmem_limit_bytes=16 * 1024 * 1024), cost_estimate=LIGHT, name="low_sum",
    )(mine, came, extra)


def pair_kernel(mine_ref, came_ref, out_ref):
    out_ref[...] = (mine_ref[...].astype(jnp.float32) + came_ref[...].astype(jnp.float32)).astype(jnp.bfloat16)


def pair_sum(mine, came):
    vmem = pl.BlockSpec(memory_space=pltpu.VMEM)
    return pl.pallas_call(
        pair_kernel, out_shape=jax.ShapeDtypeStruct(mine.shape, jnp.bfloat16), in_specs=[vmem] * 2, out_specs=vmem,
        compiler_params=pltpu.CompilerParams(vmem_limit_bytes=16 * 1024 * 1024), cost_estimate=LIGHT, name="pair_sum",
    )(mine, came)


def place_out_kernel(place_ref, *refs):
    out_ref = refs[-1]
    out_ref[...] = jnp.zeros_like(out_ref)
    for step, ref in enumerate(refs[:-1]):
        chunk = jnp.bitwise_xor(place_ref[0], step)
        rows = ref.shape[0]
        at = pl.multiple_of(lax.div(chunk, 2) * LANES + lax.rem(chunk, 2) * rows, 16)
        out_ref[pl.ds(at, rows), :] = ref[...]


def place_out(place, pieces):
    vmem = pl.BlockSpec(memory_space=pltpu.VMEM)
    return pl.pallas_call(
        place_out_kernel,
        out_shape=jax.ShapeDtypeStruct((2 * LANES, pieces[0].shape[1]), jnp.bfloat16),
        in_specs=[pl.BlockSpec(memory_space=pltpu.SMEM)] + [vmem] * len(pieces),
        out_specs=vmem,
        compiler_params=pltpu.CompilerParams(vmem_limit_bytes=16 * 1024 * 1024),
        cost_estimate=LIGHT,
        name="place_out",
    )(place, *pieces)


def branch_kernel(grouped_ref, out_ref, *refs):
    weight = out_ref[...]
    for row in range(grouped_ref.shape[0]):
        mine_ref, theirs_ref = refs[2 * row : 2 * row + 2]
        half_len = mine_ref.shape[0]
        mine_ref[...] = jnp.dot(grouped_ref[row, :half_len, :], weight, preferred_element_type=jnp.float32).astype(
            jnp.bfloat16
        )
        theirs_ref[...] = jnp.dot(grouped_ref[row, half_len:, :], weight, preferred_element_type=jnp.float32).astype(
            jnp.bfloat16
        )


def branch_rows_of(grouped, out_own):
    vmem = pl.BlockSpec(memory_space=pltpu.VMEM)
    rows, half_len, width = grouped.shape[0], grouped.shape[1] // 2, out_own.shape[1]
    flat = pl.pallas_call(
        branch_kernel,
        out_shape=(
            jax.ShapeDtypeStruct((half_len, width), jnp.bfloat16),
        ) * (2 * rows),
        in_specs=[vmem] * 2,
        out_specs=(vmem,) * (2 * rows),
        compiler_params=pltpu.CompilerParams(vmem_limit_bytes=32 * 1024 * 1024),
        cost_estimate=LIGHT,
        name="branch",
    )(grouped, out_own)
    return flat[0::2], flat[1::2]


def pick_kernel(place_ref, *refs):
    ins, outs = refs[:4], refs[4:]
    for step, out in enumerate(outs):
        behind = jnp.bitwise_and(place_ref[2] - jnp.bitwise_xor(place_ref[0], step), 3)
        for k, ref in enumerate(ins):

            @pl.when(behind == k)
            def _():
                out[...] = ref[...]


def pick_out(place, pieces):
    vmem = pl.BlockSpec(memory_space=pltpu.VMEM)
    return pl.pallas_call(
        pick_kernel,
        out_shape=(jax.ShapeDtypeStruct(pieces[0].shape, pieces[0].dtype),) * 4,
        in_specs=[pl.BlockSpec(memory_space=pltpu.SMEM)] + [vmem] * 4,
        out_specs=(vmem,) * 4,
        compiler_params=pltpu.CompilerParams(vmem_limit_bytes=16 * 1024 * 1024),
        cost_estimate=LIGHT,
        name="pick_out",
    )(place, *pieces)


from jax.sharding import PartitionSpec as P

PLANE = ("narrow", "seq")
SWAP = [(0, 1), (1, 0)]


def seq_swap(array):
    return lax.ppermute(array, "seq", SWAP)


def x_swap(array):
    return lax.ppermute(array, "narrow", [(0, 1), (1, 0), (2, 3), (3, 2)])


def y_swap(array):
    return lax.ppermute(array, "narrow", [(0, 2), (2, 0), (1, 3), (3, 1)])


def diagonal_swap(array):
    return lax.ppermute(array, "narrow", [(i, i ^ 3) for i in range(4)])


def gather_plane(own):
    half = own.shape[0] // 2
    from_x = x_swap(own)
    from_y = y_swap(own)
    corner = jnp.concatenate([y_swap(from_x[:half]), x_swap(from_y[half:])], 0)
    return [(a, seq_swap(a)) for a in (own, from_x, from_y, corner)]


def after(array, *others):
    return lax.optimization_barrier((array, *others))[0] if others else array


class Steps:
    def __init__(self):
        self.ended = ()

    def hold(self, array):
        return after(array, *self.ended)

    def end(self, *arrays):
        self.ended = arrays


def half_rows(array, second):
    cut = array.shape[0] // 2
    return array[cut:] if second else array[:cut]


def whole_sum(mine, came, from_x, from_y):
    return mine.astype(jnp.float32) + came.astype(jnp.float32) + from_x.astype(jnp.float32) + from_y.astype(jnp.float32)


def wide_shift(array, by):
    count = lax.axis_size("wide")
    return lax.ppermute(array, "wide", [(i, (i + by) % count) for i in range(count)])


def wide_block(blocks, step):
    count = lax.axis_size("wide")
    at = (lax.axis_index("wide") - step) % count
    return lax.dynamic_index_in_dim(blocks, at, 0, keepdims=False)


def wide_stack(pieces):
    whole = jnp.zeros((len(pieces),) + pieces[0].shape, pieces[0].dtype)
    for step, piece in enumerate(pieces):
        whole = lax.dynamic_update_index_in_dim(whole, piece, (lax.axis_index("wide") - step) % len(pieces), 0)
    return whole


def gather_wide(piece):
    return lax.all_gather(piece, "wide", axis=0, tiled=True)


def scatter_wide(whole):
    return lax.psum_scatter(whole, "wide", scatter_dimension=0, tiled=True)


def exchange_plane(blocks):
    line = lax.axis_index("narrow")

    def block(k):
        return lax.dynamic_index_in_dim(blocks, line ^ k, 0, keepdims=False)

    return [block(0), x_swap(block(1)), y_swap(block(2)), diagonal_swap(block(3))]


def in_place(pieces):
    line = lax.axis_index("narrow")
    whole = jnp.zeros((4,) + pieces[0].shape, pieces[0].dtype)
    for k in range(4):
        whole = lax.dynamic_update_index_in_dim(whole, pieces[k], line ^ k, 0)
    return whole


def pad_heads(array, head_size):
    heads = array.shape[1] // head_size
    split = array.reshape(array.shape[0], heads, head_size)
    return jnp.pad(split, ((0, 0), (0, 0), (0, LANES - head_size))).reshape(array.shape[0], heads * LANES)


def times(left, right):
    return jnp.dot(left, right, preferred_element_type=jnp.float32)


def norm_scale(values):
    return lax.rsqrt(jnp.mean(values * values, axis=-1, keepdims=True) + 1e-06)


def norm_back(values, scale, gain, grad):
    lift = grad * gain
    along = jnp.mean(lift * values, axis=-1, keepdims=True)
    return scale * lift - values * (scale * scale * scale * along), jnp.sum(grad * values * scale, axis=0)


def on_device(
    inputs,
    doc_start,
    norm_gain,
    qkv_weight,
    logit_kernel,
    head_mix,
    group_gain,
    out_weight,
    feed_gain,
    gate_up,
    down_weight,
    cotangent,
):
    tokens_dev, width = inputs.shape
    head_count, taps_q, taps_k = logit_kernel.shape
    head_size = width // head_count
    group_cols = 2 * head_size
    cores = lax.axis_size(PLANE)
    wide = lax.axis_size("wide")
    line = lax.axis_index("narrow")
    part = lax.axis_index(PLANE)
    chunk = gate_up.shape[1] // (2 * wide * cores)
    scaling = head_size ** (-0.5)

    core = lax.axis_index("seq").astype(jnp.int32).reshape(1)
    place = jnp.stack([line, lax.axis_index("seq"), lax.axis_index("wide")]).astype(jnp.int32)

    joined_piece = jnp.concatenate(
        [
            lax.dynamic_slice_in_dim(qkv_weight, s * width + part * group_cols, group_cols, 1)
            for s in range(3)
        ]
        + [jnp.zeros((qkv_weight.shape[0], -3 * group_cols % LANES), qkv_weight.dtype)],
        1,
    )
    joined = gather_wide(joined_piece)
    inputs, doc_start, out_weight = lax.optimization_barrier((inputs, doc_start, out_weight, joined_piece))[:3]

    flow = Steps()
    hold = flow.hold
    feed_cols = wide * chunk
    first_pos = lax.axis_index(("narrow", "wide", "seq")) * tokens_dev

    out_rows = group_cols // 4
    ring = wide == 4

    inputs_f = inputs.astype(jnp.float32)
    scale_in = norm_scale(inputs_f)
    normed = (inputs_f * scale_in * norm_gain).astype(jnp.bfloat16)
    since = first_pos + jnp.arange(tokens_dev, dtype=jnp.int32) - doc_start
    since_same = jnp.stack([since, x_swap(since), y_swap(since), diagonal_swap(since)])
    out_pieces = [lax.dynamic_slice_in_dim(out_weight, (lax.axis_index("seq") * 4 + line) * out_rows, out_rows, 0)]

    def out_step():
        if ring:
            out_pieces.append(wide_shift(hold(out_pieces[-1]), 1))

    out_step()
    flow.end(normed, out_pieces[-1])

    normed_x, normed_y, normed_o = x_swap(hold(normed)), y_swap(hold(normed)), seq_swap(hold(normed))
    out_step()
    kernels = lax.dynamic_slice_in_dim(logit_kernel, 2 * part, 2, 0)
    mix = lax.dynamic_slice_in_dim(head_mix, 2 * part, 2, 0)
    taps_forward, taps_backward = tap_bands(hold(kernels), scaling)
    gain_pad = pad_heads(lax.dynamic_slice_in_dim(group_gain, part * group_cols, group_cols, 0)[None], head_size)
    gate_piece = jnp.concatenate(
        [
            lax.dynamic_slice_in_dim(hold(gate_up), (s * cores + part) * chunk, chunk, 1)
            for s in range(2 * wide)
        ],
        1,
    )
    down_piece = lax.dynamic_slice_in_dim(hold(down_weight), part * chunk, chunk, 0)
    down_piece = jnp.concatenate(
        [down_piece[:, at : at + feed_cols] for at in range(0, width, feed_cols)], 0
    )
    feed_piece = jnp.concatenate([gate_piece, down_piece], 1)
    flow.end(normed_x, normed_y, normed_o, taps_forward, since_same, feed_piece, out_pieces[-1])

    low, high = half_rows(normed_x, False), half_rows(normed_y, True)
    flow.end(low, high, *flow.ended)
    corner_low, corner_high = y_swap(hold(low)), x_swap(hold(high))
    cot_x, cot_y = x_swap(hold(cotangent)), y_swap(hold(cotangent))
    out_step()
    since_other = seq_swap(hold(since_same))
    flow.end(corner_low, corner_high, since_other, out_pieces[-1])

    normed_c = jnp.concatenate([corner_low, corner_high], 0)
    normed_xo, normed_yo, normed_co = seq_swap(normed_x), seq_swap(normed_y), seq_swap(hold(normed_c))
    first = lax.axis_index("seq") == 0
    since_all = hold(
        jnp.concatenate([jnp.where(first, since_same, since_other), jnp.where(first, since_other, since_same)], 1)
    )
    since_rows = jnp.broadcast_to(since_all[:, :, None], since_all.shape + (LANES,))
    normed_rows = [(normed, normed_o), (normed_x, normed_xo), (normed_y, normed_yo), (normed_c, normed_co)]
    if ring:
        out_picked = pick_out(hold(place), out_pieces)
        flow.end(normed_co, normed_xo, normed_yo, joined, since_rows, *out_picked)
    else:
        flow.end(normed_co, normed_xo, normed_yo, joined, since_rows)

    feed_own = gather_wide(hold(feed_piece))
    if ring:
        out_picked = [hold(a) for a in out_picked]
        out_pieces = [
            out_picked[0], x_swap(out_picked[1]), y_swap(out_picked[2]), diagonal_swap(out_picked[3])
        ]
    projected, attended, grouped, weights = attend_rows(
        hold(core), [a for k in normed_rows for a in k], since_rows, mix, joined, taps_forward, gain_pad, taps_q,
        head_size,
    )
    flow.end(grouped, cot_x, cot_y, *out_pieces)
    if ring:
        out_own = place_out(hold(place), out_pieces)
    else:
        out_own = lax.dynamic_slice_in_dim(gather_wide(hold(out_weight)), part * group_cols, group_cols, 0)
        out_own = jnp.pad(
            out_own.reshape(2, head_size, width), ((0, 0), (0, LANES - head_size), (0, 0))
        ).reshape(2 * LANES, width)
    branch_mine, branch_theirs = branch_rows_of(grouped, out_own)
    flow.end(*branch_mine, *branch_theirs)
    came_3, came_1, came_2 = (seq_swap(hold(branch_theirs[k])) for k in (3, 1, 2))
    flow.end(came_3, came_1, came_2)
    low, high = sum_halves(branch_mine[3], hold(came_3))
    flow.end(low, high)
    to_y, to_x = x_swap(hold(low)), y_swap(hold(high))
    came_0, cot_o = seq_swap(hold(branch_theirs[0])), seq_swap(hold(cotangent))
    flow.end(came_0, to_x, to_y, cot_o)
    low_x = low_sum(branch_mine[1], came_1, hold(to_x), True)
    low_y = low_sum(branch_mine[2], came_2, hold(to_y), False)
    flow.end(low_x, low_y)
    cot_xo, cot_yo = seq_swap(hold(cot_x)), seq_swap(hold(cot_y))
    branch_x, branch_y = x_swap(hold(low_x)), y_swap(hold(low_y))
    flow.end(branch_x, branch_y, cot_xo, cot_yo, feed_own)
    residual = inputs_f + whole_sum(branch_mine[0], hold(came_0), branch_x, branch_y)
    scale_mid = norm_scale(residual)
    normed_ffn = (residual * scale_mid * feed_gain).astype(jnp.bfloat16)
    flow.end(normed_ffn)

    ffn_x, ffn_y, ffn_o = x_swap(hold(normed_ffn)), y_swap(hold(normed_ffn)), seq_swap(hold(normed_ffn))
    flow.end(ffn_o)
    hidden_rows, gate_grads, feed_out = [None] * 4, [None] * 4, [None] * 4
    ffn_rows = [(normed_ffn, ffn_o), None, None, None]
    cotangent_rows = [(cotangent, cot_o), (cot_x, cot_xo), (cot_y, cot_yo), None]

    gate_own, down_own = split_feed(hold(feed_own), wide)

    def feed(k):
        hidden_rows[k], gate_grads[k], *feed_out[k] = feed_row(
            hold(ffn_rows[k][0]), ffn_rows[k][1], *cotangent_rows[k], gate_own, down_own
        )

    feed(0)
    flow.end(hidden_rows[0], ffn_x, ffn_y)
    ffn_xo, ffn_yo = seq_swap(hold(ffn_x)), seq_swap(hold(ffn_y))
    ffn_rows[1], ffn_rows[2] = (ffn_x, ffn_xo), (ffn_y, ffn_yo)
    low, high = half_rows(cot_x, False), half_rows(cot_y, True)
    flow.end(ffn_xo, ffn_yo, low, high)
    cot_low, cot_high = y_swap(hold(low)), x_swap(hold(high))
    back_came = [None] * 4
    feed(1)
    flow.end(hidden_rows[1], cot_low, cot_high)
    low, high = half_rows(ffn_x, False), half_rows(ffn_y, True)
    cot_c = jnp.concatenate([cot_low, cot_high], 0)
    flow.end(low, high, cot_c)
    corner_low, corner_high = y_swap(hold(low)), x_swap(hold(high))
    cot_co = seq_swap(hold(cot_c))
    back_came[1] = seq_swap(hold(feed_out[1][3]))
    feed(2)
    flow.end(hidden_rows[2], corner_low, corner_high, cot_co, back_came[1])
    back_came[2] = seq_swap(hold(feed_out[2][3]))
    ffn_c = jnp.concatenate([corner_low, corner_high], 0)
    low_x = pair_sum(feed_out[1][2], hold(back_came[1]))
    flow.end(ffn_c, back_came[2], low_x)
    ffn_co = seq_swap(hold(ffn_c))
    low_y = pair_sum(feed_out[2][2], hold(back_came[2]))
    ffn_rows[3], cotangent_rows[3] = (ffn_c, ffn_co), (cot_c, cot_co)
    flow.end(ffn_co, low_x, low_y)
    back_x, back_y = x_swap(hold(low_x)), y_swap(hold(low_y))
    feed(3)
    flow.end(hidden_rows[3], back_x, back_y)
    back_came[3], back_came[0] = seq_swap(hold(feed_out[3][3])), seq_swap(hold(feed_out[0][3]))
    flow.end(back_came[3], back_came[0])
    low = pair_sum(feed_out[3][2], hold(back_came[3]))
    flow.end(low)
    back_d = diagonal_swap(hold(low))
    feed_grad_own = feed_grad(
        [hold(a) for k in ffn_rows for a in k], gate_grads, hidden_rows, [a for k in cotangent_rows for a in k], wide
    )
    flow.end(back_d, feed_grad_own)
    shard_feed = scatter_wide(hold(feed_grad_own))
    feed_came = [seq_swap(hold(feed_out[k][1])) for k in range(4)]
    grad_ffn = whole_sum(feed_out[0][2], back_came[0], back_x, back_y) + hold(back_d).astype(jnp.float32)
    norm_part, grad_feed = norm_back(residual, scale_mid, feed_gain, grad_ffn)
    grad_residual = norm_part + cotangent.astype(jnp.float32)
    grad_branch = grad_residual.astype(jnp.bfloat16)
    flow.end(grad_branch, *feed_came)

    gb_x, gb_y, gb_o = x_swap(hold(grad_branch)), y_swap(hold(grad_branch)), seq_swap(hold(grad_branch))
    low, high = sum_halves(feed_out[3][0], hold(feed_came[3]))
    flow.end(gb_o, low, high)
    branch_rows = [(grad_branch, gb_o), None, None, None]
    grad_joined, normed_mine, normed_theirs, smalls, tap_sums = ([None] * 4 for _ in range(5))

    def attend_back(k):
        grad_joined[k], normed_mine[k], normed_theirs[k], smalls[k], tap_sums[k] = attend_row_back(
            k, hold(core), *branch_rows[k], out_own, joined, (projected, attended, weights), since_rows, mix,
            taps_backward, gain_pad, taps_q, taps_k, head_size,
        )

    attend_back(0)
    flow.end(grad_joined[0], gb_x, gb_y)
    gb_xo, gb_yo = seq_swap(hold(gb_x)), seq_swap(hold(gb_y))
    branch_rows[1], branch_rows[2] = (gb_x, gb_xo), (gb_y, gb_yo)
    flow.end(gb_xo, gb_yo)
    corner_low, corner_high = y_swap(hold(half_rows(gb_x, False))), x_swap(hold(half_rows(gb_y, True)))
    to_y, to_x = x_swap(hold(low)), y_swap(hold(high))
    attend_back(1)
    flow.end(grad_joined[1], corner_low, corner_high, to_x, to_y)
    low_x = low_sum(feed_out[1][0], feed_came[1], hold(to_x), True)
    low_y = low_sum(feed_out[2][0], feed_came[2], hold(to_y), False)
    gb_c = jnp.concatenate([corner_low, corner_high], 0)
    flow.end(low_x, low_y, gb_c)
    gb_co = seq_swap(hold(gb_c))
    flow.end(low_x, low_y, gb_co)
    feed_main_x, feed_main_y = x_swap(hold(low_x)), y_swap(hold(low_y))
    branch_rows[3] = (gb_c, gb_co)
    normed_came = [None] * 4
    normed_came[1] = seq_swap(hold(normed_theirs[1]))
    attend_back(2)
    grad_out_own = small_weight_grad([grouped.reshape(-1, 2 * LANES)], [hold(a) for k in branch_rows for a in k], "out_grad")
    flow.end(grad_joined[2], normed_came[1], grad_out_own, feed_main_x, feed_main_y)
    normed_came[2] = seq_swap(hold(normed_theirs[2]))
    low_x = pair_sum(normed_mine[1], hold(normed_came[1]))
    grad_out_own = hold(grad_out_own).reshape(2, LANES, width)[:, :head_size].reshape(2 * head_size, width)
    flow.end(normed_came[2], low_x, grad_out_own)
    low_y = pair_sum(normed_mine[2], hold(normed_came[2]))
    flow.end(low_x, low_y)
    grad_x, grad_y = x_swap(hold(low_x)), y_swap(hold(low_y))
    out_terms = hold(grad_out_own)
    if ring:
        out_terms = in_place(exchange_plane(out_terms.reshape(4, out_rows, width)))
    attend_back(3)
    flow.end(grad_joined[3], grad_x, grad_y, out_terms)

    normed_came[3], normed_came[0] = seq_swap(hold(normed_theirs[3])), seq_swap(hold(normed_theirs[0]))
    flow.end(normed_came[3], normed_came[0])
    low = pair_sum(normed_mine[3], hold(normed_came[3]))
    flow.end(low)
    grad_d = diagonal_swap(hold(low))
    out_came = [out_terms]
    if ring:
        out_came = [wide_shift(hold(wide_block(out_terms, -step)), step) for step in range(1, 4)]
    joined_grad_own = weight_grad(
        [hold(a) for k in normed_rows for a in k], grad_joined, 2 * LANES, "joined_grad"
    )
    flow.end(grad_d, joined_grad_own, *out_came)
    shard_joined = scatter_wide(hold(joined_grad_own))
    if ring:
        out_sum = wide_block(out_terms, 0).astype(jnp.float32)
        for came in out_came:
            out_sum = out_sum + hold(came).astype(jnp.float32)
        shard_feed = jnp.concatenate([shard_feed, out_sum.astype(jnp.bfloat16)], 0)
    flow.end(shard_feed)
    feed_x, feed_y, feed_o = x_swap(hold(shard_feed)), y_swap(hold(shard_feed)), seq_swap(hold(shard_feed))
    grad_normed = whole_sum(normed_mine[0], normed_came[0], grad_x, grad_y) + hold(grad_d).astype(jnp.float32)
    norm_part, grad_norm = norm_back(inputs_f, scale_in, norm_gain, grad_normed)
    grad_input = norm_part + grad_residual
    small = hold(smalls[0] + smalls[1] + smalls[2] + smalls[3])
    taps = jnp.sum(tap_sums[0] + tap_sums[1] + tap_sums[2] + tap_sums[3], axis=2) * scaling

    def placed(array, total):
        array = array.reshape(-1)
        return lax.dynamic_update_slice(jnp.zeros((total,), jnp.float32), array, (part * array.shape[0],))

    pieces = [
        grad_feed,
        placed(small[:2, :head_size], width),
        placed(hold(taps), head_count * taps_q * taps_k),
        placed(jnp.sum(small[2:6], axis=1), 2 * head_count),
    ]
    lengths = [a.shape[0] for a in pieces]
    fill = -(sum(lengths) + width) % (8 * LANES)
    packed = jnp.concatenate(pieces + [jnp.zeros((fill,), jnp.float32)]).reshape(-1, LANES)
    packed = jnp.concatenate([packed, grad_norm.reshape(-1, LANES)], 0)
    packed = packed + seq_swap(packed)
    if wide & (wide - 1):
        packed = lax.psum(packed, "wide")
    else:
        for hop in [1 << i for i in range(16) if 1 << i < wide]:
            packed = packed + lax.ppermute(packed, "wide", [(i, i ^ hop) for i in range(wide)])
    flow.end(packed, feed_x, feed_y, feed_o)
    packed = packed + x_swap(hold(packed))
    feed_low, feed_high = y_swap(hold(half_rows(feed_x, False))), x_swap(hold(half_rows(feed_y, True)))
    feed_xo, feed_yo = seq_swap(hold(feed_x)), seq_swap(hold(feed_y))
    block_out = (residual + whole_sum(feed_out[0][0], hold(feed_came[0]), feed_main_x, feed_main_y)).astype(jnp.bfloat16)
    flow.end(feed_low, feed_high, feed_xo, feed_yo, packed, shard_joined, block_out)

    def columns(rows_of, sections, size):
        if 2 * size % LANES == 0:
            return place_columns(place, [a for k in rows_of for a in k], sections, size)
        every = lax.all_gather(rows_of[0][0], PLANE, axis=0)[:, :, : sections * size]
        split = every.reshape(cores, rows_of[0][0].shape[0], sections, size)
        return jnp.moveaxis(split, 0, 2).reshape(rows_of[0][0].shape[0], -1).astype(jnp.float32)

    joined_x, joined_y, joined_o = x_swap(hold(shard_joined)), y_swap(hold(shard_joined)), seq_swap(hold(shard_joined))
    feed_c = jnp.concatenate([feed_low, feed_high], 0)
    feed_co = seq_swap(hold(feed_c))
    if ring:
        grad_gate, grad_down, grad_out = place_feed(
            place, [hold(shard_feed), feed_o, feed_x, feed_xo, feed_y, feed_yo, feed_c, feed_co], chunk,
            width // feed_cols,
        )
    else:
        every = lax.all_gather(shard_feed, PLANE, axis=0)
        split = every[:, :, : 2 * feed_cols].reshape(cores, shard_feed.shape[0], 2 * wide, chunk)
        grad_gate = jnp.moveaxis(split, 0, 2).reshape(shard_feed.shape[0], -1).astype(jnp.float32)
        split = every[:, :, 2 * feed_cols :].reshape(cores, width // feed_cols, chunk, feed_cols)
        grad_down = jnp.swapaxes(split, 1, 2).reshape(cores * chunk, width).astype(jnp.float32)
        grad_out = scatter_wide(lax.all_gather(grad_out_own, PLANE, axis=0, tiled=True)).astype(jnp.float32)
    flow.end(joined_x, joined_y, joined_o, packed, grad_gate)
    joined_low, joined_high = y_swap(hold(half_rows(joined_x, False))), x_swap(hold(half_rows(joined_y, True)))
    joined_xo, joined_yo = seq_swap(hold(joined_x)), seq_swap(hold(joined_y))
    packed = packed + y_swap(hold(packed))
    flow.end(joined_low, joined_high, joined_xo, joined_yo, packed)
    joined_c = jnp.concatenate([joined_low, joined_high], 0)
    joined_co = seq_swap(hold(joined_c))
    joined_rows = [(shard_joined, joined_o), (joined_x, joined_xo), (joined_y, joined_yo), (joined_c, joined_co)]
    grad_qkv = columns(joined_rows, 3, group_cols)
    packed = packed.reshape(-1)
    grad_norm = packed[-width:]
    parts = []
    for length in lengths:
        parts.append(packed[:length])
        packed = packed[length:]
    grad_feed, grad_group, grad_kernel, grad_mix = parts
    return (
        block_out,
        grad_input,
        grad_norm,
        grad_qkv,
        grad_kernel.reshape(head_count, taps_q, taps_k),
        grad_mix.reshape(head_count, 2),
        grad_group,
        grad_out,
        grad_feed,
        grad_gate,
        grad_down,
    )


def solution(mesh):
    tokens = P(("narrow", "wide", "seq"), None)
    rows = P("wide", None)
    return jax.shard_map(
        on_device,
        mesh=mesh,
        in_specs=(tokens, P(("narrow", "wide", "seq")), P(), rows, P(), P(), P(), rows, P(), rows, rows, tokens),
        out_specs=(tokens, tokens, P(), rows, P(), P(), P(), rows, P(), rows, rows),
        check_vma=False,
    )
```

```python
import functools
import jax
import jax.numpy as jnp
from jax import lax
from jax.experimental import pallas as pl
from jax.experimental.pallas import tpu as pltpu

LANES = 128
EDGE = 64
TOP = 16
ROOM = 60 * 1024 * 1024
LIGHT = pl.CostEstimate(flops=1_000_000, bytes_accessed=1_000_000, transcendentals=0)


def cost(micros):
    return pl.CostEstimate(flops=0, bytes_accessed=3_600_000 * micros, transcendentals=0)


def taps_kernel(taps_q, taps_k, scaling, kernel_ref, forward_ref, backward_ref):
    half = (taps_k - 1) // 2
    row = lax.broadcasted_iota(jnp.int32, (2 * LANES, LANES), 0)
    col = lax.broadcasted_iota(jnp.int32, (2 * LANES, LANES), 1)
    forth = col - row + EDGE + half
    back = row - col - EDGE + half
    for head in range(2):
        for tap in range(taps_q):
            ahead = jnp.zeros((2 * LANES, LANES), jnp.float32)
            behind = jnp.zeros((2 * LANES, LANES), jnp.float32)
            for tap_k in range(taps_k):
                value = kernel_ref[head, tap, tap_k]
                ahead = jnp.where(forth == tap_k, value, ahead)
                behind = jnp.where(back == tap_k, value, behind)
            ahead = ahead * scaling
            high = ahead.astype(jnp.bfloat16)
            cols = slice(tap * LANES, (tap + 1) * LANES)
            forward_ref[head, : 2 * LANES, cols] = high
            forward_ref[head, 2 * LANES : 4 * LANES, cols] = high
            forward_ref[head, 4 * LANES :, cols] = (ahead - high.astype(jnp.float32)).astype(jnp.bfloat16)
            backward_ref[head, tap * 2 * LANES : (tap + 1) * 2 * LANES, :] = behind.astype(jnp.bfloat16)


def tap_bands(kernels, scaling):
    heads, taps_q, taps_k = kernels.shape
    return pl.pallas_call(
        functools.partial(taps_kernel, taps_q, taps_k, scaling),
        out_shape=(
            jax.ShapeDtypeStruct((heads, 6 * LANES, taps_q * LANES), jnp.bfloat16),
            jax.ShapeDtypeStruct((heads, taps_q * 2 * LANES, LANES), jnp.bfloat16),
        ),
        in_specs=[pl.BlockSpec(memory_space=pltpu.SMEM)],
        out_specs=(pl.BlockSpec(memory_space=pltpu.VMEM),) * 2,
        compiler_params=pltpu.CompilerParams(vmem_limit_bytes=32 * 1024 * 1024),
        cost_estimate=LIGHT,
        name="tap_bands",
    )(kernels)


def columns_pair(own_ref, other_ref, core, chunk, s):
    own = own_ref[:, s * chunk : (s + 1) * chunk].astype(jnp.float32)
    other = other_ref[:, s * chunk : (s + 1) * chunk].astype(jnp.float32)
    return jnp.concatenate([jnp.where(core == 0, own, other), jnp.where(core == 0, other, own)], 1)


def place_columns_kernel(sections, chunk, chips, where_ref, *refs):
    ins, out_ref = refs[:-1], refs[-1]
    line, core = where_ref[0], where_ref[1]
    width = 2 * chunk
    for k in range(len(ins) // 2):
        for s in range(sections):
            at = pl.multiple_of(s * chips * width + (line ^ k) * width, LANES)
            out_ref[:, pl.ds(at, width)] = columns_pair(ins[2 * k], ins[2 * k + 1], core, chunk, s)


def place_columns(place, pieces, sections, chunk, chips):
    rows, cols = pieces[0].shape
    cols_out = 2 * sections * chunk * chips
    steps = 4 if rows % 64 == 0 else 1
    spec = pl.BlockSpec((rows // steps, cols), lambda s, place: (s, 0))
    return pl.pallas_call(
        functools.partial(place_columns_kernel, sections, chunk, chips),
        out_shape=jax.ShapeDtypeStruct((rows, cols_out), jnp.float32),
        grid_spec=pltpu.PrefetchScalarGridSpec(
            num_scalar_prefetch=1,
            grid=(steps,),
            in_specs=[spec] * len(pieces),
            out_specs=pl.BlockSpec((rows // steps, cols_out), lambda s, place: (s, 0)),
        ),
        compiler_params=pltpu.CompilerParams(vmem_limit_bytes=24 * 1024 * 1024),
        cost_estimate=cost(5),
        name="place_columns",
    )(place, *pieces)


def add_columns_kernel(sections, chunk, chips, chip, place_ref, own_ref, other_ref, base_ref, out_ref, blocks, sems):
    del base_ref
    line, core = place_ref[0], place_ref[1]
    width = 2 * chunk
    copies = []
    for s in range(sections):
        blocks[s] = columns_pair(own_ref, other_ref, core, chunk, s)
        at = pl.multiple_of(s * chips * width + (line ^ chip) * width, LANES)
        copy = pltpu.make_async_copy(blocks.at[s], out_ref.at[:, pl.ds(at, width)], sems.at[s])
        copy.start()
        copies.append(copy)
    for copy in copies:
        copy.wait()


def add_columns(place, own, other, base, sections, chunk, chips, chip):
    vmem = pl.BlockSpec(memory_space=pltpu.VMEM)
    anywhere = pl.BlockSpec(memory_space=pl.ANY)
    return pl.pallas_call(
        functools.partial(add_columns_kernel, sections, chunk, chips, chip),
        out_shape=jax.ShapeDtypeStruct(base.shape, base.dtype),
        in_specs=[pl.BlockSpec(memory_space=pltpu.SMEM), vmem, vmem, anywhere],
        out_specs=anywhere,
        scratch_shapes=[
            pltpu.VMEM((sections, own.shape[0], 2 * chunk), jnp.float32), pltpu.SemaphoreType.DMA((sections,)),
        ],
        input_output_aliases={3: 0},
        compiler_params=pltpu.CompilerParams(vmem_limit_bytes=12 * 1024 * 1024),
        cost_estimate=cost(2),
        name="add_columns",
    )(place, own, other, base)


def place_feed_kernel(sections, chunk, pieces, where_ref, *refs):
    ins, gate_ref, down_ref = refs[:pieces], refs[pieces], refs[pieces + 1]
    line, core = where_ref[0], where_ref[1]
    width = 2 * chunk
    chips = pieces // 2
    gate_cols = sections * chunk
    for k in range(chips):
        own = ins[2 * k][...].astype(jnp.float32)
        other = ins[2 * k + 1][...].astype(jnp.float32)
        first = jnp.where(core == 0, own, other)
        second = jnp.where(core == 0, other, own)
        for s in range(sections):
            both = jnp.concatenate([first[:, s * chunk : (s + 1) * chunk], second[:, s * chunk : (s + 1) * chunk]], 1)
            at = pl.multiple_of(s * chips * width + (line ^ k) * width, LANES)
            gate_ref[:, pl.ds(at, width)] = both
        at = pl.multiple_of((line ^ k) * width, width)
        down_ref[pl.ds(at, chunk), :] = first[:, gate_cols:]
        down_ref[pl.ds(at + chunk, chunk), :] = second[:, gate_cols:]


def place_feed(place, pieces, chunk):
    rows, cols = pieces[0].shape
    blocks = rows // chunk
    sections = (cols // chunk) * 2 // 3
    hidden = cols - sections * chunk
    spec = pl.BlockSpec((chunk, cols), lambda s, place: (s, 0))
    gate_cols = sections * chunk * len(pieces)
    return pl.pallas_call(
        functools.partial(place_feed_kernel, sections, chunk, len(pieces)),
        out_shape=(
            jax.ShapeDtypeStruct((rows, gate_cols), jnp.float32),
            jax.ShapeDtypeStruct((chunk * len(pieces), hidden * blocks), jnp.float32),
        ),
        grid_spec=pltpu.PrefetchScalarGridSpec(
            num_scalar_prefetch=1,
            grid=(blocks,),
            in_specs=[spec] * len(pieces),
            out_specs=(
                pl.BlockSpec((chunk, gate_cols), lambda s, place: (s, 0)),
                pl.BlockSpec((chunk * len(pieces), hidden), lambda s, place: (0, s)),
            ),
        ),
        compiler_params=pltpu.CompilerParams(vmem_limit_bytes=ROOM),
        cost_estimate=cost(11),
        name="place_feed",
    )(place, *pieces)


def masked_scores(q_blk, keys, since, first_row):
    scores = lax.dot_general(q_blk, keys, (((1,), (1,)), ((), ())), preferred_element_type=jnp.float32)
    rows = first_row + lax.broadcasted_iota(jnp.int32, scores.shape, 0)
    back = rows + EDGE - lax.broadcasted_iota(jnp.int32, scores.shape, 1)
    limit = jnp.concatenate([since] * (scores.shape[1] // LANES), 1)
    return jnp.where((back >= 0) & (back <= limit), scores, 0.0)


def head_places(heads, head_size):
    return [((head * head_size) // LANES, (head * head_size) % LANES) for head in range(heads)]


def split_heads(joined, heads, head_size):
    real = lax.broadcasted_iota(jnp.int32, (joined.shape[0], LANES), 1) < head_size
    out = []
    for tile, shift in head_places(heads, head_size):
        if shift:
            both = joined[:, tile * LANES : (tile + 2) * LANES]
            piece = pltpu.roll(both, 2 * LANES - shift, 1)[:, :LANES]
        else:
            piece = joined[:, tile * LANES : (tile + 1) * LANES]
        out.append(jnp.where(real, piece, 0.0))
    return out


def join_heads(pieces, head_size):
    count = pieces[0].shape[0]
    nothing = jnp.zeros((count, LANES), jnp.float32)
    tiles = [nothing] * 5
    for piece, (tile, shift) in zip(pieces, head_places(len(pieces), head_size)):
        if shift:
            both = pltpu.roll(jnp.concatenate([piece, nothing], 1), shift, 1)
            tiles[tile] = tiles[tile] + both[:, :LANES]
            tiles[tile + 1] = tiles[tile + 1] + both[:, LANES:]
        else:
            tiles[tile] = tiles[tile] + piece
    return jnp.concatenate(tiles, 1)


def forward_kernel(taps_q, head_size, rows, core_ref, mix_ref, since_all, joined_ref, taps_ref, gain_ref, *refs):
    halves, outs = refs[: 2 * rows], refs[2 * rows : 2 * rows + 4]
    pieces, proj, att, grouped, maps, keys_pad, s_high, s_low, spread, grouped_row, in_sems, out_sems = refs[2 * rows + 4 :]
    arrivals = [pltpu.make_async_copy(ref, pieces.at[i], in_sems.at[i]) for i, ref in enumerate(halves)]
    for arrival in arrivals:
        arrival.start()
    seq_len = proj.shape[1]
    half_len = seq_len // 2
    blocks = seq_len // LANES
    core = core_ref[0]
    keys_pad[...] = jnp.zeros_like(keys_pad)
    s_high[...] = jnp.zeros_like(s_high)
    s_low[...] = jnp.zeros_like(s_low)

    def project(step, carry):
        pltpu.make_async_copy(halves[0], pieces.at[step], in_sems.at[step]).wait()
        row, part = lax.div(step, 2), lax.rem(step, 2)
        at = pl.multiple_of(jnp.bitwise_xor(core, part) * half_len, half_len)
        joined = jnp.dot(pieces[step], joined_ref[...], preferred_element_type=jnp.float32)
        for head, piece in enumerate(split_heads(joined, 6, head_size)):
            proj[row, pl.ds(at, half_len), head * LANES : (head + 1) * LANES] = piece.astype(jnp.bfloat16)
        return carry

    lax.fori_loop(0, 2 * rows, project, 0)
    real = lax.broadcasted_iota(jnp.int32, (LANES, LANES), 1) < head_size

    def mix_row(row):
        for qi in range(blocks):
            first = qi * LANES
            width = (qi + 1) * LANES
            low = maps[row, 0, first : first + LANES, :width]
            upp = maps[row, 1, first : first + LANES, :width]
            for head in range(2):
                mixed = (mix_ref[head, 0] * low + mix_ref[head, 1] * upp).astype(jnp.bfloat16)
                cols = slice(head * LANES, (head + 1) * LANES)
                attended = jnp.dot(
                    mixed, proj[row, :width, (4 + head) * LANES : (5 + head) * LANES],
                    preferred_element_type=jnp.float32,
                )
                att[row, first : first + LANES, cols] = attended
                normal, _ = normalize(attended, real, head_size)
                grouped_row[first : first + LANES, cols] = (normal * gain_ref[:, cols]).astype(jnp.bfloat16)
        for part in range(2):
            at = pl.multiple_of(jnp.bitwise_xor(core, part) * half_len, half_len)
            grouped[row, part * half_len : (part + 1) * half_len, :] = grouped_row[pl.ds(at, half_len), :]
        for copy in copies_out(row):
            copy.start()

    def copies_out(row):
        return [
            pltpu.make_async_copy(here.at[row], there.at[row], out_sems.at[kind, row])
            for kind, (here, there) in enumerate(zip((proj, att, grouped, maps), outs))
        ]

    def one_head(step, carry):
        row, head = lax.div(step, 2), lax.rem(step, 2)
        proj_ref, since_ref, weights_ref = proj.at[row], since_all.at[row], maps.at[row]
        lane = pl.multiple_of(head * LANES, LANES)
        lane_k = pl.multiple_of((head + 2) * LANES, LANES)
        keys_pad[EDGE : EDGE + seq_len, :] = proj_ref[:, pl.ds(lane_k, LANES)]
        for qi in range(blocks):
            first = qi * LANES
            width = (qi + 2) * LANES
            scores = masked_scores(
                proj_ref[first : first + LANES, pl.ds(lane, LANES)],
                keys_pad[:width, :],
                since_ref[first : first + LANES, :],
                first,
            )
            high = scores.astype(jnp.bfloat16)
            s_high[TOP + first : TOP + first + LANES, :width] = high
            s_low[TOP + first : TOP + first + LANES, :width] = (scores - high.astype(jnp.float32)).astype(jnp.bfloat16)
        for m in range(blocks):
            first = m * LANES
            count = seq_len - first
            high = s_high[first:, first : first + 2 * LANES]
            left = jnp.concatenate([high, s_low[first:, first : first + 2 * LANES], high], 1)
            spread[first:, :] = jnp.dot(left, taps_ref[head], preferred_element_type=jnp.float32)
            since = since_ref[first:, :]
            logits = spread[TOP + first :, :LANES]
            for tap in range(1, taps_q):
                moved = spread[TOP + first - tap : TOP + seq_len - tap, tap * LANES : (tap + 1) * LANES]
                logits = logits + jnp.where(since >= tap, moved, 0.0)
            weights_ref[head, first:, first : first + LANES] = logits
        for qi in range(blocks):
            first = qi * LANES
            width = (qi + 1) * LANES
            logits = weights_ref[head, first : first + LANES, :width]
            rows = first + lax.broadcasted_iota(jnp.int32, logits.shape, 0)
            back = rows - lax.broadcasted_iota(jnp.int32, logits.shape, 1)
            limit = jnp.concatenate([since_ref[first : first + LANES, :]] * (qi + 1), 1)
            logits = jnp.where((back >= 0) & (back <= limit), logits, -1e30)
            raised = jnp.exp(logits - jnp.max(logits, axis=1, keepdims=True))
            weights_ref[head, first : first + LANES, :width] = raised / jnp.sum(raised, axis=1, keepdims=True)

        @pl.when(head == 1)
        def _():
            mix_row(row)

        return carry

    lax.fori_loop(0, 2 * rows, one_head, 0)
    for row in range(rows):
        for copy in copies_out(row):
            copy.wait()


def normalize(att, real, head_size):
    mean = jnp.sum(att, axis=1, keepdims=True) * (1.0 / head_size)
    centered = jnp.where(real, att - mean, 0.0)
    spread = jnp.sum(centered * centered, axis=1, keepdims=True) * (1.0 / head_size)
    scale = lax.rsqrt(spread + 1e-05)
    return centered * scale, scale


def attend_rows(core, halves, since, mix, joined, taps_forward, gain_pad, taps_q, head_size):
    rows, seq_len = since.shape[:2]
    full = seq_len + 2 * EDGE
    vmem = pl.BlockSpec(memory_space=pltpu.VMEM)
    smem = pl.BlockSpec(memory_space=pltpu.SMEM)
    anywhere = pl.BlockSpec(memory_space=pl.ANY)
    shapes = (
        ((rows, seq_len, 6 * LANES), jnp.bfloat16),
        ((rows, seq_len, 2 * LANES), jnp.float32),
        ((rows, seq_len, 2 * LANES), jnp.bfloat16),
        ((rows, 2, seq_len, seq_len), jnp.float32),
    )
    return pl.pallas_call(
        functools.partial(forward_kernel, taps_q, head_size, rows),
        out_shape=tuple(jax.ShapeDtypeStruct(*a) for a in shapes),
        in_specs=[smem, smem] + [vmem] * 4 + [anywhere] * len(halves),
        out_specs=(anywhere,) * 4,
        scratch_shapes=[pltpu.VMEM((len(halves),) + halves[0].shape, jnp.bfloat16)]
        + [pltpu.VMEM(*a) for a in shapes]
        + [
            pltpu.VMEM((full, LANES), jnp.bfloat16),
            pltpu.VMEM((TOP + seq_len, full), jnp.bfloat16),
            pltpu.VMEM((TOP + seq_len, full), jnp.bfloat16),
            pltpu.VMEM((TOP + seq_len, taps_q * LANES), jnp.float32),
            pltpu.VMEM((seq_len, 2 * LANES), jnp.bfloat16),
            pltpu.SemaphoreType.DMA((len(halves),)),
            pltpu.SemaphoreType.DMA((4, rows)),
        ],
        compiler_params=pltpu.CompilerParams(vmem_limit_bytes=52 * 1024 * 1024),
        cost_estimate=LIGHT,
        name="attend_rows",
    )(core, mix, since, joined, taps_forward, gain_pad, *halves)


def backward_kernel(
    taps_q, taps_k, head_size, scaling, row, core_ref, mix_ref, own_ref, other_ref, out_weight_ref, joined_ref,
    taps_ref, gain_ref, proj_all, since_all, att_all, weights_all,
    joined_grad_ref, mine_ref, theirs_ref, small_ref, tap_ref,
    keys_pad, grad_att, conv_grad, shifted, s_low, s_grad, since_pad, grad_ref, out_ref,
    proj_ref, since_ref, att_ref, weights_ref, sems,
):
    arrivals = [
        pltpu.make_async_copy(source.at[row], here, sems.at[i])
        for i, (source, here) in enumerate(
            ((since_all, since_ref), (att_all, att_ref), (proj_all, proj_ref), (weights_all, weights_ref))
        )
    ]
    for arrival in arrivals:
        arrival.start()
    seq_len = proj_ref.shape[0]
    half_len = seq_len // 2
    own_at = pl.multiple_of(core_ref[0] * half_len, half_len)
    other_at = pl.multiple_of((1 - core_ref[0]) * half_len, half_len)
    for ref, at in ((own_ref, own_at), (other_ref, other_at)):
        grad_ref[pl.ds(at, half_len), :] = lax.dot_general(
            ref[...], out_weight_ref[...], (((1,), (1,)), ((), ())), preferred_element_type=jnp.float32
        )
    blocks = seq_len // LANES
    half = (taps_k - 1) // 2
    full = seq_len + 2 * EDGE
    keys_pad[...] = jnp.zeros_like(keys_pad)
    s_low[...] = jnp.zeros_like(s_low)
    s_grad[...] = jnp.zeros_like(s_grad)
    shifted[...] = jnp.zeros_like(shifted)
    conv_grad[...] = jnp.zeros_like(conv_grad)
    for arrival in arrivals:
        arrival.wait()
    since_pad[:seq_len, :] = since_ref[...]
    since_pad[seq_len:, :] = jnp.zeros((8, LANES), jnp.int32)
    small_ref[...] = jnp.zeros_like(small_ref)

    real = lax.broadcasted_iota(jnp.int32, (LANES, LANES), 1) < head_size
    for head in range(2):
        cols = slice(head * LANES, (head + 1) * LANES)
        group_sum = jnp.zeros((1, LANES), jnp.float32)
        for qi in range(blocks):
            rows = slice(qi * LANES, (qi + 1) * LANES)
            normal, scale = normalize(att_ref[rows, cols], real, head_size)
            grad = grad_ref[rows, cols]
            group_sum = group_sum + jnp.sum(grad * normal, axis=0, keepdims=True)
            lift = grad * gain_ref[:, cols]
            mean = jnp.sum(lift, axis=1, keepdims=True) * (1.0 / head_size)
            along = jnp.sum(lift * normal, axis=1, keepdims=True) * (1.0 / head_size)
            grad_att[rows, cols] = jnp.where(real, scale * (lift - mean - normal * along), 0.0).astype(jnp.bfloat16)
        small_ref[head : head + 1, :] = group_sum

    sums = [[jnp.zeros((1, LANES), jnp.float32) for _ in range(2)] for _ in range(2)]
    grad_v = [[], []]
    for qi in range(blocks):
        first = qi * LANES
        width = (qi + 1) * LANES
        rows = slice(first, first + LANES)
        maps = [weights_ref[k, rows, :width] for k in range(2)]
        grad_mixed = []
        for head in range(2):
            cols = slice(head * LANES, (head + 1) * LANES)
            values = proj_ref[:width, (4 + head) * LANES : (5 + head) * LANES]
            gm = lax.dot_general(
                grad_att[rows, cols], values, (((1,), (1,)), ((), ())), preferred_element_type=jnp.float32
            )
            grad_mixed.append(gm)
        for head in range(2):
            for k in range(2):
                part = jnp.sum(grad_mixed[head] * maps[k], axis=0, keepdims=True)
                for b in range(qi + 1):
                    sums[head][k] = sums[head][k] + part[:, b * LANES : (b + 1) * LANES]
        for k in range(2):
            grad_w = mix_ref[0, k] * grad_mixed[0] + mix_ref[1, k] * grad_mixed[1]
            inner = jnp.sum(grad_w * maps[k], axis=1, keepdims=True)
            conv_grad[k, rows, :width] = maps[k] * (grad_w - inner)
    for head in range(2):
        for k in range(2):
            small_ref[2 + 2 * head + k : 3 + 2 * head + k, :] = sums[head][k]
        cols = slice(head * LANES, (head + 1) * LANES)
        for kb in range(blocks):
            first = kb * LANES
            mixed = (
                mix_ref[head, 0] * weights_ref[0, first:, first : first + LANES]
                + mix_ref[head, 1] * weights_ref[1, first:, first : first + LANES]
            ).astype(jnp.bfloat16)
            out_ref[first : first + LANES, (4 + head) * LANES : (5 + head) * LANES] = lax.dot_general(
                mixed, grad_att[first:, cols], (((0,), (0,)), ((), ())), preferred_element_type=jnp.float32
            )

    def one_head(head, carry):
        lane = pl.multiple_of(head * LANES, LANES)
        lane_k = pl.multiple_of((head + 2) * LANES, LANES)
        keys_pad[EDGE : EDGE + seq_len, :] = proj_ref[:, pl.ds(lane_k, LANES)]
        for qi in range(blocks):
            first = qi * LANES
            width = (qi + 2) * LANES
            scores = masked_scores(
                proj_ref[first : first + LANES, pl.ds(lane, LANES)],
                keys_pad[:width, :],
                since_ref[first : first + LANES, :],
                first,
            )
            s_low[TOP + first : TOP + first + LANES, :width] = scores.astype(jnp.bfloat16)
            reach = min(width, seq_len)
            for tap in range(taps_q):
                moved = conv_grad[head, first + tap : first + tap + LANES, :reach]
                if tap > 0:
                    limit = since_pad[first + tap : first + tap + LANES, :]
                    limit = jnp.concatenate([limit] * (reach // LANES), 1)
                    moved = jnp.where(limit >= tap, moved, 0.0)
                shifted[tap, TOP + first : TOP + first + LANES, LANES : LANES + reach] = moved.astype(jnp.bfloat16)
        for m in range(blocks + 1):
            first = max(m - 1, 0) * LANES
            left = jnp.concatenate(
                [shifted[tap, TOP + first :, m * LANES : (m + 2) * LANES] for tap in range(taps_q)], 1
            )
            grad = jnp.dot(left, taps_ref[head], preferred_element_type=jnp.float32)
            rows = first + lax.broadcasted_iota(jnp.int32, grad.shape, 0)
            back = rows + EDGE - m * LANES - lax.broadcasted_iota(jnp.int32, grad.shape, 1)
            keep = (back >= 0) & (back <= since_ref[first:, :])
            s_grad[first:, m * LANES : (m + 1) * LANES] = jnp.where(keep, grad, 0.0).astype(jnp.bfloat16)
        total = jnp.zeros((2 * LANES, taps_q * LANES), jnp.float32)
        for m in range(blocks):
            first = m * LANES
            right = jnp.concatenate(
                [shifted[tap, first:, (m + 1) * LANES : (m + 2) * LANES] for tap in range(taps_q)], 1
            )
            total = total + lax.dot_general(
                s_low[first:, first : first + 2 * LANES], right, (((0,), (0,)), ((), ())),
                preferred_element_type=jnp.float32,
            )
        ridge = lax.broadcasted_iota(jnp.int32, (2 * LANES, LANES), 1) - lax.broadcasted_iota(
            jnp.int32, (2 * LANES, LANES), 0
        )
        for tap_k in range(taps_k):
            on = ridge == tap_k - EDGE - half
            for tap in range(taps_q):
                line = jnp.where(on, total[:, tap * LANES : (tap + 1) * LANES], 0.0)
                tap_ref[head, tap * taps_k + tap_k : tap * taps_k + tap_k + 1, :] = jnp.sum(line, axis=0, keepdims=True)
        for qi in range(blocks):
            first = qi * LANES
            width = (qi + 2) * LANES
            grad_q = jnp.dot(
                s_grad[first : first + LANES, :width], keys_pad[:width, :], preferred_element_type=jnp.float32
            )
            out_ref[first : first + LANES, pl.ds(lane, LANES)] = grad_q * scaling
        for kb in range(blocks):
            first = kb * LANES
            grad_k = lax.dot_general(
                s_grad[first:, first + EDGE : first + EDGE + LANES],
                proj_ref[first:, pl.ds(lane, LANES)],
                (((0,), (0,)), ((), ())),
                preferred_element_type=jnp.float32,
            )
            out_ref[first : first + LANES, pl.ds(lane_k, LANES)] = grad_k * scaling
        return carry

    lax.fori_loop(0, 2, one_head, 0)
    for at, first in ((own_at, 0), (other_at, half_len)):
        pieces = [out_ref[pl.ds(at, half_len), head * LANES : (head + 1) * LANES] for head in range(6)]
        joined = join_heads(pieces, head_size).astype(jnp.bfloat16)
        joined_grad_ref[first : first + half_len, :] = joined
        grad_in = lax.dot_general(
            joined, joined_ref[...], (((1,), (1,)), ((), ())), preferred_element_type=jnp.float32
        )
        if first:
            theirs_ref[...] = grad_in.astype(jnp.bfloat16)
        else:
            mine_ref[...] = grad_in.astype(jnp.bfloat16)


def attend_row_back(
    row, core, own, other, out_weight, joined, saved, since, mix, taps_backward, gain_pad, taps_q, taps_k, head_size
):
    projected, att, weights = saved
    seq_len = projected.shape[1]
    width = own.shape[1]
    full = seq_len + 2 * EDGE
    vmem = pl.BlockSpec(memory_space=pltpu.VMEM)
    smem = pl.BlockSpec(memory_space=pltpu.SMEM)
    anywhere = pl.BlockSpec(memory_space=pl.ANY)
    return pl.pallas_call(
        functools.partial(backward_kernel, taps_q, taps_k, head_size, head_size ** (-0.5), row),
        out_shape=(
            jax.ShapeDtypeStruct((seq_len, joined.shape[1]), jnp.bfloat16),
            jax.ShapeDtypeStruct((seq_len // 2, width), jnp.bfloat16),
            jax.ShapeDtypeStruct((seq_len // 2, width), jnp.bfloat16),
            jax.ShapeDtypeStruct((8, LANES), jnp.float32),
            jax.ShapeDtypeStruct((2, taps_q * taps_k, LANES), jnp.float32),
        ),
        in_specs=[smem, smem] + [vmem] * 6 + [anywhere] * 4,
        out_specs=(vmem,) * 5,
        scratch_shapes=[
            pltpu.VMEM((full, LANES), jnp.bfloat16),
            pltpu.VMEM((seq_len, 2 * LANES), jnp.bfloat16),
            pltpu.VMEM((2, seq_len + 8, seq_len), jnp.float32),
            pltpu.VMEM((taps_q, TOP + seq_len, seq_len + 2 * LANES), jnp.bfloat16),
            pltpu.VMEM((TOP + seq_len, full), jnp.bfloat16),
            pltpu.VMEM((seq_len, full), jnp.bfloat16),
            pltpu.VMEM((seq_len + 8, LANES), jnp.int32),
            pltpu.VMEM((seq_len, 2 * LANES), jnp.float32),
            pltpu.VMEM((seq_len, 6 * LANES), jnp.float32),
            pltpu.VMEM(projected.shape[1:], jnp.bfloat16),
            pltpu.VMEM(since.shape[1:], jnp.int32),
            pltpu.VMEM(att.shape[1:], jnp.float32),
            pltpu.VMEM(weights.shape[1:], jnp.float32),
            pltpu.SemaphoreType.DMA((4,)),
        ],
        compiler_params=pltpu.CompilerParams(vmem_limit_bytes=48 * 1024 * 1024),
        cost_estimate=cost(14),
        name="attend_row_back",
    )(core, mix, own, other, out_weight, joined, taps_backward, gain_pad, projected, since, att, weights)


def split_kernel(wide, feed_ref, gate_ref, down_ref):
    cols = down_ref.shape[0]
    chunk = cols // wide
    blocks = down_ref.shape[1] // cols
    gate_ref[...] = feed_ref[:, : 2 * cols]
    for z in range(wide):
        for b in range(blocks):
            first = (z * blocks + b) * chunk
            down_ref[z * chunk : (z + 1) * chunk, b * cols : (b + 1) * cols] = feed_ref[first : first + chunk, 2 * cols :]


def split_feed(feed, wide):
    vmem = pl.BlockSpec(memory_space=pltpu.VMEM)
    rows, cols = feed.shape[0], feed.shape[1] // 3
    return pl.pallas_call(
        functools.partial(split_kernel, wide),
        out_shape=(
            jax.ShapeDtypeStruct((rows, 2 * cols), jnp.bfloat16), jax.ShapeDtypeStruct((cols, rows), jnp.bfloat16),
        ),
        in_specs=[vmem],
        out_specs=(vmem,) * 2,
        compiler_params=pltpu.CompilerParams(vmem_limit_bytes=24 * 1024 * 1024),
        cost_estimate=LIGHT,
        name="split_feed",
    )(feed)


def feed_kernel(own_ref, other_ref, cot_own_ref, cot_other_ref, gate_ref, down_ref,
                hidden_ref, grads_ref, ffn_mine_ref, ffn_theirs_ref, back_mine_ref, back_theirs_ref):
    half_len = own_ref.shape[0]
    cols = down_ref.shape[0]
    for first, ref, cot_ref in ((0, own_ref, cot_own_ref), (half_len, other_ref, cot_other_ref)):
        rows = slice(first, first + half_len)
        both = jnp.dot(ref[...], gate_ref[...], preferred_element_type=jnp.float32)
        gating, upward = both[:, :cols], both[:, cols:]
        grad = lax.dot_general(
            cot_ref[...], down_ref[...], (((1,), (1,)), ((), ())), preferred_element_type=jnp.float32
        )
        sig = 1.0 / (1.0 + jnp.exp(-gating))
        silu = gating * sig
        hidden = (silu * upward).astype(jnp.bfloat16)
        hidden_ref[rows, :] = hidden
        grads_ref[rows, :cols] = (grad * upward * (sig * (1.0 + gating * (1.0 - sig)))).astype(jnp.bfloat16)
        grads_ref[rows, cols:] = (grad * silu).astype(jnp.bfloat16)
        back = lax.dot_general(
            grads_ref[rows, :], gate_ref[...], (((1,), (1,)), ((), ())), preferred_element_type=jnp.float32
        )
        ffn = jnp.dot(hidden, down_ref[...], preferred_element_type=jnp.float32)
        if first:
            back_theirs_ref[...] = back.astype(jnp.bfloat16)
            ffn_theirs_ref[...] = ffn.astype(jnp.bfloat16)
        else:
            back_mine_ref[...] = back.astype(jnp.bfloat16)
            ffn_mine_ref[...] = ffn.astype(jnp.bfloat16)


def feed_row(own, other, cot_own, cot_other, gate, down):
    half_len, width = own.shape
    cols = down.shape[0]
    vmem = pl.BlockSpec(memory_space=pltpu.VMEM)
    return pl.pallas_call(
        feed_kernel,
        out_shape=(
            jax.ShapeDtypeStruct((2 * half_len, cols), jnp.bfloat16),
            jax.ShapeDtypeStruct((2 * half_len, 2 * cols), jnp.bfloat16),
            jax.ShapeDtypeStruct((half_len, width), jnp.bfloat16),
            jax.ShapeDtypeStruct((half_len, width), jnp.bfloat16),
            jax.ShapeDtypeStruct((half_len, width), jnp.bfloat16),
            jax.ShapeDtypeStruct((half_len, width), jnp.bfloat16),
        ),
        in_specs=[vmem] * 6,
        out_specs=(vmem,) * 6,
        compiler_params=pltpu.CompilerParams(vmem_limit_bytes=48 * 1024 * 1024),
        cost_estimate=cost(8),
        name="feed_row",
    )(own, other, cot_own, cot_other, gate, down)


def feed_grad_kernel(counts, *refs):
    lefts, grads, hiddens, cots = (
        jnp.concatenate([ref[...] for ref in refs[sum(counts[:i]) : sum(counts[: i + 1])]], 0) for i in range(4)
    )
    out_ref = refs[-1]
    chunk = hiddens.shape[1]
    cols = out_ref.shape[1] - grads.shape[1]
    out_ref[:, : grads.shape[1]] = lax.dot_general(
        lefts, grads, (((0,), (0,)), ((), ())), preferred_element_type=jnp.float32
    ).astype(jnp.bfloat16)
    down = lax.dot_general(hiddens, cots, (((0,), (0,)), ((), ())), preferred_element_type=jnp.float32)
    for b in range(down.shape[1] // cols):
        out_ref[b * chunk : (b + 1) * chunk, grads.shape[1] :] = down[:, b * cols : (b + 1) * cols].astype(jnp.bfloat16)


def feed_grad(lefts, grads, hiddens, cots, wide):
    width = lefts[0].shape[1]
    cols = hiddens[0].shape[1]
    block, chunk = width // wide, cols // wide
    if block % LANES or chunk % LANES:
        gate = lax.dot_general(
            jnp.concatenate(lefts, 0), jnp.concatenate(grads, 0), (((0,), (0,)), ((), ())),
            preferred_element_type=jnp.float32,
        )
        down = lax.dot_general(
            jnp.concatenate(hiddens, 0), jnp.concatenate(cots, 0), (((0,), (0,)), ((), ())),
            preferred_element_type=jnp.float32,
        )
        down = jnp.swapaxes(down.reshape(wide, chunk, width // cols, cols), 1, 2).reshape(width, cols)
        return jnp.concatenate([gate, down], 1).astype(jnp.bfloat16)
    count = sum(a.shape[0] for a in lefts)
    cols_out = grads[0].shape[1] + cols
    return pl.pallas_call(
        functools.partial(feed_grad_kernel, (len(lefts), len(grads), len(hiddens), len(cots))),
        out_shape=jax.ShapeDtypeStruct((width, cols_out), jnp.bfloat16),
        grid=(wide,),
        in_specs=[pl.BlockSpec((a.shape[0], block), lambda s: (0, s)) for a in lefts]
        + [pl.BlockSpec(a.shape, lambda s: (0, 0)) for a in grads]
        + [pl.BlockSpec((a.shape[0], chunk), lambda s: (0, s)) for a in hiddens]
        + [pl.BlockSpec(a.shape, lambda s: (0, 0)) for a in cots],
        out_specs=pl.BlockSpec((block, cols_out), lambda s: (s, 0)),
        compiler_params=pltpu.CompilerParams(vmem_limit_bytes=ROOM),
        cost_estimate=cost(17),
        name="feed_grad",
    )(*lefts, *grads, *hiddens, *cots)


def weight_kernel(lefts, *refs):
    left = jnp.concatenate([ref[...] for ref in refs[:lefts]], 0)
    right = jnp.concatenate([ref[...] for ref in refs[lefts:-1]], 0)
    refs[-1][...] = lax.dot_general(
        left, right, (((0,), (0,)), ((), ())), preferred_element_type=jnp.float32
    ).astype(jnp.bfloat16)


def small_weight_grad(lefts, rights, name):
    vmem = pl.BlockSpec(memory_space=pltpu.VMEM)
    return pl.pallas_call(
        functools.partial(weight_kernel, len(lefts)),
        out_shape=jax.ShapeDtypeStruct((lefts[0].shape[1], rights[0].shape[1]), jnp.bfloat16),
        in_specs=[vmem] * (len(lefts) + len(rights)),
        out_specs=vmem,
        compiler_params=pltpu.CompilerParams(vmem_limit_bytes=32 * 1024 * 1024),
        cost_estimate=cost(3),
        name=name,
    )(*lefts, *rights)


def weight_grad(lefts, rights, block, name):
    rows_out, cols_out = lefts[0].shape[1], rights[0].shape[1]
    count = sum(a.shape[0] for a in lefts)
    return pl.pallas_call(
        functools.partial(weight_kernel, len(lefts)),
        out_shape=jax.ShapeDtypeStruct((rows_out, cols_out), jnp.bfloat16),
        grid=(rows_out // block,),
        in_specs=[pl.BlockSpec((a.shape[0], block), lambda s: (0, s)) for a in lefts]
        + [pl.BlockSpec(a.shape, lambda s: (0, 0)) for a in rights],
        out_specs=pl.BlockSpec((block, cols_out), lambda s: (s, 0)),
        compiler_params=pltpu.CompilerParams(vmem_limit_bytes=ROOM),
        cost_estimate=cost(8),
        name=name,
    )(*lefts, *rights)


def halves_kernel(mine_ref, came_ref, low_ref, high_ref):
    cut = low_ref.shape[0]
    low_ref[...] = (mine_ref[:cut, :].astype(jnp.float32) + came_ref[:cut, :].astype(jnp.float32)).astype(jnp.bfloat16)
    high_ref[...] = (mine_ref[cut:, :].astype(jnp.float32) + came_ref[cut:, :].astype(jnp.float32)).astype(jnp.bfloat16)


def sum_halves(mine, came):
    half = jax.ShapeDtypeStruct((mine.shape[0] // 2, mine.shape[1]), jnp.bfloat16)
    vmem = pl.BlockSpec(memory_space=pltpu.VMEM)
    return pl.pallas_call(
        halves_kernel, out_shape=(half, half), in_specs=[vmem] * 2, out_specs=(vmem,) * 2,
        compiler_params=pltpu.CompilerParams(vmem_limit_bytes=4 * 1024 * 1024), cost_estimate=LIGHT, name="sum_halves",
    )(mine, came)


def sum_kernel(second, mine_ref, came_ref, extra_ref, out_ref):
    cut = extra_ref.shape[0]
    rows, rest = (slice(cut, 2 * cut), slice(0, cut)) if second else (slice(0, cut), slice(cut, 2 * cut))
    total = mine_ref[rows, :].astype(jnp.float32) + came_ref[rows, :].astype(jnp.float32) + extra_ref[...].astype(jnp.float32)
    out_ref[rows, :] = total.astype(jnp.bfloat16)
    out_ref[rest, :] = (mine_ref[rest, :].astype(jnp.float32) + came_ref[rest, :].astype(jnp.float32)).astype(jnp.bfloat16)


def low_sum(mine, came, extra, second):
    vmem = pl.BlockSpec(memory_space=pltpu.VMEM)
    return pl.pallas_call(
        functools.partial(sum_kernel, second), out_shape=jax.ShapeDtypeStruct(mine.shape, jnp.bfloat16),
        in_specs=[vmem] * 3, out_specs=vmem,
        compiler_params=pltpu.CompilerParams(vmem_limit_bytes=4 * 1024 * 1024), cost_estimate=LIGHT, name="low_sum",
    )(mine, came, extra)


def pair_kernel(mine_ref, came_ref, out_ref):
    out_ref[...] = (mine_ref[...].astype(jnp.float32) + came_ref[...].astype(jnp.float32)).astype(jnp.bfloat16)


def pair_sum(mine, came):
    vmem = pl.BlockSpec(memory_space=pltpu.VMEM)
    return pl.pallas_call(
        pair_kernel, out_shape=jax.ShapeDtypeStruct(mine.shape, jnp.bfloat16), in_specs=[vmem] * 2, out_specs=vmem,
        compiler_params=pltpu.CompilerParams(vmem_limit_bytes=4 * 1024 * 1024), cost_estimate=LIGHT, name="pair_sum",
    )(mine, came)


def place_out_kernel(place_ref, *refs):
    out_ref = refs[-1]
    out_ref[...] = jnp.zeros_like(out_ref)
    for step, ref in enumerate(refs[:-1]):
        chunk = jnp.bitwise_xor(place_ref[0], step)
        rows = ref.shape[0]
        at = pl.multiple_of(lax.div(chunk, 2) * LANES + lax.rem(chunk, 2) * rows, 16)
        out_ref[pl.ds(at, rows), :] = ref[...]


def place_out(place, pieces):
    vmem = pl.BlockSpec(memory_space=pltpu.VMEM)
    return pl.pallas_call(
        place_out_kernel,
        out_shape=jax.ShapeDtypeStruct((2 * LANES, pieces[0].shape[1]), jnp.bfloat16),
        in_specs=[pl.BlockSpec(memory_space=pltpu.SMEM)] + [vmem] * len(pieces),
        out_specs=vmem,
        compiler_params=pltpu.CompilerParams(vmem_limit_bytes=16 * 1024 * 1024),
        cost_estimate=LIGHT,
        name="place_out",
    )(place, *pieces)


def branch_kernel(grouped_ref, out_ref, *refs):
    weight = out_ref[...]
    for row in range(grouped_ref.shape[0]):
        mine_ref, theirs_ref = refs[2 * row : 2 * row + 2]
        half_len = mine_ref.shape[0]
        mine_ref[...] = jnp.dot(grouped_ref[row, :half_len, :], weight, preferred_element_type=jnp.float32).astype(
            jnp.bfloat16
        )
        theirs_ref[...] = jnp.dot(grouped_ref[row, half_len:, :], weight, preferred_element_type=jnp.float32).astype(
            jnp.bfloat16
        )


def branch_rows_of(grouped, out_own):
    vmem = pl.BlockSpec(memory_space=pltpu.VMEM)
    rows, half_len, width = grouped.shape[0], grouped.shape[1] // 2, out_own.shape[1]
    flat = pl.pallas_call(
        branch_kernel,
        out_shape=(
            jax.ShapeDtypeStruct((half_len, width), jnp.bfloat16),
        ) * (2 * rows),
        in_specs=[vmem] * 2,
        out_specs=(vmem,) * (2 * rows),
        compiler_params=pltpu.CompilerParams(vmem_limit_bytes=32 * 1024 * 1024),
        cost_estimate=LIGHT,
        name="branch",
    )(grouped, out_own)
    return flat[0::2], flat[1::2]


def pick_kernel(place_ref, *refs):
    ins, outs = refs[:4], refs[4:]
    for step, out in enumerate(outs):
        behind = jnp.bitwise_and(place_ref[2] - jnp.bitwise_xor(place_ref[0], step), 3)
        for k, ref in enumerate(ins):

            @pl.when(behind == k)
            def _():
                out[...] = ref[...]


def pick_out(place, pieces):
    vmem = pl.BlockSpec(memory_space=pltpu.VMEM)
    return pl.pallas_call(
        pick_kernel,
        out_shape=(jax.ShapeDtypeStruct(pieces[0].shape, pieces[0].dtype),) * 4,
        in_specs=[pl.BlockSpec(memory_space=pltpu.SMEM)] + [vmem] * 4,
        out_specs=(vmem,) * 4,
        compiler_params=pltpu.CompilerParams(vmem_limit_bytes=16 * 1024 * 1024),
        cost_estimate=LIGHT,
        name="pick_out",
    )(place, *pieces)


def place_quarters_kernel(place_ref, own_ref, other_ref, out_ref):
    chips, rows = own_ref.shape[:2]
    for k in range(chips):
        for e, ref in enumerate((own_ref, other_ref)):
            core = jnp.bitwise_xor(place_ref[1], e)
            at = pl.multiple_of((core * chips + jnp.bitwise_xor(place_ref[0], k)) * rows, rows)
            out_ref[pl.ds(at, rows), :] = ref[k].astype(jnp.float32)


def place_quarters(place, own, other):
    vmem = pl.BlockSpec(memory_space=pltpu.VMEM)
    chips, rows, cols = own.shape
    return pl.pallas_call(
        place_quarters_kernel,
        out_shape=jax.ShapeDtypeStruct((2 * chips * rows, cols), jnp.float32),
        in_specs=[pl.BlockSpec(memory_space=pltpu.SMEM)] + [vmem] * 2,
        out_specs=vmem,
        compiler_params=pltpu.CompilerParams(vmem_limit_bytes=16 * 1024 * 1024),
        cost_estimate=LIGHT,
        name="place_quarters",
    )(place, own, other)


from jax.sharding import PartitionSpec as P

PLANE = ("narrow", "seq")
SWAP = [(0, 1), (1, 0)]


def seq_swap(array):
    return lax.ppermute(array, "seq", SWAP)


def x_swap(array):
    return lax.ppermute(array, "narrow", [(0, 1), (1, 0), (2, 3), (3, 2)])


def y_swap(array):
    return lax.ppermute(array, "narrow", [(0, 2), (2, 0), (1, 3), (3, 1)])


def diagonal_swap(array):
    return lax.ppermute(array, "narrow", [(i, i ^ 3) for i in range(4)])


def gather_plane(own):
    half = own.shape[0] // 2
    from_x = x_swap(own)
    from_y = y_swap(own)
    corner = jnp.concatenate([y_swap(from_x[:half]), x_swap(from_y[half:])], 0)
    return [(a, seq_swap(a)) for a in (own, from_x, from_y, corner)]


def after(array, *others):
    return lax.optimization_barrier((array, *others))[0] if others else array


class Steps:
    def __init__(self):
        self.ended = ()

    def hold(self, array):
        return after(array, *self.ended)

    def end(self, *arrays):
        self.ended = arrays


def half_rows(array, second):
    cut = array.shape[0] // 2
    return array[cut:] if second else array[:cut]


def whole_sum(mine, came, from_x, from_y):
    return mine.astype(jnp.float32) + came.astype(jnp.float32) + from_x.astype(jnp.float32) + from_y.astype(jnp.float32)


def wide_shift(array, by):
    count = lax.axis_size("wide")
    return lax.ppermute(array, "wide", [(i, (i + by) % count) for i in range(count)])


def wide_block(blocks, step):
    count = lax.axis_size("wide")
    at = (lax.axis_index("wide") - step) % count
    return lax.dynamic_index_in_dim(blocks, at, 0, keepdims=False)


def wide_stack(pieces):
    whole = jnp.zeros((len(pieces),) + pieces[0].shape, pieces[0].dtype)
    for step, piece in enumerate(pieces):
        whole = lax.dynamic_update_index_in_dim(whole, piece, (lax.axis_index("wide") - step) % len(pieces), 0)
    return whole


def gather_wide(piece):
    return lax.all_gather(piece, "wide", axis=0, tiled=True)


def scatter_wide(whole):
    return lax.psum_scatter(whole, "wide", scatter_dimension=0, tiled=True)


def exchange_plane(blocks):
    line = lax.axis_index("narrow")

    def block(k):
        return lax.dynamic_index_in_dim(blocks, line ^ k, 0, keepdims=False)

    return [block(0), x_swap(block(1)), y_swap(block(2)), diagonal_swap(block(3))]


def in_place(pieces):
    line = lax.axis_index("narrow")
    whole = jnp.zeros((4,) + pieces[0].shape, pieces[0].dtype)
    for k in range(4):
        whole = lax.dynamic_update_index_in_dim(whole, pieces[k], line ^ k, 0)
    return whole


def pad_heads(array, head_size):
    heads = array.shape[1] // head_size
    split = array.reshape(array.shape[0], heads, head_size)
    return jnp.pad(split, ((0, 0), (0, 0), (0, LANES - head_size))).reshape(array.shape[0], heads * LANES)


def times(left, right):
    return jnp.dot(left, right, preferred_element_type=jnp.float32)


def norm_scale(values):
    return lax.rsqrt(jnp.mean(values * values, axis=-1, keepdims=True) + 1e-06)


def norm_back(values, scale, gain, grad):
    lift = grad * gain
    along = jnp.mean(lift * values, axis=-1, keepdims=True)
    return scale * lift - values * (scale * scale * scale * along), jnp.sum(grad * values * scale, axis=0)


def on_device(
    inputs,
    doc_start,
    norm_gain,
    qkv_weight,
    logit_kernel,
    head_mix,
    group_gain,
    out_weight,
    feed_gain,
    gate_up,
    down_weight,
    cotangent,
):
    tokens_dev, width = inputs.shape
    head_count, taps_q, taps_k = logit_kernel.shape
    head_size = width // head_count
    group_cols = 2 * head_size
    cores = lax.axis_size(PLANE)
    wide = lax.axis_size("wide")
    line = lax.axis_index("narrow")
    part = lax.axis_index(PLANE)
    chunk = gate_up.shape[1] // (2 * wide * cores)
    scaling = head_size ** (-0.5)

    core = lax.axis_index("seq").astype(jnp.int32).reshape(1)
    place = jnp.stack([line, lax.axis_index("seq"), lax.axis_index("wide")]).astype(jnp.int32)

    joined_piece = jnp.concatenate(
        [
            lax.dynamic_slice_in_dim(qkv_weight, s * width + part * group_cols, group_cols, 1)
            for s in range(3)
        ]
        + [jnp.zeros((qkv_weight.shape[0], -3 * group_cols % LANES), qkv_weight.dtype)],
        1,
    )
    joined = gather_wide(joined_piece)
    inputs, doc_start, out_weight = lax.optimization_barrier((inputs, doc_start, out_weight, joined_piece))[:3]

    flow = Steps()
    hold = flow.hold
    feed_cols = wide * chunk
    first_pos = lax.axis_index(("narrow", "wide", "seq")) * tokens_dev

    out_rows = group_cols // 4
    ring = wide == 4

    inputs_f = inputs.astype(jnp.float32)
    scale_in = norm_scale(inputs_f)
    normed = (inputs_f * scale_in * norm_gain).astype(jnp.bfloat16)
    since = first_pos + jnp.arange(tokens_dev, dtype=jnp.int32) - doc_start
    since_same = jnp.stack([since, x_swap(since), y_swap(since), diagonal_swap(since)])
    out_pieces = [lax.dynamic_slice_in_dim(out_weight, (lax.axis_index("seq") * 4 + line) * out_rows, out_rows, 0)]

    def out_step():
        if ring:
            out_pieces.append(wide_shift(hold(out_pieces[-1]), 1))

    out_step()
    flow.end(normed, out_pieces[-1])

    normed_x, normed_y, normed_o = x_swap(hold(normed)), y_swap(hold(normed)), seq_swap(hold(normed))
    out_step()
    kernels = lax.dynamic_slice_in_dim(logit_kernel, 2 * part, 2, 0)
    mix = lax.dynamic_slice_in_dim(head_mix, 2 * part, 2, 0)
    taps_forward, taps_backward = tap_bands(hold(kernels), scaling)
    gain_pad = pad_heads(lax.dynamic_slice_in_dim(group_gain, part * group_cols, group_cols, 0)[None], head_size)
    gate_piece = jnp.concatenate(
        [
            lax.dynamic_slice_in_dim(hold(gate_up), (s * cores + part) * chunk, chunk, 1)
            for s in range(2 * wide)
        ],
        1,
    )
    down_piece = lax.dynamic_slice_in_dim(hold(down_weight), part * chunk, chunk, 0)
    down_piece = jnp.concatenate(
        [down_piece[:, at : at + feed_cols] for at in range(0, width, feed_cols)], 0
    )
    feed_piece = jnp.concatenate([gate_piece, down_piece], 1)
    flow.end(normed_x, normed_y, normed_o, taps_forward, since_same, feed_piece, out_pieces[-1])

    low, high = half_rows(normed_x, False), half_rows(normed_y, True)
    flow.end(low, high, *flow.ended)
    corner_low, corner_high = y_swap(hold(low)), x_swap(hold(high))
    cot_x, cot_y = x_swap(hold(cotangent)), y_swap(hold(cotangent))
    out_step()
    since_other = seq_swap(hold(since_same))
    flow.end(corner_low, corner_high, since_other, out_pieces[-1])

    normed_c = jnp.concatenate([corner_low, corner_high], 0)
    normed_xo, normed_yo, normed_co = seq_swap(normed_x), seq_swap(normed_y), seq_swap(hold(normed_c))
    first = lax.axis_index("seq") == 0
    since_all = hold(
        jnp.concatenate([jnp.where(first, since_same, since_other), jnp.where(first, since_other, since_same)], 1)
    )
    since_rows = jnp.broadcast_to(since_all[:, :, None], since_all.shape + (LANES,))
    normed_rows = [(normed, normed_o), (normed_x, normed_xo), (normed_y, normed_yo), (normed_c, normed_co)]
    if ring:
        out_picked = pick_out(hold(place), out_pieces)
        flow.end(normed_co, normed_xo, normed_yo, joined, since_rows, *out_picked)
    else:
        flow.end(normed_co, normed_xo, normed_yo, joined, since_rows)

    feed_own = gather_wide(hold(feed_piece))
    if ring:
        out_picked = [hold(a) for a in out_picked]
        out_pieces = [
            out_picked[0], x_swap(out_picked[1]), y_swap(out_picked[2]), diagonal_swap(out_picked[3])
        ]
    projected, attended, grouped, weights = attend_rows(
        hold(core), [a for k in normed_rows for a in k], since_rows, mix, joined, taps_forward, gain_pad, taps_q,
        head_size,
    )
    flow.end(grouped, cot_x, cot_y, *out_pieces)
    if ring:
        out_own = place_out(hold(place), out_pieces)
    else:
        out_own = lax.dynamic_slice_in_dim(gather_wide(hold(out_weight)), part * group_cols, group_cols, 0)
        out_own = jnp.pad(
            out_own.reshape(2, head_size, width), ((0, 0), (0, LANES - head_size), (0, 0))
        ).reshape(2 * LANES, width)
    branch_mine, branch_theirs = branch_rows_of(grouped, out_own)
    flow.end(*branch_mine, *branch_theirs)
    came_3, came_1, came_2 = (seq_swap(hold(branch_theirs[k])) for k in (3, 1, 2))
    flow.end(came_3, came_1, came_2)
    low, high = sum_halves(branch_mine[3], hold(came_3))
    flow.end(low, high)
    to_y, to_x = x_swap(hold(low)), y_swap(hold(high))
    came_0, cot_o = seq_swap(hold(branch_theirs[0])), seq_swap(hold(cotangent))
    flow.end(came_0, to_x, to_y, cot_o)
    low_x = low_sum(branch_mine[1], came_1, hold(to_x), True)
    low_y = low_sum(branch_mine[2], came_2, hold(to_y), False)
    flow.end(low_x, low_y)
    cot_xo, cot_yo = seq_swap(hold(cot_x)), seq_swap(hold(cot_y))
    branch_x, branch_y = x_swap(hold(low_x)), y_swap(hold(low_y))
    cot_halves = half_rows(hold(cot_x), False), half_rows(hold(cot_y), True)
    flow.end(branch_x, branch_y, cot_xo, cot_yo, feed_own, *cot_halves)
    residual = inputs_f + whole_sum(branch_mine[0], hold(came_0), branch_x, branch_y)
    scale_mid = norm_scale(residual)
    normed_ffn = (residual * scale_mid * feed_gain).astype(jnp.bfloat16)
    flow.end(normed_ffn)

    ffn_x, ffn_y, ffn_o = x_swap(hold(normed_ffn)), y_swap(hold(normed_ffn)), seq_swap(hold(normed_ffn))
    flow.end(ffn_o)
    hidden_rows, gate_grads, feed_out = [None] * 4, [None] * 4, [None] * 4
    ffn_rows = [(normed_ffn, ffn_o), None, None, None]
    cotangent_rows = [(cotangent, cot_o), (cot_x, cot_xo), (cot_y, cot_yo), None]

    gate_own, down_own = split_feed(hold(feed_own), wide)

    def feed(k):
        hidden_rows[k], gate_grads[k], *feed_out[k] = feed_row(
            hold(ffn_rows[k][0]), ffn_rows[k][1], *cotangent_rows[k], gate_own, down_own
        )

    feed(0)
    flow.end(hidden_rows[0], ffn_x, ffn_y)
    ffn_xo, ffn_yo = seq_swap(hold(ffn_x)), seq_swap(hold(ffn_y))
    ffn_rows[1], ffn_rows[2] = (ffn_x, ffn_xo), (ffn_y, ffn_yo)
    flow.end(ffn_xo, ffn_yo)
    cot_low, cot_high = y_swap(hold(cot_halves[0])), x_swap(hold(cot_halves[1]))
    low, high = half_rows(hold(ffn_x), False), half_rows(hold(ffn_y), True)
    back_came = [None] * 4
    feed(1)
    flow.end(hidden_rows[1], cot_low, cot_high, low, high)
    cot_c = jnp.concatenate([cot_low, cot_high], 0)
    flow.end(low, high, cot_c)
    corner_low, corner_high = y_swap(hold(low)), x_swap(hold(high))
    cot_co = seq_swap(hold(cot_c))
    back_came[1] = seq_swap(hold(feed_out[1][3]))
    feed(2)
    flow.end(hidden_rows[2], corner_low, corner_high, cot_co, back_came[1])
    back_came[2] = seq_swap(hold(feed_out[2][3]))
    ffn_c = jnp.concatenate([corner_low, corner_high], 0)
    ffn_co = seq_swap(ffn_c)
    low_x = pair_sum(feed_out[1][2], hold(back_came[1]))
    low_y = pair_sum(feed_out[2][2], back_came[2])
    ffn_rows[3], cotangent_rows[3] = (ffn_c, ffn_co), (cot_c, cot_co)
    flow.end(ffn_co, low_x, low_y)
    back_x, back_y = x_swap(hold(low_x)), y_swap(hold(low_y))
    feed(3)
    flow.end(hidden_rows[3], back_x, back_y)
    back_came[3], back_came[0] = seq_swap(hold(feed_out[3][3])), seq_swap(hold(feed_out[0][3]))
    flow.end(back_came[3], back_came[0])
    low = pair_sum(feed_out[3][2], hold(back_came[3]))
    flow.end(low)
    back_d = diagonal_swap(hold(low))
    feed_grad_own = feed_grad(
        [hold(a) for k in ffn_rows for a in k], gate_grads, hidden_rows, [a for k in cotangent_rows for a in k], wide
    )
    flow.end(back_d, feed_grad_own)
    shard_feed = scatter_wide(hold(feed_grad_own))
    feed_came = [seq_swap(hold(feed_out[k][1])) for k in range(4)]
    grad_ffn = whole_sum(feed_out[0][2], back_came[0], back_x, back_y) + hold(back_d).astype(jnp.float32)
    norm_part, grad_feed = norm_back(residual, scale_mid, feed_gain, grad_ffn)
    grad_residual = norm_part + cotangent.astype(jnp.float32)
    grad_branch = grad_residual.astype(jnp.bfloat16)
    flow.end(grad_branch, *feed_came)

    gb_x, gb_y, gb_o = x_swap(hold(grad_branch)), y_swap(hold(grad_branch)), seq_swap(hold(grad_branch))
    low, high = sum_halves(feed_out[3][0], hold(feed_came[3]))
    flow.end(gb_o, low, high)
    branch_rows = [(grad_branch, gb_o), None, None, None]
    grad_joined, normed_mine, normed_theirs, smalls, tap_sums = ([None] * 4 for _ in range(5))

    def attend_back(k):
        grad_joined[k], normed_mine[k], normed_theirs[k], smalls[k], tap_sums[k] = attend_row_back(
            k, hold(core), *branch_rows[k], out_own, joined, (projected, attended, weights), since_rows, mix,
            taps_backward, gain_pad, taps_q, taps_k, head_size,
        )

    attend_back(0)
    flow.end(grad_joined[0], gb_x, gb_y)
    gb_xo, gb_yo = seq_swap(hold(gb_x)), seq_swap(hold(gb_y))
    branch_rows[1], branch_rows[2] = (gb_x, gb_xo), (gb_y, gb_yo)
    flow.end(gb_xo, gb_yo)
    corner_low, corner_high = y_swap(hold(half_rows(gb_x, False))), x_swap(hold(half_rows(gb_y, True)))
    to_y, to_x = x_swap(hold(low)), y_swap(hold(high))
    attend_back(1)
    flow.end(grad_joined[1], corner_low, corner_high, to_x, to_y)
    low_x = low_sum(feed_out[1][0], feed_came[1], hold(to_x), True)
    low_y = low_sum(feed_out[2][0], feed_came[2], hold(to_y), False)
    gb_c = jnp.concatenate([corner_low, corner_high], 0)
    flow.end(low_x, low_y, gb_c)
    gb_co = seq_swap(hold(gb_c))
    flow.end(low_x, low_y, gb_co)
    feed_main_x, feed_main_y = x_swap(hold(low_x)), y_swap(hold(low_y))
    branch_rows[3] = (gb_c, gb_co)
    normed_came = [None] * 4
    normed_came[1] = seq_swap(hold(normed_theirs[1]))
    attend_back(2)
    grad_out_own = small_weight_grad([grouped.reshape(-1, 2 * LANES)], [hold(a) for k in branch_rows for a in k], "out_grad")
    flow.end(grad_joined[2], normed_came[1], grad_out_own, feed_main_x, feed_main_y)
    normed_came[2] = seq_swap(hold(normed_theirs[2]))
    low_x = pair_sum(normed_mine[1], hold(normed_came[1]))
    grad_out_own = hold(grad_out_own).reshape(2, LANES, width)[:, :head_size].reshape(2 * head_size, width)
    flow.end(normed_came[2], low_x, grad_out_own)
    low_y = pair_sum(normed_mine[2], hold(normed_came[2]))
    flow.end(low_x, low_y)
    grad_x, grad_y = x_swap(hold(low_x)), y_swap(hold(low_y))
    out_terms = hold(grad_out_own)
    if ring:
        out_terms = in_place(exchange_plane(out_terms.reshape(4, out_rows, width)))
    attend_back(3)
    flow.end(grad_joined[3], grad_x, grad_y, out_terms)

    normed_came[3], normed_came[0] = seq_swap(hold(normed_theirs[3])), seq_swap(hold(normed_theirs[0]))
    flow.end(normed_came[3], normed_came[0])
    low = pair_sum(normed_mine[3], hold(normed_came[3]))
    flow.end(low)
    grad_d = diagonal_swap(hold(low))
    out_came = []
    if ring:
        out_came = [wide_shift(hold(wide_block(out_terms, -step)), step) for step in range(1, 4)]
    joined_grad_own = weight_grad(
        [hold(a) for k in normed_rows for a in k], grad_joined, 2 * LANES, "joined_grad"
    )
    flow.end(grad_d, joined_grad_own, *out_came)
    shard_joined = scatter_wide(hold(joined_grad_own))
    feed_x, feed_y, feed_o = x_swap(hold(shard_feed)), y_swap(hold(shard_feed)), seq_swap(hold(shard_feed))
    grad_normed = whole_sum(normed_mine[0], normed_came[0], grad_x, grad_y) + hold(grad_d).astype(jnp.float32)
    norm_part, grad_norm = norm_back(inputs_f, scale_in, norm_gain, grad_normed)
    grad_input = norm_part + grad_residual
    small = hold(smalls[0] + smalls[1] + smalls[2] + smalls[3])
    taps = jnp.sum(tap_sums[0] + tap_sums[1] + tap_sums[2] + tap_sums[3], axis=2) * scaling

    def placed(array, total):
        array = array.reshape(-1)
        return lax.dynamic_update_slice(jnp.zeros((total,), jnp.float32), array, (part * array.shape[0],))

    pieces = [
        grad_feed,
        placed(small[:2, :head_size], width),
        placed(hold(taps), head_count * taps_q * taps_k),
        placed(jnp.sum(small[2:6], axis=1), 2 * head_count),
    ]
    lengths = [a.shape[0] for a in pieces]
    fill = -(sum(lengths) + width) % (8 * LANES)
    packed = jnp.concatenate(pieces + [jnp.zeros((fill,), jnp.float32)]).reshape(-1, LANES)
    packed = jnp.concatenate([packed, grad_norm.reshape(-1, LANES)], 0)
    packed = packed + seq_swap(packed)
    if wide & (wide - 1):
        packed = lax.psum(packed, "wide")
    else:
        for hop in [1 << i for i in range(16) if 1 << i < wide]:
            packed = packed + lax.ppermute(packed, "wide", [(i, i ^ hop) for i in range(wide)])
    packed = packed + x_swap(packed)
    flow.end(packed, feed_x, feed_y, feed_o)
    shard_out = out_x = out_y = grad_out_own
    if ring:
        out_sum = wide_block(out_terms, 0).astype(jnp.float32) + sum(hold(a).astype(jnp.float32) for a in out_came)
        shard_out = out_sum.astype(jnp.bfloat16)
    packed = packed + y_swap(hold(packed))
    feed_low, feed_high = y_swap(hold(half_rows(feed_x, False))), x_swap(hold(half_rows(feed_y, True)))
    feed_xo, feed_yo = seq_swap(hold(feed_x)), seq_swap(hold(feed_y))
    block_out = (residual + whole_sum(feed_out[0][0], hold(feed_came[0]), feed_main_x, feed_main_y)).astype(jnp.bfloat16)
    flow.end(feed_low, feed_high, feed_xo, feed_yo, packed, shard_joined, block_out, shard_out)

    joined_x, joined_y, joined_o = x_swap(hold(shard_joined)), y_swap(hold(shard_joined)), seq_swap(hold(shard_joined))
    feed_c = jnp.concatenate([feed_low, feed_high], 0)
    feed_co = seq_swap(hold(feed_c))
    if ring:
        out_x, out_y = x_swap(hold(shard_out)), y_swap(hold(shard_out))
        grad_gate, grad_down = place_feed(
            place, [hold(shard_feed), feed_o, feed_x, feed_xo, feed_y, feed_yo, feed_c, feed_co], chunk
        )
    else:
        every = lax.all_gather(shard_feed, PLANE, axis=0)
        split = every[:, :, : 2 * feed_cols].reshape(cores, shard_feed.shape[0], 2 * wide, chunk)
        grad_gate = jnp.moveaxis(split, 0, 2).reshape(shard_feed.shape[0], -1).astype(jnp.float32)
        split = every[:, :, 2 * feed_cols :].reshape(cores, width // feed_cols, chunk, feed_cols)
        grad_down = jnp.swapaxes(split, 1, 2).reshape(cores * chunk, width).astype(jnp.float32)
        grad_out = scatter_wide(lax.all_gather(grad_out_own, PLANE, axis=0, tiled=True)).astype(jnp.float32)
    flow.end(joined_x, joined_y, joined_o, packed, grad_gate, out_x, out_y)
    joined_low, joined_high = y_swap(hold(half_rows(joined_x, False))), x_swap(hold(half_rows(joined_y, True)))
    if ring:
        out_c = y_swap(hold(out_x))
    joined_xo, joined_yo = seq_swap(hold(joined_x)), seq_swap(hold(joined_y))
    joined_rows = [(shard_joined, joined_o), (joined_x, joined_xo), (joined_y, joined_yo)]
    whole_columns = 2 * group_cols % LANES == 0
    if whole_columns:
        grad_qkv = place_columns(hold(place), [a for k in joined_rows for a in k], 3, group_cols, 4)
        flow.end(joined_low, joined_high, grad_qkv, *([out_c] if ring else []))
    else:
        flow.end(joined_low, joined_high)
    joined_c = jnp.concatenate([joined_low, joined_high], 0)
    joined_co = seq_swap(hold(joined_c))
    if ring:
        quarters = jnp.stack([shard_out, out_x, out_y, out_c])
        grad_out = place_quarters(place, quarters, seq_swap(hold(quarters)))
    if whole_columns:
        grad_qkv = add_columns(place, joined_c, joined_co, grad_qkv, 3, group_cols, 4, 3)
    else:
        every = lax.all_gather(shard_joined, PLANE, axis=0)[:, :, : 3 * group_cols]
        split = every.reshape(cores, shard_joined.shape[0], 3, group_cols)
        grad_qkv = jnp.moveaxis(split, 0, 2).reshape(shard_joined.shape[0], -1).astype(jnp.float32)
    packed = packed.reshape(-1)
    grad_norm = packed[-width:]
    parts = []
    for length in lengths:
        parts.append(packed[:length])
        packed = packed[length:]
    grad_feed, grad_group, grad_kernel, grad_mix = parts
    return (
        block_out,
        grad_input,
        grad_norm,
        grad_qkv,
        grad_kernel.reshape(head_count, taps_q, taps_k),
        grad_mix.reshape(head_count, 2),
        grad_group,
        grad_out,
        grad_feed,
        grad_gate,
        grad_down,
    )


def solution(mesh):
    tokens = P(("narrow", "wide", "seq"), None)
    rows = P("wide", None)
    return jax.shard_map(
        on_device,
        mesh=mesh,
        in_specs=(tokens, P(("narrow", "wide", "seq")), P(), rows, P(), P(), P(), rows, P(), rows, rows, tokens),
        out_specs=(tokens, tokens, P(), rows, P(), P(), P(), rows, P(), rows, rows),
        check_vma=False,
    )
```

```python
import functools
import jax
import jax.numpy as jnp
from jax import lax
from jax.experimental import pallas as pl
from jax.experimental.pallas import tpu as pltpu

LANES = 128
EDGE = 64
TOP = 16
ROOM = 60 * 1024 * 1024
LIGHT = pl.CostEstimate(flops=1_000_000, bytes_accessed=1_000_000, transcendentals=0)


def cost(micros):
    return pl.CostEstimate(flops=0, bytes_accessed=3_600_000 * micros, transcendentals=0)


def taps_kernel(taps_q, taps_k, scaling, kernel_ref, forward_ref, backward_ref):
    half = (taps_k - 1) // 2
    row = lax.broadcasted_iota(jnp.int32, (2 * LANES, LANES), 0)
    col = lax.broadcasted_iota(jnp.int32, (2 * LANES, LANES), 1)
    forth = col - row + EDGE + half
    back = row - col - EDGE + half
    for head in range(2):
        for tap in range(taps_q):
            ahead = jnp.zeros((2 * LANES, LANES), jnp.float32)
            behind = jnp.zeros((2 * LANES, LANES), jnp.float32)
            for tap_k in range(taps_k):
                value = kernel_ref[head, tap, tap_k]
                ahead = jnp.where(forth == tap_k, value, ahead)
                behind = jnp.where(back == tap_k, value, behind)
            ahead = ahead * scaling
            high = ahead.astype(jnp.bfloat16)
            cols = slice(tap * LANES, (tap + 1) * LANES)
            forward_ref[head, : 2 * LANES, cols] = high
            forward_ref[head, 2 * LANES : 4 * LANES, cols] = high
            forward_ref[head, 4 * LANES :, cols] = (ahead - high.astype(jnp.float32)).astype(jnp.bfloat16)
            backward_ref[head, tap * 2 * LANES : (tap + 1) * 2 * LANES, :] = behind.astype(jnp.bfloat16)


def tap_bands(kernels, scaling):
    heads, taps_q, taps_k = kernels.shape
    return pl.pallas_call(
        functools.partial(taps_kernel, taps_q, taps_k, scaling),
        out_shape=(
            jax.ShapeDtypeStruct((heads, 6 * LANES, taps_q * LANES), jnp.bfloat16),
            jax.ShapeDtypeStruct((heads, taps_q * 2 * LANES, LANES), jnp.bfloat16),
        ),
        in_specs=[pl.BlockSpec(memory_space=pltpu.SMEM)],
        out_specs=(pl.BlockSpec(memory_space=pltpu.VMEM),) * 2,
        compiler_params=pltpu.CompilerParams(vmem_limit_bytes=32 * 1024 * 1024),
        cost_estimate=LIGHT,
        name="tap_bands",
    )(kernels)


def columns_pair(own_ref, other_ref, core, chunk, s):
    own = own_ref[:, s * chunk : (s + 1) * chunk].astype(jnp.float32)
    other = other_ref[:, s * chunk : (s + 1) * chunk].astype(jnp.float32)
    return jnp.concatenate([jnp.where(core == 0, own, other), jnp.where(core == 0, other, own)], 1)


def place_columns_kernel(sections, chunk, chips, where_ref, *refs):
    ins, out_ref = refs[:-1], refs[-1]
    line, core = where_ref[0], where_ref[1]
    width = 2 * chunk
    for k in range(len(ins) // 2):
        for s in range(sections):
            at = pl.multiple_of(s * chips * width + (line ^ k) * width, LANES)
            out_ref[:, pl.ds(at, width)] = columns_pair(ins[2 * k], ins[2 * k + 1], core, chunk, s)


def place_columns(place, pieces, sections, chunk, chips):
    rows, cols = pieces[0].shape
    cols_out = 2 * sections * chunk * chips
    steps = 4 if rows % 64 == 0 else 1
    spec = pl.BlockSpec((rows // steps, cols), lambda s, place: (s, 0))
    return pl.pallas_call(
        functools.partial(place_columns_kernel, sections, chunk, chips),
        out_shape=jax.ShapeDtypeStruct((rows, cols_out), jnp.float32),
        grid_spec=pltpu.PrefetchScalarGridSpec(
            num_scalar_prefetch=1,
            grid=(steps,),
            in_specs=[spec] * len(pieces),
            out_specs=pl.BlockSpec((rows // steps, cols_out), lambda s, place: (s, 0)),
        ),
        compiler_params=pltpu.CompilerParams(vmem_limit_bytes=24 * 1024 * 1024),
        cost_estimate=cost(5),
        name="place_columns",
    )(place, *pieces)


def add_columns_kernel(sections, chunk, chips, chip, place_ref, own_ref, other_ref, base_ref, out_ref, blocks, sems):
    del base_ref
    line, core = place_ref[0], place_ref[1]
    width = 2 * chunk
    copies = []
    for s in range(sections):
        blocks[s] = columns_pair(own_ref, other_ref, core, chunk, s)
        at = pl.multiple_of(s * chips * width + (line ^ chip) * width, LANES)
        copy = pltpu.make_async_copy(blocks.at[s], out_ref.at[:, pl.ds(at, width)], sems.at[s])
        copy.start()
        copies.append(copy)
    for copy in copies:
        copy.wait()


def add_columns(place, own, other, base, sections, chunk, chips, chip):
    vmem = pl.BlockSpec(memory_space=pltpu.VMEM)
    anywhere = pl.BlockSpec(memory_space=pl.ANY)
    return pl.pallas_call(
        functools.partial(add_columns_kernel, sections, chunk, chips, chip),
        out_shape=jax.ShapeDtypeStruct(base.shape, base.dtype),
        in_specs=[pl.BlockSpec(memory_space=pltpu.SMEM), vmem, vmem, anywhere],
        out_specs=anywhere,
        scratch_shapes=[
            pltpu.VMEM((sections, own.shape[0], 2 * chunk), jnp.float32), pltpu.SemaphoreType.DMA((sections,)),
        ],
        input_output_aliases={3: 0},
        compiler_params=pltpu.CompilerParams(vmem_limit_bytes=12 * 1024 * 1024),
        cost_estimate=cost(2),
        name="add_columns",
    )(place, own, other, base)


def place_feed_kernel(sections, chunk, pieces, where_ref, *refs):
    ins, gate_ref, down_ref = refs[:pieces], refs[pieces], refs[pieces + 1]
    line, core = where_ref[0], where_ref[1]
    width = 2 * chunk
    chips = pieces // 2
    gate_cols = sections * chunk
    for k in range(chips):
        own = ins[2 * k][...].astype(jnp.float32)
        other = ins[2 * k + 1][...].astype(jnp.float32)
        first = jnp.where(core == 0, own, other)
        second = jnp.where(core == 0, other, own)
        for s in range(sections):
            both = jnp.concatenate([first[:, s * chunk : (s + 1) * chunk], second[:, s * chunk : (s + 1) * chunk]], 1)
            at = pl.multiple_of(s * chips * width + (line ^ k) * width, LANES)
            gate_ref[:, pl.ds(at, width)] = both
        at = pl.multiple_of((line ^ k) * width, width)
        down_ref[pl.ds(at, chunk), :] = first[:, gate_cols:]
        down_ref[pl.ds(at + chunk, chunk), :] = second[:, gate_cols:]


def place_feed(place, pieces, chunk):
    rows, cols = pieces[0].shape
    blocks = rows // chunk
    sections = (cols // chunk) * 2 // 3
    hidden = cols - sections * chunk
    spec = pl.BlockSpec((chunk, cols), lambda s, place: (s, 0))
    gate_cols = sections * chunk * len(pieces)
    return pl.pallas_call(
        functools.partial(place_feed_kernel, sections, chunk, len(pieces)),
        out_shape=(
            jax.ShapeDtypeStruct((rows, gate_cols), jnp.float32),
            jax.ShapeDtypeStruct((chunk * len(pieces), hidden * blocks), jnp.float32),
        ),
        grid_spec=pltpu.PrefetchScalarGridSpec(
            num_scalar_prefetch=1,
            grid=(blocks,),
            in_specs=[spec] * len(pieces),
            out_specs=(
                pl.BlockSpec((chunk, gate_cols), lambda s, place: (s, 0)),
                pl.BlockSpec((chunk * len(pieces), hidden), lambda s, place: (0, s)),
            ),
        ),
        compiler_params=pltpu.CompilerParams(vmem_limit_bytes=ROOM),
        cost_estimate=cost(11),
        name="place_feed",
    )(place, *pieces)


def masked_scores(q_blk, keys, since, first_row):
    scores = lax.dot_general(q_blk, keys, (((1,), (1,)), ((), ())), preferred_element_type=jnp.float32)
    rows = first_row + lax.broadcasted_iota(jnp.int32, scores.shape, 0)
    back = rows + EDGE - lax.broadcasted_iota(jnp.int32, scores.shape, 1)
    limit = jnp.concatenate([since] * (scores.shape[1] // LANES), 1)
    return jnp.where((back >= 0) & (back <= limit), scores, 0.0)


def head_places(heads, head_size):
    return [((head * head_size) // LANES, (head * head_size) % LANES) for head in range(heads)]


def split_heads(joined, heads, head_size):
    real = lax.broadcasted_iota(jnp.int32, (joined.shape[0], LANES), 1) < head_size
    out = []
    for tile, shift in head_places(heads, head_size):
        if shift:
            both = joined[:, tile * LANES : (tile + 2) * LANES]
            piece = pltpu.roll(both, 2 * LANES - shift, 1)[:, :LANES]
        else:
            piece = joined[:, tile * LANES : (tile + 1) * LANES]
        out.append(jnp.where(real, piece, 0.0))
    return out


def join_heads(pieces, head_size):
    count = pieces[0].shape[0]
    nothing = jnp.zeros((count, LANES), jnp.float32)
    tiles = [nothing] * 5
    for piece, (tile, shift) in zip(pieces, head_places(len(pieces), head_size)):
        if shift:
            both = pltpu.roll(jnp.concatenate([piece, nothing], 1), shift, 1)
            tiles[tile] = tiles[tile] + both[:, :LANES]
            tiles[tile + 1] = tiles[tile + 1] + both[:, LANES:]
        else:
            tiles[tile] = tiles[tile] + piece
    return jnp.concatenate(tiles, 1)


def forward_kernel(taps_q, head_size, rows, core_ref, mix_ref, joined_ref, taps_ref, gain_ref, *refs):
    halves, outs = refs[: 2 * rows], refs[2 * rows : 2 * rows + 5]
    (
        pieces, proj, att, grouped, maps, since_all, keys_pad, s_high, s_low, spread, grouped_row, in_sems, out_sems
    ) = refs[2 * rows + 5 :]
    width = joined_ref.shape[0]
    arrivals = [pltpu.make_async_copy(ref, pieces.at[i], in_sems.at[i]) for i, ref in enumerate(halves)]
    for arrival in arrivals:
        arrival.start()
    seq_len = proj.shape[1]
    half_len = seq_len // 2
    blocks = seq_len // LANES
    core = core_ref[0]
    keys_pad[...] = jnp.zeros_like(keys_pad)
    s_high[...] = jnp.zeros_like(s_high)
    s_low[...] = jnp.zeros_like(s_low)

    def project(step, carry):
        pltpu.make_async_copy(halves[0], pieces.at[step], in_sems.at[step]).wait()
        row, part = lax.div(step, 2), lax.rem(step, 2)
        at = pl.multiple_of(jnp.bitwise_xor(core, part) * half_len, half_len)
        joined = jnp.dot(pieces[step, :, :width], joined_ref[...], preferred_element_type=jnp.float32)
        extra = pieces[step, :, width:].astype(jnp.float32)
        since = (extra[:, 0:1] * 256.0 + extra[:, 1:2]).astype(jnp.int32)
        since_all[row, pl.ds(at, half_len), :] = jnp.broadcast_to(since, (half_len, LANES))
        for head, piece in enumerate(split_heads(joined, 6, head_size)):
            proj[row, pl.ds(at, half_len), head * LANES : (head + 1) * LANES] = piece.astype(jnp.bfloat16)
        return carry

    lax.fori_loop(0, 2 * rows, project, 0)
    real = lax.broadcasted_iota(jnp.int32, (LANES, LANES), 1) < head_size

    def mix_row(row):
        for qi in range(blocks):
            first = qi * LANES
            width = (qi + 1) * LANES
            low = maps[row, 0, first : first + LANES, :width]
            upp = maps[row, 1, first : first + LANES, :width]
            for head in range(2):
                mixed = (mix_ref[head, 0] * low + mix_ref[head, 1] * upp).astype(jnp.bfloat16)
                cols = slice(head * LANES, (head + 1) * LANES)
                attended = jnp.dot(
                    mixed, proj[row, :width, (4 + head) * LANES : (5 + head) * LANES],
                    preferred_element_type=jnp.float32,
                )
                att[row, first : first + LANES, cols] = attended
                normal, _ = normalize(attended, real, head_size)
                grouped_row[first : first + LANES, cols] = (normal * gain_ref[:, cols]).astype(jnp.bfloat16)
        for part in range(2):
            at = pl.multiple_of(jnp.bitwise_xor(core, part) * half_len, half_len)
            grouped[row, part * half_len : (part + 1) * half_len, :] = grouped_row[pl.ds(at, half_len), :]
        for copy in copies_out(row):
            copy.start()

    def copies_out(row):
        return [
            pltpu.make_async_copy(here.at[row], there.at[row], out_sems.at[kind, row])
            for kind, (here, there) in enumerate(zip((proj, att, grouped, maps, since_all), outs))
        ]

    def one_head(step, carry):
        row, head = lax.div(step, 2), lax.rem(step, 2)
        proj_ref, since_ref, weights_ref = proj.at[row], since_all.at[row], maps.at[row]
        lane = pl.multiple_of(head * LANES, LANES)
        lane_k = pl.multiple_of((head + 2) * LANES, LANES)
        keys_pad[EDGE : EDGE + seq_len, :] = proj_ref[:, pl.ds(lane_k, LANES)]
        for qi in range(blocks):
            first = qi * LANES
            width = (qi + 2) * LANES
            scores = masked_scores(
                proj_ref[first : first + LANES, pl.ds(lane, LANES)],
                keys_pad[:width, :],
                since_ref[first : first + LANES, :],
                first,
            )
            high = scores.astype(jnp.bfloat16)
            s_high[TOP + first : TOP + first + LANES, :width] = high
            s_low[TOP + first : TOP + first + LANES, :width] = (scores - high.astype(jnp.float32)).astype(jnp.bfloat16)
        for m in range(blocks):
            first = m * LANES
            count = seq_len - first
            high = s_high[first:, first : first + 2 * LANES]
            left = jnp.concatenate([high, s_low[first:, first : first + 2 * LANES], high], 1)
            spread[first:, :] = jnp.dot(left, taps_ref[head], preferred_element_type=jnp.float32)
            since = since_ref[first:, :]
            logits = spread[TOP + first :, :LANES]
            for tap in range(1, taps_q):
                moved = spread[TOP + first - tap : TOP + seq_len - tap, tap * LANES : (tap + 1) * LANES]
                logits = logits + jnp.where(since >= tap, moved, 0.0)
            weights_ref[head, first:, first : first + LANES] = logits
        for qi in range(blocks):
            first = qi * LANES
            width = (qi + 1) * LANES
            logits = weights_ref[head, first : first + LANES, :width]
            rows = first + lax.broadcasted_iota(jnp.int32, logits.shape, 0)
            back = rows - lax.broadcasted_iota(jnp.int32, logits.shape, 1)
            limit = jnp.concatenate([since_ref[first : first + LANES, :]] * (qi + 1), 1)
            logits = jnp.where((back >= 0) & (back <= limit), logits, -1e30)
            raised = jnp.exp(logits - jnp.max(logits, axis=1, keepdims=True))
            weights_ref[head, first : first + LANES, :width] = raised / jnp.sum(raised, axis=1, keepdims=True)

        @pl.when(head == 1)
        def _():
            mix_row(row)

        return carry

    lax.fori_loop(0, 2 * rows, one_head, 0)
    for row in range(rows):
        for copy in copies_out(row):
            copy.wait()


def normalize(att, real, head_size):
    mean = jnp.sum(att, axis=1, keepdims=True) * (1.0 / head_size)
    centered = jnp.where(real, att - mean, 0.0)
    spread = jnp.sum(centered * centered, axis=1, keepdims=True) * (1.0 / head_size)
    scale = lax.rsqrt(spread + 1e-05)
    return centered * scale, scale


def attend_rows(core, halves, mix, joined, taps_forward, gain_pad, taps_q, head_size):
    rows, seq_len = len(halves) // 2, 2 * halves[0].shape[0]
    full = seq_len + 2 * EDGE
    vmem = pl.BlockSpec(memory_space=pltpu.VMEM)
    smem = pl.BlockSpec(memory_space=pltpu.SMEM)
    anywhere = pl.BlockSpec(memory_space=pl.ANY)
    shapes = (
        ((rows, seq_len, 6 * LANES), jnp.bfloat16),
        ((rows, seq_len, 2 * LANES), jnp.float32),
        ((rows, seq_len, 2 * LANES), jnp.bfloat16),
        ((rows, 2, seq_len, seq_len), jnp.float32),
        ((rows, seq_len, LANES), jnp.int32),
    )
    return pl.pallas_call(
        functools.partial(forward_kernel, taps_q, head_size, rows),
        out_shape=tuple(jax.ShapeDtypeStruct(*a) for a in shapes),
        in_specs=[smem, smem] + [vmem] * 3 + [anywhere] * len(halves),
        out_specs=(anywhere,) * 5,
        scratch_shapes=[pltpu.VMEM((len(halves),) + halves[0].shape, jnp.bfloat16)]
        + [pltpu.VMEM(*a) for a in shapes]
        + [
            pltpu.VMEM((full, LANES), jnp.bfloat16),
            pltpu.VMEM((TOP + seq_len, full), jnp.bfloat16),
            pltpu.VMEM((TOP + seq_len, full), jnp.bfloat16),
            pltpu.VMEM((TOP + seq_len, taps_q * LANES), jnp.float32),
            pltpu.VMEM((seq_len, 2 * LANES), jnp.bfloat16),
            pltpu.SemaphoreType.DMA((len(halves),)),
            pltpu.SemaphoreType.DMA((5, rows)),
        ],
        compiler_params=pltpu.CompilerParams(vmem_limit_bytes=52 * 1024 * 1024),
        cost_estimate=LIGHT,
        name="attend_rows",
    )(core, mix, joined, taps_forward, gain_pad, *halves)


def backward_kernel(
    taps_q, taps_k, head_size, scaling, row, core_ref, mix_ref, own_ref, other_ref, out_weight_ref, joined_ref,
    taps_ref, gain_ref, proj_all, since_all, att_all, weights_all,
    joined_grad_ref, mine_ref, theirs_ref, small_ref, tap_ref,
    keys_pad, grad_att, conv_grad, shifted, s_low, s_grad, since_pad, grad_ref, out_ref,
    proj_ref, since_ref, att_ref, weights_ref, sems,
):
    arrivals = [
        pltpu.make_async_copy(source.at[row], here, sems.at[i])
        for i, (source, here) in enumerate(
            ((since_all, since_ref), (att_all, att_ref), (proj_all, proj_ref), (weights_all, weights_ref))
        )
    ]
    for arrival in arrivals:
        arrival.start()
    seq_len = proj_ref.shape[0]
    half_len = seq_len // 2
    own_at = pl.multiple_of(core_ref[0] * half_len, half_len)
    other_at = pl.multiple_of((1 - core_ref[0]) * half_len, half_len)
    for ref, at in ((own_ref, own_at), (other_ref, other_at)):
        grad_ref[pl.ds(at, half_len), :] = lax.dot_general(
            ref[...], out_weight_ref[...], (((1,), (1,)), ((), ())), preferred_element_type=jnp.float32
        )
    blocks = seq_len // LANES
    half = (taps_k - 1) // 2
    full = seq_len + 2 * EDGE
    keys_pad[...] = jnp.zeros_like(keys_pad)
    s_low[...] = jnp.zeros_like(s_low)
    s_grad[...] = jnp.zeros_like(s_grad)
    shifted[...] = jnp.zeros_like(shifted)
    conv_grad[...] = jnp.zeros_like(conv_grad)
    for arrival in arrivals:
        arrival.wait()
    since_pad[:seq_len, :] = since_ref[...]
    since_pad[seq_len:, :] = jnp.zeros((8, LANES), jnp.int32)
    small_ref[...] = jnp.zeros_like(small_ref)

    real = lax.broadcasted_iota(jnp.int32, (LANES, LANES), 1) < head_size
    for head in range(2):
        cols = slice(head * LANES, (head + 1) * LANES)
        group_sum = jnp.zeros((1, LANES), jnp.float32)
        for qi in range(blocks):
            rows = slice(qi * LANES, (qi + 1) * LANES)
            normal, scale = normalize(att_ref[rows, cols], real, head_size)
            grad = grad_ref[rows, cols]
            group_sum = group_sum + jnp.sum(grad * normal, axis=0, keepdims=True)
            lift = grad * gain_ref[:, cols]
            mean = jnp.sum(lift, axis=1, keepdims=True) * (1.0 / head_size)
            along = jnp.sum(lift * normal, axis=1, keepdims=True) * (1.0 / head_size)
            grad_att[rows, cols] = jnp.where(real, scale * (lift - mean - normal * along), 0.0).astype(jnp.bfloat16)
        small_ref[head : head + 1, :] = group_sum

    sums = [[jnp.zeros((1, LANES), jnp.float32) for _ in range(2)] for _ in range(2)]
    grad_v = [[], []]
    for qi in range(blocks):
        first = qi * LANES
        width = (qi + 1) * LANES
        rows = slice(first, first + LANES)
        maps = [weights_ref[k, rows, :width] for k in range(2)]
        grad_mixed = []
        for head in range(2):
            cols = slice(head * LANES, (head + 1) * LANES)
            values = proj_ref[:width, (4 + head) * LANES : (5 + head) * LANES]
            gm = lax.dot_general(
                grad_att[rows, cols], values, (((1,), (1,)), ((), ())), preferred_element_type=jnp.float32
            )
            grad_mixed.append(gm)
        for head in range(2):
            for k in range(2):
                part = jnp.sum(grad_mixed[head] * maps[k], axis=0, keepdims=True)
                for b in range(qi + 1):
                    sums[head][k] = sums[head][k] + part[:, b * LANES : (b + 1) * LANES]
        for k in range(2):
            grad_w = mix_ref[0, k] * grad_mixed[0] + mix_ref[1, k] * grad_mixed[1]
            inner = jnp.sum(grad_w * maps[k], axis=1, keepdims=True)
            conv_grad[k, rows, :width] = maps[k] * (grad_w - inner)
    for head in range(2):
        for k in range(2):
            small_ref[2 + 2 * head + k : 3 + 2 * head + k, :] = sums[head][k]
        cols = slice(head * LANES, (head + 1) * LANES)
        for kb in range(blocks):
            first = kb * LANES
            mixed = (
                mix_ref[head, 0] * weights_ref[0, first:, first : first + LANES]
                + mix_ref[head, 1] * weights_ref[1, first:, first : first + LANES]
            ).astype(jnp.bfloat16)
            out_ref[first : first + LANES, (4 + head) * LANES : (5 + head) * LANES] = lax.dot_general(
                mixed, grad_att[first:, cols], (((0,), (0,)), ((), ())), preferred_element_type=jnp.float32
            )

    def one_head(head, carry):
        lane = pl.multiple_of(head * LANES, LANES)
        lane_k = pl.multiple_of((head + 2) * LANES, LANES)
        keys_pad[EDGE : EDGE + seq_len, :] = proj_ref[:, pl.ds(lane_k, LANES)]
        for qi in range(blocks):
            first = qi * LANES
            width = (qi + 2) * LANES
            scores = masked_scores(
                proj_ref[first : first + LANES, pl.ds(lane, LANES)],
                keys_pad[:width, :],
                since_ref[first : first + LANES, :],
                first,
            )
            s_low[TOP + first : TOP + first + LANES, :width] = scores.astype(jnp.bfloat16)
            reach = min(width, seq_len)
            for tap in range(taps_q):
                moved = conv_grad[head, first + tap : first + tap + LANES, :reach]
                if tap > 0:
                    limit = since_pad[first + tap : first + tap + LANES, :]
                    limit = jnp.concatenate([limit] * (reach // LANES), 1)
                    moved = jnp.where(limit >= tap, moved, 0.0)
                shifted[tap, TOP + first : TOP + first + LANES, LANES : LANES + reach] = moved.astype(jnp.bfloat16)
        for m in range(blocks + 1):
            first = max(m - 1, 0) * LANES
            left = jnp.concatenate(
                [shifted[tap, TOP + first :, m * LANES : (m + 2) * LANES] for tap in range(taps_q)], 1
            )
            grad = jnp.dot(left, taps_ref[head], preferred_element_type=jnp.float32)
            rows = first + lax.broadcasted_iota(jnp.int32, grad.shape, 0)
            back = rows + EDGE - m * LANES - lax.broadcasted_iota(jnp.int32, grad.shape, 1)
            keep = (back >= 0) & (back <= since_ref[first:, :])
            s_grad[first:, m * LANES : (m + 1) * LANES] = jnp.where(keep, grad, 0.0).astype(jnp.bfloat16)
        total = jnp.zeros((2 * LANES, taps_q * LANES), jnp.float32)
        for m in range(blocks):
            first = m * LANES
            right = jnp.concatenate(
                [shifted[tap, first:, (m + 1) * LANES : (m + 2) * LANES] for tap in range(taps_q)], 1
            )
            total = total + lax.dot_general(
                s_low[first:, first : first + 2 * LANES], right, (((0,), (0,)), ((), ())),
                preferred_element_type=jnp.float32,
            )
        ridge = lax.broadcasted_iota(jnp.int32, (2 * LANES, LANES), 1) - lax.broadcasted_iota(
            jnp.int32, (2 * LANES, LANES), 0
        )
        for tap_k in range(taps_k):
            on = ridge == tap_k - EDGE - half
            for tap in range(taps_q):
                line = jnp.where(on, total[:, tap * LANES : (tap + 1) * LANES], 0.0)
                tap_ref[head, tap * taps_k + tap_k : tap * taps_k + tap_k + 1, :] = jnp.sum(line, axis=0, keepdims=True)
        for qi in range(blocks):
            first = qi * LANES
            width = (qi + 2) * LANES
            grad_q = jnp.dot(
                s_grad[first : first + LANES, :width], keys_pad[:width, :], preferred_element_type=jnp.float32
            )
            out_ref[first : first + LANES, pl.ds(lane, LANES)] = grad_q * scaling
        for kb in range(blocks):
            first = kb * LANES
            grad_k = lax.dot_general(
                s_grad[first:, first + EDGE : first + EDGE + LANES],
                proj_ref[first:, pl.ds(lane, LANES)],
                (((0,), (0,)), ((), ())),
                preferred_element_type=jnp.float32,
            )
            out_ref[first : first + LANES, pl.ds(lane_k, LANES)] = grad_k * scaling
        return carry

    lax.fori_loop(0, 2, one_head, 0)
    for at, first in ((own_at, 0), (other_at, half_len)):
        pieces = [out_ref[pl.ds(at, half_len), head * LANES : (head + 1) * LANES] for head in range(6)]
        joined = join_heads(pieces, head_size).astype(jnp.bfloat16)
        joined_grad_ref[first : first + half_len, :] = joined
        grad_in = lax.dot_general(
            joined, joined_ref[...], (((1,), (1,)), ((), ())), preferred_element_type=jnp.float32
        )
        if first:
            theirs_ref[...] = grad_in.astype(jnp.bfloat16)
        else:
            mine_ref[...] = grad_in.astype(jnp.bfloat16)


def attend_row_back(
    row, core, own, other, out_weight, joined, saved, since, mix, taps_backward, gain_pad, taps_q, taps_k, head_size
):
    projected, att, weights = saved
    seq_len = projected.shape[1]
    width = own.shape[1]
    full = seq_len + 2 * EDGE
    vmem = pl.BlockSpec(memory_space=pltpu.VMEM)
    smem = pl.BlockSpec(memory_space=pltpu.SMEM)
    anywhere = pl.BlockSpec(memory_space=pl.ANY)
    return pl.pallas_call(
        functools.partial(backward_kernel, taps_q, taps_k, head_size, head_size ** (-0.5), row),
        out_shape=(
            jax.ShapeDtypeStruct((seq_len, joined.shape[1]), jnp.bfloat16),
            jax.ShapeDtypeStruct((seq_len // 2, width), jnp.bfloat16),
            jax.ShapeDtypeStruct((seq_len // 2, width), jnp.bfloat16),
            jax.ShapeDtypeStruct((8, LANES), jnp.float32),
            jax.ShapeDtypeStruct((2, taps_q * taps_k, LANES), jnp.float32),
        ),
        in_specs=[smem, smem] + [vmem] * 6 + [anywhere] * 4,
        out_specs=(vmem,) * 5,
        scratch_shapes=[
            pltpu.VMEM((full, LANES), jnp.bfloat16),
            pltpu.VMEM((seq_len, 2 * LANES), jnp.bfloat16),
            pltpu.VMEM((2, seq_len + 8, seq_len), jnp.float32),
            pltpu.VMEM((taps_q, TOP + seq_len, seq_len + 2 * LANES), jnp.bfloat16),
            pltpu.VMEM((TOP + seq_len, full), jnp.bfloat16),
            pltpu.VMEM((seq_len, full), jnp.bfloat16),
            pltpu.VMEM((seq_len + 8, LANES), jnp.int32),
            pltpu.VMEM((seq_len, 2 * LANES), jnp.float32),
            pltpu.VMEM((seq_len, 6 * LANES), jnp.float32),
            pltpu.VMEM(projected.shape[1:], jnp.bfloat16),
            pltpu.VMEM(since.shape[1:], jnp.int32),
            pltpu.VMEM(att.shape[1:], jnp.float32),
            pltpu.VMEM(weights.shape[1:], jnp.float32),
            pltpu.SemaphoreType.DMA((4,)),
        ],
        compiler_params=pltpu.CompilerParams(vmem_limit_bytes=48 * 1024 * 1024),
        cost_estimate=cost(14),
        name="attend_row_back",
    )(core, mix, own, other, out_weight, joined, taps_backward, gain_pad, projected, since, att, weights)


def split_kernel(wide, feed_ref, gate_ref, down_ref):
    cols = down_ref.shape[0]
    chunk = cols // wide
    blocks = down_ref.shape[1] // cols
    gate_ref[...] = feed_ref[:, : 2 * cols]
    for z in range(wide):
        for b in range(blocks):
            first = (z * blocks + b) * chunk
            down_ref[z * chunk : (z + 1) * chunk, b * cols : (b + 1) * cols] = feed_ref[first : first + chunk, 2 * cols :]


def split_feed(feed, wide):
    vmem = pl.BlockSpec(memory_space=pltpu.VMEM)
    rows, cols = feed.shape[0], feed.shape[1] // 3
    return pl.pallas_call(
        functools.partial(split_kernel, wide),
        out_shape=(
            jax.ShapeDtypeStruct((rows, 2 * cols), jnp.bfloat16), jax.ShapeDtypeStruct((cols, rows), jnp.bfloat16),
        ),
        in_specs=[vmem],
        out_specs=(vmem,) * 2,
        compiler_params=pltpu.CompilerParams(vmem_limit_bytes=24 * 1024 * 1024),
        cost_estimate=LIGHT,
        name="split_feed",
    )(feed)


def feed_kernel(own_ref, other_ref, cot_own_ref, cot_other_ref, gate_ref, down_ref,
                hidden_ref, grads_ref, ffn_mine_ref, ffn_theirs_ref, back_mine_ref, back_theirs_ref):
    half_len = own_ref.shape[0]
    cols = down_ref.shape[0]
    for first, ref, cot_ref in ((0, own_ref, cot_own_ref), (half_len, other_ref, cot_other_ref)):
        rows = slice(first, first + half_len)
        both = jnp.dot(ref[...], gate_ref[...], preferred_element_type=jnp.float32)
        gating, upward = both[:, :cols], both[:, cols:]
        grad = lax.dot_general(
            cot_ref[...], down_ref[...], (((1,), (1,)), ((), ())), preferred_element_type=jnp.float32
        )
        sig = 1.0 / (1.0 + jnp.exp(-gating))
        silu = gating * sig
        hidden = (silu * upward).astype(jnp.bfloat16)
        hidden_ref[rows, :] = hidden
        grads_ref[rows, :cols] = (grad * upward * (sig * (1.0 + gating * (1.0 - sig)))).astype(jnp.bfloat16)
        grads_ref[rows, cols:] = (grad * silu).astype(jnp.bfloat16)
        back = lax.dot_general(
            grads_ref[rows, :], gate_ref[...], (((1,), (1,)), ((), ())), preferred_element_type=jnp.float32
        )
        ffn = jnp.dot(hidden, down_ref[...], preferred_element_type=jnp.float32)
        if first:
            back_theirs_ref[...] = back.astype(jnp.bfloat16)
            ffn_theirs_ref[...] = ffn.astype(jnp.bfloat16)
        else:
            back_mine_ref[...] = back.astype(jnp.bfloat16)
            ffn_mine_ref[...] = ffn.astype(jnp.bfloat16)


def feed_row(own, other, cot_own, cot_other, gate, down):
    half_len, width = own.shape
    cols = down.shape[0]
    vmem = pl.BlockSpec(memory_space=pltpu.VMEM)
    return pl.pallas_call(
        feed_kernel,
        out_shape=(
            jax.ShapeDtypeStruct((2 * half_len, cols), jnp.bfloat16),
            jax.ShapeDtypeStruct((2 * half_len, 2 * cols), jnp.bfloat16),
            jax.ShapeDtypeStruct((half_len, width), jnp.bfloat16),
            jax.ShapeDtypeStruct((half_len, width), jnp.bfloat16),
            jax.ShapeDtypeStruct((half_len, width), jnp.bfloat16),
            jax.ShapeDtypeStruct((half_len, width), jnp.bfloat16),
        ),
        in_specs=[vmem] * 6,
        out_specs=(vmem,) * 6,
        compiler_params=pltpu.CompilerParams(vmem_limit_bytes=48 * 1024 * 1024),
        cost_estimate=cost(8),
        name="feed_row",
    )(own, other, cot_own, cot_other, gate, down)


def feed_grad_kernel(counts, *refs):
    lefts, grads, hiddens, cots = (
        jnp.concatenate([ref[...] for ref in refs[sum(counts[:i]) : sum(counts[: i + 1])]], 0) for i in range(4)
    )
    out_ref = refs[-1]
    chunk = hiddens.shape[1]
    cols = out_ref.shape[1] - grads.shape[1]
    out_ref[:, : grads.shape[1]] = lax.dot_general(
        lefts, grads, (((0,), (0,)), ((), ())), preferred_element_type=jnp.float32
    ).astype(jnp.bfloat16)
    down = lax.dot_general(hiddens, cots, (((0,), (0,)), ((), ())), preferred_element_type=jnp.float32)
    for b in range(down.shape[1] // cols):
        out_ref[b * chunk : (b + 1) * chunk, grads.shape[1] :] = down[:, b * cols : (b + 1) * cols].astype(jnp.bfloat16)


def feed_grad(lefts, grads, hiddens, cots, wide):
    width = lefts[0].shape[1]
    cols = hiddens[0].shape[1]
    block, chunk = width // wide, cols // wide
    if block % LANES or chunk % LANES:
        gate = lax.dot_general(
            jnp.concatenate(lefts, 0), jnp.concatenate(grads, 0), (((0,), (0,)), ((), ())),
            preferred_element_type=jnp.float32,
        )
        down = lax.dot_general(
            jnp.concatenate(hiddens, 0), jnp.concatenate(cots, 0), (((0,), (0,)), ((), ())),
            preferred_element_type=jnp.float32,
        )
        down = jnp.swapaxes(down.reshape(wide, chunk, width // cols, cols), 1, 2).reshape(width, cols)
        return jnp.concatenate([gate, down], 1).astype(jnp.bfloat16)
    count = sum(a.shape[0] for a in lefts)
    cols_out = grads[0].shape[1] + cols
    return pl.pallas_call(
        functools.partial(feed_grad_kernel, (len(lefts), len(grads), len(hiddens), len(cots))),
        out_shape=jax.ShapeDtypeStruct((width, cols_out), jnp.bfloat16),
        grid=(wide,),
        in_specs=[pl.BlockSpec((a.shape[0], block), lambda s: (0, s)) for a in lefts]
        + [pl.BlockSpec(a.shape, lambda s: (0, 0)) for a in grads]
        + [pl.BlockSpec((a.shape[0], chunk), lambda s: (0, s)) for a in hiddens]
        + [pl.BlockSpec(a.shape, lambda s: (0, 0)) for a in cots],
        out_specs=pl.BlockSpec((block, cols_out), lambda s: (s, 0)),
        compiler_params=pltpu.CompilerParams(vmem_limit_bytes=ROOM),
        cost_estimate=cost(17),
        name="feed_grad",
    )(*lefts, *grads, *hiddens, *cots)


def weight_kernel(lefts, *refs):
    left = jnp.concatenate([ref[...] for ref in refs[:lefts]], 0)
    right = jnp.concatenate([ref[...] for ref in refs[lefts:-1]], 0)
    refs[-1][...] = lax.dot_general(
        left, right, (((0,), (0,)), ((), ())), preferred_element_type=jnp.float32
    ).astype(jnp.bfloat16)


def small_weight_grad(lefts, rights, name):
    vmem = pl.BlockSpec(memory_space=pltpu.VMEM)
    return pl.pallas_call(
        functools.partial(weight_kernel, len(lefts)),
        out_shape=jax.ShapeDtypeStruct((lefts[0].shape[1], rights[0].shape[1]), jnp.bfloat16),
        in_specs=[vmem] * (len(lefts) + len(rights)),
        out_specs=vmem,
        compiler_params=pltpu.CompilerParams(vmem_limit_bytes=32 * 1024 * 1024),
        cost_estimate=cost(3),
        name=name,
    )(*lefts, *rights)


def weight_grad(lefts, rights, block, name):
    rows_out, cols_out = lefts[0].shape[1] // block * block, rights[0].shape[1]
    count = sum(a.shape[0] for a in lefts)
    return pl.pallas_call(
        functools.partial(weight_kernel, len(lefts)),
        out_shape=jax.ShapeDtypeStruct((rows_out, cols_out), jnp.bfloat16),
        grid=(rows_out // block,),
        in_specs=[pl.BlockSpec((a.shape[0], block), lambda s: (0, s)) for a in lefts]
        + [pl.BlockSpec(a.shape, lambda s: (0, 0)) for a in rights],
        out_specs=pl.BlockSpec((block, cols_out), lambda s: (s, 0)),
        compiler_params=pltpu.CompilerParams(vmem_limit_bytes=ROOM),
        cost_estimate=cost(8),
        name=name,
    )(*lefts, *rights)


def halves_kernel(mine_ref, came_ref, low_ref, high_ref):
    cut = low_ref.shape[0]
    low_ref[...] = (mine_ref[:cut, :].astype(jnp.float32) + came_ref[:cut, :].astype(jnp.float32)).astype(jnp.bfloat16)
    high_ref[...] = (mine_ref[cut:, :].astype(jnp.float32) + came_ref[cut:, :].astype(jnp.float32)).astype(jnp.bfloat16)


def sum_halves(mine, came):
    half = jax.ShapeDtypeStruct((mine.shape[0] // 2, mine.shape[1]), jnp.bfloat16)
    vmem = pl.BlockSpec(memory_space=pltpu.VMEM)
    return pl.pallas_call(
        halves_kernel, out_shape=(half, half), in_specs=[vmem] * 2, out_specs=(vmem,) * 2,
        compiler_params=pltpu.CompilerParams(vmem_limit_bytes=4 * 1024 * 1024), cost_estimate=LIGHT, name="sum_halves",
    )(mine, came)


def sum_kernel(second, mine_ref, came_ref, extra_ref, out_ref):
    cut = extra_ref.shape[0]
    rows, rest = (slice(cut, 2 * cut), slice(0, cut)) if second else (slice(0, cut), slice(cut, 2 * cut))
    total = mine_ref[rows, :].astype(jnp.float32) + came_ref[rows, :].astype(jnp.float32) + extra_ref[...].astype(jnp.float32)
    out_ref[rows, :] = total.astype(jnp.bfloat16)
    out_ref[rest, :] = (mine_ref[rest, :].astype(jnp.float32) + came_ref[rest, :].astype(jnp.float32)).astype(jnp.bfloat16)


def low_sum(mine, came, extra, second):
    vmem = pl.BlockSpec(memory_space=pltpu.VMEM)
    return pl.pallas_call(
        functools.partial(sum_kernel, second), out_shape=jax.ShapeDtypeStruct(mine.shape, jnp.bfloat16),
        in_specs=[vmem] * 3, out_specs=vmem,
        compiler_params=pltpu.CompilerParams(vmem_limit_bytes=4 * 1024 * 1024), cost_estimate=LIGHT, name="low_sum",
    )(mine, came, extra)


def pair_kernel(mine_ref, came_ref, out_ref):
    out_ref[...] = (mine_ref[...].astype(jnp.float32) + came_ref[...].astype(jnp.float32)).astype(jnp.bfloat16)


def pair_sum(mine, came):
    vmem = pl.BlockSpec(memory_space=pltpu.VMEM)
    return pl.pallas_call(
        pair_kernel, out_shape=jax.ShapeDtypeStruct(mine.shape, jnp.bfloat16), in_specs=[vmem] * 2, out_specs=vmem,
        compiler_params=pltpu.CompilerParams(vmem_limit_bytes=4 * 1024 * 1024), cost_estimate=LIGHT, name="pair_sum",
    )(mine, came)


def place_out_kernel(place_ref, *refs):
    out_ref = refs[-1]
    out_ref[...] = jnp.zeros_like(out_ref)
    for step, ref in enumerate(refs[:-1]):
        chunk = jnp.bitwise_xor(place_ref[0], step)
        rows = ref.shape[0]
        at = pl.multiple_of(lax.div(chunk, 2) * LANES + lax.rem(chunk, 2) * rows, 16)
        out_ref[pl.ds(at, rows), :] = ref[...]


def place_out(place, pieces):
    vmem = pl.BlockSpec(memory_space=pltpu.VMEM)
    return pl.pallas_call(
        place_out_kernel,
        out_shape=jax.ShapeDtypeStruct((2 * LANES, pieces[0].shape[1]), jnp.bfloat16),
        in_specs=[pl.BlockSpec(memory_space=pltpu.SMEM)] + [vmem] * len(pieces),
        out_specs=vmem,
        compiler_params=pltpu.CompilerParams(vmem_limit_bytes=16 * 1024 * 1024),
        cost_estimate=LIGHT,
        name="place_out",
    )(place, *pieces)


def branch_kernel(grouped_ref, out_ref, *refs):
    weight = out_ref[...]
    for row in range(grouped_ref.shape[0]):
        mine_ref, theirs_ref = refs[2 * row : 2 * row + 2]
        half_len = mine_ref.shape[0]
        mine_ref[...] = jnp.dot(grouped_ref[row, :half_len, :], weight, preferred_element_type=jnp.float32).astype(
            jnp.bfloat16
        )
        theirs_ref[...] = jnp.dot(grouped_ref[row, half_len:, :], weight, preferred_element_type=jnp.float32).astype(
            jnp.bfloat16
        )


def branch_rows_of(grouped, out_own):
    vmem = pl.BlockSpec(memory_space=pltpu.VMEM)
    rows, half_len, width = grouped.shape[0], grouped.shape[1] // 2, out_own.shape[1]
    flat = pl.pallas_call(
        branch_kernel,
        out_shape=(
            jax.ShapeDtypeStruct((half_len, width), jnp.bfloat16),
        ) * (2 * rows),
        in_specs=[vmem] * 2,
        out_specs=(vmem,) * (2 * rows),
        compiler_params=pltpu.CompilerParams(vmem_limit_bytes=32 * 1024 * 1024),
        cost_estimate=LIGHT,
        name="branch",
    )(grouped, out_own)
    return flat[0::2], flat[1::2]


def pick_kernel(place_ref, *refs):
    ins, outs = refs[:4], refs[4:]
    for step, out in enumerate(outs):
        behind = jnp.bitwise_and(place_ref[2] - jnp.bitwise_xor(place_ref[0], step), 3)
        for k, ref in enumerate(ins):

            @pl.when(behind == k)
            def _():
                out[...] = ref[...]


def pick_out(place, pieces):
    vmem = pl.BlockSpec(memory_space=pltpu.VMEM)
    return pl.pallas_call(
        pick_kernel,
        out_shape=(jax.ShapeDtypeStruct(pieces[0].shape, pieces[0].dtype),) * 4,
        in_specs=[pl.BlockSpec(memory_space=pltpu.SMEM)] + [vmem] * 4,
        out_specs=(vmem,) * 4,
        compiler_params=pltpu.CompilerParams(vmem_limit_bytes=16 * 1024 * 1024),
        cost_estimate=LIGHT,
        name="pick_out",
    )(place, *pieces)


def place_quarters_kernel(place_ref, own_ref, other_ref, out_ref):
    chips, rows = own_ref.shape[:2]
    for k in range(chips):
        for e, ref in enumerate((own_ref, other_ref)):
            core = jnp.bitwise_xor(place_ref[1], e)
            at = pl.multiple_of((core * chips + jnp.bitwise_xor(place_ref[0], k)) * rows, rows)
            out_ref[pl.ds(at, rows), :] = ref[k].astype(jnp.float32)


def place_quarters(place, own, other):
    vmem = pl.BlockSpec(memory_space=pltpu.VMEM)
    chips, rows, cols = own.shape
    return pl.pallas_call(
        place_quarters_kernel,
        out_shape=jax.ShapeDtypeStruct((2 * chips * rows, cols), jnp.float32),
        in_specs=[pl.BlockSpec(memory_space=pltpu.SMEM)] + [vmem] * 2,
        out_specs=vmem,
        compiler_params=pltpu.CompilerParams(vmem_limit_bytes=16 * 1024 * 1024),
        cost_estimate=LIGHT,
        name="place_quarters",
    )(place, own, other)


from jax.sharding import PartitionSpec as P

PLANE = ("narrow", "seq")
SWAP = [(0, 1), (1, 0)]


def seq_swap(array):
    return lax.ppermute(array, "seq", SWAP)


def x_swap(array):
    return lax.ppermute(array, "narrow", [(0, 1), (1, 0), (2, 3), (3, 2)])


def y_swap(array):
    return lax.ppermute(array, "narrow", [(0, 2), (2, 0), (1, 3), (3, 1)])


def diagonal_swap(array):
    return lax.ppermute(array, "narrow", [(i, i ^ 3) for i in range(4)])


def gather_plane(own):
    half = own.shape[0] // 2
    from_x = x_swap(own)
    from_y = y_swap(own)
    corner = jnp.concatenate([y_swap(from_x[:half]), x_swap(from_y[half:])], 0)
    return [(a, seq_swap(a)) for a in (own, from_x, from_y, corner)]


def after(array, *others):
    return lax.optimization_barrier((array, *others))[0] if others else array


class Steps:
    def __init__(self):
        self.ended = ()

    def hold(self, array):
        return after(array, *self.ended)

    def end(self, *arrays):
        self.ended = arrays


def half_rows(array, second):
    cut = array.shape[0] // 2
    return array[cut:] if second else array[:cut]


def whole_sum(mine, came, from_x, from_y):
    return mine.astype(jnp.float32) + came.astype(jnp.float32) + from_x.astype(jnp.float32) + from_y.astype(jnp.float32)


def wide_shift(array, by):
    count = lax.axis_size("wide")
    return lax.ppermute(array, "wide", [(i, (i + by) % count) for i in range(count)])


def wide_block(blocks, step):
    count = lax.axis_size("wide")
    at = (lax.axis_index("wide") - step) % count
    return lax.dynamic_index_in_dim(blocks, at, 0, keepdims=False)


def wide_stack(pieces):
    whole = jnp.zeros((len(pieces),) + pieces[0].shape, pieces[0].dtype)
    for step, piece in enumerate(pieces):
        whole = lax.dynamic_update_index_in_dim(whole, piece, (lax.axis_index("wide") - step) % len(pieces), 0)
    return whole


def gather_wide(piece):
    return lax.all_gather(piece, "wide", axis=0, tiled=True)


def scatter_wide(whole):
    return lax.psum_scatter(whole, "wide", scatter_dimension=0, tiled=True)


def exchange_plane(blocks):
    line = lax.axis_index("narrow")

    def block(k):
        return lax.dynamic_index_in_dim(blocks, line ^ k, 0, keepdims=False)

    return [block(0), x_swap(block(1)), y_swap(block(2)), diagonal_swap(block(3))]


def in_place(pieces):
    line = lax.axis_index("narrow")
    whole = jnp.zeros((4,) + pieces[0].shape, pieces[0].dtype)
    for k in range(4):
        whole = lax.dynamic_update_index_in_dim(whole, pieces[k], line ^ k, 0)
    return whole


def pad_heads(array, head_size):
    heads = array.shape[1] // head_size
    split = array.reshape(array.shape[0], heads, head_size)
    return jnp.pad(split, ((0, 0), (0, 0), (0, LANES - head_size))).reshape(array.shape[0], heads * LANES)


def times(left, right):
    return jnp.dot(left, right, preferred_element_type=jnp.float32)


def norm_scale(values):
    return lax.rsqrt(jnp.mean(values * values, axis=-1, keepdims=True) + 1e-06)


def norm_back(values, scale, gain, grad):
    lift = grad * gain
    along = jnp.mean(lift * values, axis=-1, keepdims=True)
    return scale * lift - values * (scale * scale * scale * along), jnp.sum(grad * values * scale, axis=0)


def on_device(
    inputs,
    doc_start,
    norm_gain,
    qkv_weight,
    logit_kernel,
    head_mix,
    group_gain,
    out_weight,
    feed_gain,
    gate_up,
    down_weight,
    cotangent,
):
    tokens_dev, width = inputs.shape
    head_count, taps_q, taps_k = logit_kernel.shape
    head_size = width // head_count
    group_cols = 2 * head_size
    cores = lax.axis_size(PLANE)
    wide = lax.axis_size("wide")
    line = lax.axis_index("narrow")
    part = lax.axis_index(PLANE)
    chunk = gate_up.shape[1] // (2 * wide * cores)
    scaling = head_size ** (-0.5)

    core = lax.axis_index("seq").astype(jnp.int32).reshape(1)
    place = jnp.stack([line, lax.axis_index("seq"), lax.axis_index("wide")]).astype(jnp.int32)

    joined_piece = jnp.concatenate(
        [
            lax.dynamic_slice_in_dim(qkv_weight, s * width + part * group_cols, group_cols, 1)
            for s in range(3)
        ]
        + [jnp.zeros((qkv_weight.shape[0], -3 * group_cols % LANES), qkv_weight.dtype)],
        1,
    )
    joined = gather_wide(joined_piece)
    inputs, doc_start, out_weight = lax.optimization_barrier((inputs, doc_start, out_weight, joined_piece))[:3]

    flow = Steps()
    hold = flow.hold
    feed_cols = wide * chunk
    first_pos = lax.axis_index(("narrow", "wide", "seq")) * tokens_dev

    out_rows = group_cols // 4
    ring = wide == 4

    inputs_f = inputs.astype(jnp.float32)
    scale_in = norm_scale(inputs_f)
    since = first_pos + jnp.arange(tokens_dev, dtype=jnp.int32) - doc_start
    high = since // 256
    lane = jnp.arange(LANES, dtype=jnp.int32)[None, :]
    extra = jnp.where(lane == 0, high[:, None], jnp.where(lane == 1, (since - 256 * high)[:, None], 0))
    normed = jnp.concatenate(
        [(inputs_f * scale_in * norm_gain).astype(jnp.bfloat16), extra.astype(jnp.bfloat16)], 1
    )
    out_pieces = [lax.dynamic_slice_in_dim(out_weight, (lax.axis_index("seq") * 4 + line) * out_rows, out_rows, 0)]

    def out_step():
        if ring:
            out_pieces.append(wide_shift(hold(out_pieces[-1]), 1))

    out_step()
    flow.end(normed, out_pieces[-1])

    normed_x, normed_y, normed_o = x_swap(hold(normed)), y_swap(hold(normed)), seq_swap(hold(normed))
    out_step()
    kernels = lax.dynamic_slice_in_dim(logit_kernel, 2 * part, 2, 0)
    mix = lax.dynamic_slice_in_dim(head_mix, 2 * part, 2, 0)
    taps_forward, taps_backward = tap_bands(hold(kernels), scaling)
    gain_pad = pad_heads(lax.dynamic_slice_in_dim(group_gain, part * group_cols, group_cols, 0)[None], head_size)
    gate_piece = jnp.concatenate(
        [
            lax.dynamic_slice_in_dim(hold(gate_up), (s * cores + part) * chunk, chunk, 1)
            for s in range(2 * wide)
        ],
        1,
    )
    down_piece = lax.dynamic_slice_in_dim(hold(down_weight), part * chunk, chunk, 0)
    down_piece = jnp.concatenate(
        [down_piece[:, at : at + feed_cols] for at in range(0, width, feed_cols)], 0
    )
    feed_piece = jnp.concatenate([gate_piece, down_piece], 1)
    flow.end(normed_x, normed_y, normed_o, taps_forward, feed_piece, out_pieces[-1])

    low, high = half_rows(normed_x, False), half_rows(normed_y, True)
    flow.end(low, high, *flow.ended)
    corner_low, corner_high = y_swap(hold(low)), x_swap(hold(high))
    cot_x, cot_y = x_swap(hold(cotangent)), y_swap(hold(cotangent))
    out_step()
    flow.end(corner_low, corner_high, out_pieces[-1])

    normed_c = jnp.concatenate([corner_low, corner_high], 0)
    normed_xo, normed_yo, normed_co = seq_swap(normed_x), seq_swap(normed_y), seq_swap(hold(normed_c))
    normed_rows = [(normed, normed_o), (normed_x, normed_xo), (normed_y, normed_yo), (normed_c, normed_co)]
    if ring:
        out_picked = pick_out(hold(place), out_pieces)
        flow.end(normed_co, normed_xo, normed_yo, joined, *out_picked)
    else:
        flow.end(normed_co, normed_xo, normed_yo, joined)

    feed_own = gather_wide(hold(feed_piece))
    if ring:
        out_picked = [hold(a) for a in out_picked]
        out_pieces = [
            out_picked[0], x_swap(out_picked[1]), y_swap(out_picked[2]), diagonal_swap(out_picked[3])
        ]
    projected, attended, grouped, weights, since_rows = attend_rows(
        hold(core), [a for k in normed_rows for a in k], mix, joined, taps_forward, gain_pad, taps_q,
        head_size,
    )
    flow.end(grouped, cot_x, cot_y, *out_pieces)
    if ring:
        out_own = place_out(hold(place), out_pieces)
    else:
        out_own = lax.dynamic_slice_in_dim(gather_wide(hold(out_weight)), part * group_cols, group_cols, 0)
        out_own = jnp.pad(
            out_own.reshape(2, head_size, width), ((0, 0), (0, LANES - head_size), (0, 0))
        ).reshape(2 * LANES, width)
    branch_mine, branch_theirs = branch_rows_of(grouped, out_own)
    flow.end(*branch_mine, *branch_theirs)
    came_3, came_1, came_2 = (seq_swap(hold(branch_theirs[k])) for k in (3, 1, 2))
    flow.end(came_3, came_1, came_2)
    low, high = sum_halves(branch_mine[3], hold(came_3))
    flow.end(low, high)
    to_y, to_x = x_swap(hold(low)), y_swap(hold(high))
    came_0, cot_o = seq_swap(hold(branch_theirs[0])), seq_swap(hold(cotangent))
    flow.end(came_0, to_x, to_y, cot_o)
    low_x = low_sum(branch_mine[1], came_1, hold(to_x), True)
    low_y = low_sum(branch_mine[2], came_2, hold(to_y), False)
    flow.end(low_x, low_y)
    cot_xo, cot_yo = seq_swap(hold(cot_x)), seq_swap(hold(cot_y))
    branch_x, branch_y = x_swap(hold(low_x)), y_swap(hold(low_y))
    cot_halves = half_rows(hold(cot_x), False), half_rows(hold(cot_y), True)
    flow.end(branch_x, branch_y, cot_xo, cot_yo, feed_own, *cot_halves)
    residual = inputs_f + whole_sum(branch_mine[0], hold(came_0), branch_x, branch_y)
    scale_mid = norm_scale(residual)
    normed_ffn = (residual * scale_mid * feed_gain).astype(jnp.bfloat16)
    flow.end(normed_ffn)

    ffn_x, ffn_y, ffn_o = x_swap(hold(normed_ffn)), y_swap(hold(normed_ffn)), seq_swap(hold(normed_ffn))
    flow.end(ffn_o)
    hidden_rows, gate_grads, feed_out = [None] * 4, [None] * 4, [None] * 4
    ffn_rows = [(normed_ffn, ffn_o), None, None, None]
    cotangent_rows = [(cotangent, cot_o), (cot_x, cot_xo), (cot_y, cot_yo), None]

    gate_own, down_own = split_feed(hold(feed_own), wide)

    def feed(k):
        hidden_rows[k], gate_grads[k], *feed_out[k] = feed_row(
            hold(ffn_rows[k][0]), ffn_rows[k][1], *cotangent_rows[k], gate_own, down_own
        )

    feed(0)
    flow.end(hidden_rows[0], ffn_x, ffn_y)
    ffn_xo, ffn_yo = seq_swap(hold(ffn_x)), seq_swap(hold(ffn_y))
    ffn_rows[1], ffn_rows[2] = (ffn_x, ffn_xo), (ffn_y, ffn_yo)
    flow.end(ffn_xo, ffn_yo)
    cot_low, cot_high = y_swap(hold(cot_halves[0])), x_swap(hold(cot_halves[1]))
    low, high = half_rows(hold(ffn_x), False), half_rows(hold(ffn_y), True)
    back_came = [None] * 4
    feed(1)
    flow.end(hidden_rows[1], cot_low, cot_high, low, high)
    cot_c = jnp.concatenate([cot_low, cot_high], 0)
    flow.end(low, high, cot_c)
    corner_low, corner_high = y_swap(hold(low)), x_swap(hold(high))
    cot_co = seq_swap(hold(cot_c))
    back_came[1] = seq_swap(hold(feed_out[1][3]))
    feed(2)
    flow.end(hidden_rows[2], corner_low, corner_high, cot_co, back_came[1])
    back_came[2] = seq_swap(hold(feed_out[2][3]))
    ffn_c = jnp.concatenate([corner_low, corner_high], 0)
    ffn_co = seq_swap(ffn_c)
    low_x = pair_sum(feed_out[1][2], hold(back_came[1]))
    low_y = pair_sum(feed_out[2][2], back_came[2])
    ffn_rows[3], cotangent_rows[3] = (ffn_c, ffn_co), (cot_c, cot_co)
    flow.end(ffn_co, low_x, low_y)
    back_x, back_y = x_swap(hold(low_x)), y_swap(hold(low_y))
    feed(3)
    flow.end(hidden_rows[3], back_x, back_y)
    back_came[3], back_came[0] = seq_swap(hold(feed_out[3][3])), seq_swap(hold(feed_out[0][3]))
    flow.end(back_came[3], back_came[0])
    low = pair_sum(feed_out[3][2], hold(back_came[3]))
    flow.end(low)
    back_d = diagonal_swap(hold(low))
    feed_grad_own = feed_grad(
        [hold(a) for k in ffn_rows for a in k], gate_grads, hidden_rows, [a for k in cotangent_rows for a in k], wide
    )
    flow.end(back_d, feed_grad_own)
    shard_feed = scatter_wide(hold(feed_grad_own))
    feed_came = [seq_swap(hold(feed_out[k][1])) for k in range(4)]
    grad_ffn = whole_sum(feed_out[0][2], back_came[0], back_x, back_y) + hold(back_d).astype(jnp.float32)
    norm_part, grad_feed = norm_back(residual, scale_mid, feed_gain, grad_ffn)
    grad_residual = norm_part + cotangent.astype(jnp.float32)
    grad_branch = grad_residual.astype(jnp.bfloat16)
    flow.end(grad_branch, *feed_came)

    gb_x, gb_y, gb_o = x_swap(hold(grad_branch)), y_swap(hold(grad_branch)), seq_swap(hold(grad_branch))
    low, high = sum_halves(feed_out[3][0], hold(feed_came[3]))
    flow.end(gb_o, low, high)
    branch_rows = [(grad_branch, gb_o), None, None, None]
    grad_joined, normed_mine, normed_theirs, smalls, tap_sums = ([None] * 4 for _ in range(5))

    def attend_back(k):
        grad_joined[k], normed_mine[k], normed_theirs[k], smalls[k], tap_sums[k] = attend_row_back(
            k, hold(core), *branch_rows[k], out_own, joined, (projected, attended, weights), since_rows, mix,
            taps_backward, gain_pad, taps_q, taps_k, head_size,
        )

    attend_back(0)
    flow.end(grad_joined[0], gb_x, gb_y)
    gb_xo, gb_yo = seq_swap(hold(gb_x)), seq_swap(hold(gb_y))
    branch_rows[1], branch_rows[2] = (gb_x, gb_xo), (gb_y, gb_yo)
    flow.end(gb_xo, gb_yo)
    corner_low, corner_high = y_swap(hold(half_rows(gb_x, False))), x_swap(hold(half_rows(gb_y, True)))
    to_y, to_x = x_swap(hold(low)), y_swap(hold(high))
    attend_back(1)
    flow.end(grad_joined[1], corner_low, corner_high, to_x, to_y)
    low_x = low_sum(feed_out[1][0], feed_came[1], hold(to_x), True)
    low_y = low_sum(feed_out[2][0], feed_came[2], hold(to_y), False)
    gb_c = jnp.concatenate([corner_low, corner_high], 0)
    flow.end(low_x, low_y, gb_c)
    gb_co = seq_swap(hold(gb_c))
    flow.end(low_x, low_y, gb_co)
    feed_main_x, feed_main_y = x_swap(hold(low_x)), y_swap(hold(low_y))
    branch_rows[3] = (gb_c, gb_co)
    normed_came = [None] * 4
    normed_came[1] = seq_swap(hold(normed_theirs[1]))
    attend_back(2)
    grad_out_own = small_weight_grad([grouped.reshape(-1, 2 * LANES)], [hold(a) for k in branch_rows for a in k], "out_grad")
    flow.end(grad_joined[2], normed_came[1], grad_out_own, feed_main_x, feed_main_y)
    normed_came[2] = seq_swap(hold(normed_theirs[2]))
    low_x = pair_sum(normed_mine[1], hold(normed_came[1]))
    grad_out_own = hold(grad_out_own).reshape(2, LANES, width)[:, :head_size].reshape(2 * head_size, width)
    flow.end(normed_came[2], low_x, grad_out_own)
    low_y = pair_sum(normed_mine[2], hold(normed_came[2]))
    flow.end(low_x, low_y)
    grad_x, grad_y = x_swap(hold(low_x)), y_swap(hold(low_y))
    out_terms = hold(grad_out_own)
    if ring:
        out_terms = in_place(exchange_plane(out_terms.reshape(4, out_rows, width)))
    attend_back(3)
    flow.end(grad_joined[3], grad_x, grad_y, out_terms)

    normed_came[3], normed_came[0] = seq_swap(hold(normed_theirs[3])), seq_swap(hold(normed_theirs[0]))
    flow.end(normed_came[3], normed_came[0])
    low = pair_sum(normed_mine[3], hold(normed_came[3]))
    flow.end(low)
    grad_d = diagonal_swap(hold(low))
    out_came = []
    if ring:
        out_came = [wide_shift(hold(wide_block(out_terms, -step)), step) for step in range(1, 4)]
    joined_grad_own = weight_grad(
        [hold(a) for k in normed_rows for a in k], grad_joined, 2 * LANES, "joined_grad"
    )
    flow.end(grad_d, joined_grad_own, *out_came)
    shard_joined = scatter_wide(hold(joined_grad_own))
    feed_x, feed_y, feed_o = x_swap(hold(shard_feed)), y_swap(hold(shard_feed)), seq_swap(hold(shard_feed))
    grad_normed = whole_sum(normed_mine[0], normed_came[0], grad_x, grad_y) + hold(grad_d).astype(jnp.float32)
    norm_part, grad_norm = norm_back(inputs_f, scale_in, norm_gain, grad_normed)
    grad_input = norm_part + grad_residual
    small = hold(smalls[0] + smalls[1] + smalls[2] + smalls[3])
    taps = jnp.sum(tap_sums[0] + tap_sums[1] + tap_sums[2] + tap_sums[3], axis=2) * scaling

    def placed(array, total):
        array = array.reshape(-1)
        return lax.dynamic_update_slice(jnp.zeros((total,), jnp.float32), array, (part * array.shape[0],))

    pieces = [
        grad_feed,
        placed(small[:2, :head_size], width),
        placed(hold(taps), head_count * taps_q * taps_k),
        placed(jnp.sum(small[2:6], axis=1), 2 * head_count),
    ]
    lengths = [a.shape[0] for a in pieces]
    fill = -(sum(lengths) + width) % (8 * LANES)
    packed = jnp.concatenate(pieces + [jnp.zeros((fill,), jnp.float32)]).reshape(-1, LANES)
    packed = jnp.concatenate([packed, grad_norm.reshape(-1, LANES)], 0)
    packed = packed + seq_swap(packed)
    if wide & (wide - 1):
        packed = lax.psum(packed, "wide")
    else:
        for hop in [1 << i for i in range(16) if 1 << i < wide]:
            packed = packed + lax.ppermute(packed, "wide", [(i, i ^ hop) for i in range(wide)])
    packed = packed + x_swap(packed)
    flow.end(packed, feed_x, feed_y, feed_o)
    shard_out = out_x = out_y = grad_out_own
    if ring:
        out_sum = wide_block(out_terms, 0).astype(jnp.float32) + sum(hold(a).astype(jnp.float32) for a in out_came)
        shard_out = out_sum.astype(jnp.bfloat16)
    packed = packed + y_swap(hold(packed))
    feed_low, feed_high = y_swap(hold(half_rows(feed_x, False))), x_swap(hold(half_rows(feed_y, True)))
    feed_xo, feed_yo = seq_swap(hold(feed_x)), seq_swap(hold(feed_y))
    block_out = (residual + whole_sum(feed_out[0][0], hold(feed_came[0]), feed_main_x, feed_main_y)).astype(jnp.bfloat16)
    flow.end(feed_low, feed_high, feed_xo, feed_yo, packed, shard_joined, block_out, shard_out)

    joined_x, joined_y, joined_o = x_swap(hold(shard_joined)), y_swap(hold(shard_joined)), seq_swap(hold(shard_joined))
    feed_c = jnp.concatenate([feed_low, feed_high], 0)
    feed_co = seq_swap(hold(feed_c))
    if ring:
        out_x, out_y = x_swap(hold(shard_out)), y_swap(hold(shard_out))
        grad_gate, grad_down = place_feed(
            place, [hold(shard_feed), feed_o, feed_x, feed_xo, feed_y, feed_yo, feed_c, feed_co], chunk
        )
    else:
        every = lax.all_gather(shard_feed, PLANE, axis=0)
        split = every[:, :, : 2 * feed_cols].reshape(cores, shard_feed.shape[0], 2 * wide, chunk)
        grad_gate = jnp.moveaxis(split, 0, 2).reshape(shard_feed.shape[0], -1).astype(jnp.float32)
        split = every[:, :, 2 * feed_cols :].reshape(cores, width // feed_cols, chunk, feed_cols)
        grad_down = jnp.swapaxes(split, 1, 2).reshape(cores * chunk, width).astype(jnp.float32)
        grad_out = scatter_wide(lax.all_gather(grad_out_own, PLANE, axis=0, tiled=True)).astype(jnp.float32)
    flow.end(joined_x, joined_y, joined_o, packed, grad_gate, out_x, out_y)
    joined_low, joined_high = y_swap(hold(half_rows(joined_x, False))), x_swap(hold(half_rows(joined_y, True)))
    if ring:
        out_c = y_swap(hold(out_x))
    joined_xo, joined_yo = seq_swap(hold(joined_x)), seq_swap(hold(joined_y))
    joined_rows = [(shard_joined, joined_o), (joined_x, joined_xo), (joined_y, joined_yo)]
    whole_columns = 2 * group_cols % LANES == 0
    if whole_columns:
        grad_qkv = place_columns(hold(place), [a for k in joined_rows for a in k], 3, group_cols, 4)
        flow.end(joined_low, joined_high, grad_qkv, *([out_c] if ring else []))
    else:
        flow.end(joined_low, joined_high)
    joined_c = jnp.concatenate([joined_low, joined_high], 0)
    joined_co = seq_swap(hold(joined_c))
    if ring:
        quarters = jnp.stack([shard_out, out_x, out_y, out_c])
        grad_out = place_quarters(place, quarters, seq_swap(hold(quarters)))
    if whole_columns:
        grad_qkv = add_columns(place, joined_c, joined_co, grad_qkv, 3, group_cols, 4, 3)
    else:
        every = lax.all_gather(shard_joined, PLANE, axis=0)[:, :, : 3 * group_cols]
        split = every.reshape(cores, shard_joined.shape[0], 3, group_cols)
        grad_qkv = jnp.moveaxis(split, 0, 2).reshape(shard_joined.shape[0], -1).astype(jnp.float32)
    packed = packed.reshape(-1)
    grad_norm = packed[-width:]
    parts = []
    for length in lengths:
        parts.append(packed[:length])
        packed = packed[length:]
    grad_feed, grad_group, grad_kernel, grad_mix = parts
    return (
        block_out,
        grad_input,
        grad_norm,
        grad_qkv,
        grad_kernel.reshape(head_count, taps_q, taps_k),
        grad_mix.reshape(head_count, 2),
        grad_group,
        grad_out,
        grad_feed,
        grad_gate,
        grad_down,
    )


def solution(mesh):
    tokens = P(("narrow", "wide", "seq"), None)
    rows = P("wide", None)
    return jax.shard_map(
        on_device,
        mesh=mesh,
        in_specs=(tokens, P(("narrow", "wide", "seq")), P(), rows, P(), P(), P(), rows, P(), rows, rows, tokens),
        out_specs=(tokens, tokens, P(), rows, P(), P(), P(), rows, P(), rows, rows),
        check_vma=False,
    )
```

```python
import functools
import jax
import jax.numpy as jnp
from jax import lax
from jax.experimental import pallas as pl
from jax.experimental.pallas import tpu as pltpu

LANES = 128
EDGE = 64
TOP = 16
ROOM = 60 * 1024 * 1024
LIGHT = pl.CostEstimate(flops=1_000_000, bytes_accessed=1_000_000, transcendentals=0)


def cost(micros):
    return pl.CostEstimate(flops=0, bytes_accessed=3_600_000 * micros, transcendentals=0)


def taps_kernel(taps_q, taps_k, scaling, kernel_ref, forward_ref, backward_ref):
    half = (taps_k - 1) // 2
    row = lax.broadcasted_iota(jnp.int32, (2 * LANES, LANES), 0)
    col = lax.broadcasted_iota(jnp.int32, (2 * LANES, LANES), 1)
    forth = col - row + EDGE + half
    back = row - col - EDGE + half
    for head in range(2):
        for tap in range(taps_q):
            ahead = jnp.zeros((2 * LANES, LANES), jnp.float32)
            behind = jnp.zeros((2 * LANES, LANES), jnp.float32)
            for tap_k in range(taps_k):
                value = kernel_ref[head, tap, tap_k]
                ahead = jnp.where(forth == tap_k, value, ahead)
                behind = jnp.where(back == tap_k, value, behind)
            ahead = ahead * scaling
            high = ahead.astype(jnp.bfloat16)
            cols = slice(tap * LANES, (tap + 1) * LANES)
            forward_ref[head, : 2 * LANES, cols] = high
            forward_ref[head, 2 * LANES : 4 * LANES, cols] = high
            forward_ref[head, 4 * LANES :, cols] = (ahead - high.astype(jnp.float32)).astype(jnp.bfloat16)
            backward_ref[head, tap * 2 * LANES : (tap + 1) * 2 * LANES, :] = behind.astype(jnp.bfloat16)


def tap_bands(kernels, scaling):
    heads, taps_q, taps_k = kernels.shape
    return pl.pallas_call(
        functools.partial(taps_kernel, taps_q, taps_k, scaling),
        out_shape=(
            jax.ShapeDtypeStruct((heads, 6 * LANES, taps_q * LANES), jnp.bfloat16),
            jax.ShapeDtypeStruct((heads, taps_q * 2 * LANES, LANES), jnp.bfloat16),
        ),
        in_specs=[pl.BlockSpec(memory_space=pltpu.SMEM)],
        out_specs=(pl.BlockSpec(memory_space=pltpu.VMEM),) * 2,
        compiler_params=pltpu.CompilerParams(vmem_limit_bytes=32 * 1024 * 1024),
        cost_estimate=LIGHT,
        name="tap_bands",
    )(kernels)


def columns_pair(own_ref, other_ref, core, chunk, s):
    own = own_ref[:, s * chunk : (s + 1) * chunk].astype(jnp.float32)
    other = other_ref[:, s * chunk : (s + 1) * chunk].astype(jnp.float32)
    return jnp.concatenate([jnp.where(core == 0, own, other), jnp.where(core == 0, other, own)], 1)


def place_columns_kernel(sections, chunk, chips, where_ref, *refs):
    ins, out_ref = refs[:-1], refs[-1]
    line, core = where_ref[0], where_ref[1]
    width = 2 * chunk
    for k in range(len(ins) // 2):
        for s in range(sections):
            at = pl.multiple_of(s * chips * width + (line ^ k) * width, LANES)
            out_ref[:, pl.ds(at, width)] = columns_pair(ins[2 * k], ins[2 * k + 1], core, chunk, s)


def place_columns(place, pieces, sections, chunk, chips):
    rows, cols = pieces[0].shape
    cols_out = 2 * sections * chunk * chips
    steps = 4 if rows % 64 == 0 else 1
    spec = pl.BlockSpec((rows // steps, cols), lambda s, place: (s, 0))
    return pl.pallas_call(
        functools.partial(place_columns_kernel, sections, chunk, chips),
        out_shape=jax.ShapeDtypeStruct((rows, cols_out), jnp.float32),
        grid_spec=pltpu.PrefetchScalarGridSpec(
            num_scalar_prefetch=1,
            grid=(steps,),
            in_specs=[spec] * len(pieces),
            out_specs=pl.BlockSpec((rows // steps, cols_out), lambda s, place: (s, 0)),
        ),
        compiler_params=pltpu.CompilerParams(vmem_limit_bytes=24 * 1024 * 1024),
        cost_estimate=cost(5),
        name="place_columns",
    )(place, *pieces)


def add_columns_kernel(sections, chunk, chips, chip, place_ref, own_ref, other_ref, base_ref, out_ref, blocks, sems):
    del base_ref
    line, core = place_ref[0], place_ref[1]
    width = 2 * chunk
    copies = []
    for s in range(sections):
        blocks[s] = columns_pair(own_ref, other_ref, core, chunk, s)
        at = pl.multiple_of(s * chips * width + (line ^ chip) * width, LANES)
        copy = pltpu.make_async_copy(blocks.at[s], out_ref.at[:, pl.ds(at, width)], sems.at[s])
        copy.start()
        copies.append(copy)
    for copy in copies:
        copy.wait()


def add_columns(place, own, other, base, sections, chunk, chips, chip):
    vmem = pl.BlockSpec(memory_space=pltpu.VMEM)
    anywhere = pl.BlockSpec(memory_space=pl.ANY)
    return pl.pallas_call(
        functools.partial(add_columns_kernel, sections, chunk, chips, chip),
        out_shape=jax.ShapeDtypeStruct(base.shape, base.dtype),
        in_specs=[pl.BlockSpec(memory_space=pltpu.SMEM), vmem, vmem, anywhere],
        out_specs=anywhere,
        scratch_shapes=[
            pltpu.VMEM((sections, own.shape[0], 2 * chunk), jnp.float32), pltpu.SemaphoreType.DMA((sections,)),
        ],
        input_output_aliases={3: 0},
        compiler_params=pltpu.CompilerParams(vmem_limit_bytes=12 * 1024 * 1024),
        cost_estimate=cost(2),
        name="add_columns",
    )(place, own, other, base)


def place_feed_kernel(sections, chunk, pieces, where_ref, *refs):
    ins, gate_ref, down_ref = refs[:pieces], refs[pieces], refs[pieces + 1]
    line, core = where_ref[0], where_ref[1]
    width = 2 * chunk
    chips = pieces // 2
    gate_cols = sections * chunk
    for k in range(chips):
        own = ins[2 * k][...].astype(jnp.float32)
        other = ins[2 * k + 1][...].astype(jnp.float32)
        first = jnp.where(core == 0, own, other)
        second = jnp.where(core == 0, other, own)
        for s in range(sections):
            both = jnp.concatenate([first[:, s * chunk : (s + 1) * chunk], second[:, s * chunk : (s + 1) * chunk]], 1)
            at = pl.multiple_of(s * chips * width + (line ^ k) * width, LANES)
            gate_ref[:, pl.ds(at, width)] = both
        at = pl.multiple_of((line ^ k) * width, width)
        down_ref[pl.ds(at, chunk), :] = first[:, gate_cols:]
        down_ref[pl.ds(at + chunk, chunk), :] = second[:, gate_cols:]


def place_feed(place, pieces, chunk):
    rows, cols = pieces[0].shape
    blocks = rows // chunk
    sections = (cols // chunk) * 2 // 3
    hidden = cols - sections * chunk
    spec = pl.BlockSpec((chunk, cols), lambda s, place: (s, 0))
    gate_cols = sections * chunk * len(pieces)
    return pl.pallas_call(
        functools.partial(place_feed_kernel, sections, chunk, len(pieces)),
        out_shape=(
            jax.ShapeDtypeStruct((rows, gate_cols), jnp.float32),
            jax.ShapeDtypeStruct((chunk * len(pieces), hidden * blocks), jnp.float32),
        ),
        grid_spec=pltpu.PrefetchScalarGridSpec(
            num_scalar_prefetch=1,
            grid=(blocks,),
            in_specs=[spec] * len(pieces),
            out_specs=(
                pl.BlockSpec((chunk, gate_cols), lambda s, place: (s, 0)),
                pl.BlockSpec((chunk * len(pieces), hidden), lambda s, place: (0, s)),
            ),
        ),
        compiler_params=pltpu.CompilerParams(vmem_limit_bytes=ROOM),
        cost_estimate=cost(11),
        name="place_feed",
    )(place, *pieces)


def masked_scores(q_blk, keys, since, first_row):
    scores = lax.dot_general(q_blk, keys, (((1,), (1,)), ((), ())), preferred_element_type=jnp.float32)
    rows = first_row + lax.broadcasted_iota(jnp.int32, scores.shape, 0)
    back = rows + EDGE - lax.broadcasted_iota(jnp.int32, scores.shape, 1)
    limit = jnp.concatenate([since] * (scores.shape[1] // LANES), 1)
    return jnp.where((back >= 0) & (back <= limit), scores, 0.0)


def head_places(heads, head_size):
    return [((head * head_size) // LANES, (head * head_size) % LANES) for head in range(heads)]


def split_heads(joined, heads, head_size):
    real = lax.broadcasted_iota(jnp.int32, (joined.shape[0], LANES), 1) < head_size
    out = []
    for tile, shift in head_places(heads, head_size):
        if shift:
            both = joined[:, tile * LANES : (tile + 2) * LANES]
            piece = pltpu.roll(both, 2 * LANES - shift, 1)[:, :LANES]
        else:
            piece = joined[:, tile * LANES : (tile + 1) * LANES]
        out.append(jnp.where(real, piece, 0.0))
    return out


def join_heads(pieces, head_size):
    count = pieces[0].shape[0]
    nothing = jnp.zeros((count, LANES), jnp.float32)
    tiles = [nothing] * 5
    for piece, (tile, shift) in zip(pieces, head_places(len(pieces), head_size)):
        if shift:
            both = pltpu.roll(jnp.concatenate([piece, nothing], 1), shift, 1)
            tiles[tile] = tiles[tile] + both[:, :LANES]
            tiles[tile + 1] = tiles[tile + 1] + both[:, LANES:]
        else:
            tiles[tile] = tiles[tile] + piece
    return jnp.concatenate(tiles, 1)


def forward_kernel(taps_q, head_size, rows, core_ref, mix_ref, joined_ref, taps_ref, gain_ref, *refs):
    halves, outs = refs[: 2 * rows], refs[2 * rows : 2 * rows + 5]
    (
        pieces, proj, att, grouped, maps, since_all, keys_pad, s_high, s_low, spread, grouped_row, in_sems, out_sems
    ) = refs[2 * rows + 5 :]
    width = joined_ref.shape[0]
    arrivals = [pltpu.make_async_copy(ref, pieces.at[i], in_sems.at[i]) for i, ref in enumerate(halves)]
    for arrival in arrivals:
        arrival.start()
    seq_len = proj.shape[1]
    half_len = seq_len // 2
    blocks = seq_len // LANES
    core = core_ref[0]
    keys_pad[...] = jnp.zeros_like(keys_pad)
    s_high[...] = jnp.zeros_like(s_high)
    s_low[...] = jnp.zeros_like(s_low)

    def project(step, carry):
        pltpu.make_async_copy(halves[0], pieces.at[step], in_sems.at[step]).wait()
        row, part = lax.div(step, 2), lax.rem(step, 2)
        at = pl.multiple_of(jnp.bitwise_xor(core, part) * half_len, half_len)
        joined = jnp.dot(pieces[step, :, :width], joined_ref[...], preferred_element_type=jnp.float32)
        extra = pieces[step, :, width:].astype(jnp.float32)
        since = (extra[:, 0:1] * 256.0 + extra[:, 1:2]).astype(jnp.int32)
        since_all[row, pl.ds(at, half_len), :] = jnp.broadcast_to(since, (half_len, LANES))
        for head, piece in enumerate(split_heads(joined, 6, head_size)):
            proj[row, pl.ds(at, half_len), head * LANES : (head + 1) * LANES] = piece.astype(jnp.bfloat16)
        return carry

    lax.fori_loop(0, 2 * rows, project, 0)
    real = lax.broadcasted_iota(jnp.int32, (LANES, LANES), 1) < head_size

    def mix_row(row):
        for qi in range(blocks):
            first = qi * LANES
            width = (qi + 1) * LANES
            low = maps[row, 0, first : first + LANES, :width]
            upp = maps[row, 1, first : first + LANES, :width]
            for head in range(2):
                mixed = (mix_ref[head, 0] * low + mix_ref[head, 1] * upp).astype(jnp.bfloat16)
                cols = slice(head * LANES, (head + 1) * LANES)
                attended = jnp.dot(
                    mixed, proj[row, :width, (4 + head) * LANES : (5 + head) * LANES],
                    preferred_element_type=jnp.float32,
                )
                att[row, first : first + LANES, cols] = attended
                normal, _ = normalize(attended, real, head_size)
                grouped_row[first : first + LANES, cols] = (normal * gain_ref[:, cols]).astype(jnp.bfloat16)
        for part in range(2):
            at = pl.multiple_of(jnp.bitwise_xor(core, part) * half_len, half_len)
            grouped[row, part * half_len : (part + 1) * half_len, :] = grouped_row[pl.ds(at, half_len), :]
        for copy in copies_out(row):
            copy.start()

    def copies_out(row):
        return [
            pltpu.make_async_copy(here.at[row], there.at[row], out_sems.at[kind, row])
            for kind, (here, there) in enumerate(zip((proj, att, grouped, maps, since_all), outs))
        ]

    def one_head(step, carry):
        row, head = lax.div(step, 2), lax.rem(step, 2)
        proj_ref, since_ref, weights_ref = proj.at[row], since_all.at[row], maps.at[row]
        lane = pl.multiple_of(head * LANES, LANES)
        lane_k = pl.multiple_of((head + 2) * LANES, LANES)
        keys_pad[EDGE : EDGE + seq_len, :] = proj_ref[:, pl.ds(lane_k, LANES)]
        for qi in range(blocks):
            first = qi * LANES
            width = (qi + 2) * LANES
            scores = masked_scores(
                proj_ref[first : first + LANES, pl.ds(lane, LANES)],
                keys_pad[:width, :],
                since_ref[first : first + LANES, :],
                first,
            )
            high = scores.astype(jnp.bfloat16)
            s_high[TOP + first : TOP + first + LANES, :width] = high
            s_low[TOP + first : TOP + first + LANES, :width] = (scores - high.astype(jnp.float32)).astype(jnp.bfloat16)
        for m in range(blocks):
            first = m * LANES
            count = seq_len - first
            high = s_high[first:, first : first + 2 * LANES]
            left = jnp.concatenate([high, s_low[first:, first : first + 2 * LANES], high], 1)
            spread[first:, :] = jnp.dot(left, taps_ref[head], preferred_element_type=jnp.float32)
            since = since_ref[first:, :]
            logits = spread[TOP + first :, :LANES]
            for tap in range(1, taps_q):
                moved = spread[TOP + first - tap : TOP + seq_len - tap, tap * LANES : (tap + 1) * LANES]
                logits = logits + jnp.where(since >= tap, moved, 0.0)
            weights_ref[head, first:, first : first + LANES] = logits
        for qi in range(blocks):
            first = qi * LANES
            width = (qi + 1) * LANES
            logits = weights_ref[head, first : first + LANES, :width]
            rows = first + lax.broadcasted_iota(jnp.int32, logits.shape, 0)
            back = rows - lax.broadcasted_iota(jnp.int32, logits.shape, 1)
            limit = jnp.concatenate([since_ref[first : first + LANES, :]] * (qi + 1), 1)
            logits = jnp.where((back >= 0) & (back <= limit), logits, -1e30)
            raised = jnp.exp(logits - jnp.max(logits, axis=1, keepdims=True))
            weights_ref[head, first : first + LANES, :width] = raised / jnp.sum(raised, axis=1, keepdims=True)

        @pl.when(head == 1)
        def _():
            mix_row(row)

        return carry

    lax.fori_loop(0, 2 * rows, one_head, 0)
    for row in range(rows):
        for copy in copies_out(row):
            copy.wait()


def normalize(att, real, head_size):
    mean = jnp.sum(att, axis=1, keepdims=True) * (1.0 / head_size)
    centered = jnp.where(real, att - mean, 0.0)
    spread = jnp.sum(centered * centered, axis=1, keepdims=True) * (1.0 / head_size)
    scale = lax.rsqrt(spread + 1e-05)
    return centered * scale, scale


def attend_rows(core, halves, mix, joined, taps_forward, gain_pad, taps_q, head_size):
    rows, seq_len = len(halves) // 2, 2 * halves[0].shape[0]
    full = seq_len + 2 * EDGE
    vmem = pl.BlockSpec(memory_space=pltpu.VMEM)
    smem = pl.BlockSpec(memory_space=pltpu.SMEM)
    anywhere = pl.BlockSpec(memory_space=pl.ANY)
    shapes = (
        ((rows, seq_len, 6 * LANES), jnp.bfloat16),
        ((rows, seq_len, 2 * LANES), jnp.float32),
        ((rows, seq_len, 2 * LANES), jnp.bfloat16),
        ((rows, 2, seq_len, seq_len), jnp.float32),
        ((rows, seq_len, LANES), jnp.int32),
    )
    return pl.pallas_call(
        functools.partial(forward_kernel, taps_q, head_size, rows),
        out_shape=tuple(jax.ShapeDtypeStruct(*a) for a in shapes),
        in_specs=[smem, smem] + [vmem] * 3 + [anywhere] * len(halves),
        out_specs=(anywhere,) * 5,
        scratch_shapes=[pltpu.VMEM((len(halves),) + halves[0].shape, jnp.bfloat16)]
        + [pltpu.VMEM(*a) for a in shapes]
        + [
            pltpu.VMEM((full, LANES), jnp.bfloat16),
            pltpu.VMEM((TOP + seq_len, full), jnp.bfloat16),
            pltpu.VMEM((TOP + seq_len, full), jnp.bfloat16),
            pltpu.VMEM((TOP + seq_len, taps_q * LANES), jnp.float32),
            pltpu.VMEM((seq_len, 2 * LANES), jnp.bfloat16),
            pltpu.SemaphoreType.DMA((len(halves),)),
            pltpu.SemaphoreType.DMA((5, rows)),
        ],
        compiler_params=pltpu.CompilerParams(vmem_limit_bytes=52 * 1024 * 1024),
        cost_estimate=LIGHT,
        name="attend_rows",
    )(core, mix, joined, taps_forward, gain_pad, *halves)


def backward_kernel(
    taps_q, taps_k, head_size, scaling, row, core_ref, mix_ref, own_ref, other_ref, out_weight_ref, joined_ref,
    taps_ref, gain_ref, proj_all, since_all, att_all, weights_all,
    joined_grad_ref, mine_ref, theirs_ref, small_ref, tap_ref,
    keys_pad, grad_att, conv_grad, shifted, s_low, s_grad, since_pad, grad_ref, out_ref,
    proj_ref, since_ref, att_ref, weights_ref, sems,
):
    arrivals = [
        pltpu.make_async_copy(source.at[row], here, sems.at[i])
        for i, (source, here) in enumerate(
            ((since_all, since_ref), (att_all, att_ref), (proj_all, proj_ref), (weights_all, weights_ref))
        )
    ]
    for arrival in arrivals:
        arrival.start()
    seq_len = proj_ref.shape[0]
    half_len = seq_len // 2
    own_at = pl.multiple_of(core_ref[0] * half_len, half_len)
    other_at = pl.multiple_of((1 - core_ref[0]) * half_len, half_len)
    for ref, at in ((own_ref, own_at), (other_ref, other_at)):
        grad_ref[pl.ds(at, half_len), :] = lax.dot_general(
            ref[...], out_weight_ref[...], (((1,), (1,)), ((), ())), preferred_element_type=jnp.float32
        )
    blocks = seq_len // LANES
    half = (taps_k - 1) // 2
    full = seq_len + 2 * EDGE
    keys_pad[...] = jnp.zeros_like(keys_pad)
    s_low[...] = jnp.zeros_like(s_low)
    s_grad[...] = jnp.zeros_like(s_grad)
    shifted[...] = jnp.zeros_like(shifted)
    conv_grad[...] = jnp.zeros_like(conv_grad)
    for arrival in arrivals:
        arrival.wait()
    since_pad[:seq_len, :] = since_ref[...]
    since_pad[seq_len:, :] = jnp.zeros((8, LANES), jnp.int32)
    small_ref[...] = jnp.zeros_like(small_ref)

    real = lax.broadcasted_iota(jnp.int32, (LANES, LANES), 1) < head_size
    for head in range(2):
        cols = slice(head * LANES, (head + 1) * LANES)
        group_sum = jnp.zeros((1, LANES), jnp.float32)
        for qi in range(blocks):
            rows = slice(qi * LANES, (qi + 1) * LANES)
            normal, scale = normalize(att_ref[rows, cols], real, head_size)
            grad = grad_ref[rows, cols]
            group_sum = group_sum + jnp.sum(grad * normal, axis=0, keepdims=True)
            lift = grad * gain_ref[:, cols]
            mean = jnp.sum(lift, axis=1, keepdims=True) * (1.0 / head_size)
            along = jnp.sum(lift * normal, axis=1, keepdims=True) * (1.0 / head_size)
            grad_att[rows, cols] = jnp.where(real, scale * (lift - mean - normal * along), 0.0).astype(jnp.bfloat16)
        small_ref[head : head + 1, :] = group_sum

    sums = [[jnp.zeros((1, LANES), jnp.float32) for _ in range(2)] for _ in range(2)]
    grad_v = [[], []]
    for qi in range(blocks):
        first = qi * LANES
        width = (qi + 1) * LANES
        rows = slice(first, first + LANES)
        maps = [weights_ref[k, rows, :width] for k in range(2)]
        grad_mixed = []
        for head in range(2):
            cols = slice(head * LANES, (head + 1) * LANES)
            values = proj_ref[:width, (4 + head) * LANES : (5 + head) * LANES]
            gm = lax.dot_general(
                grad_att[rows, cols], values, (((1,), (1,)), ((), ())), preferred_element_type=jnp.float32
            )
            grad_mixed.append(gm)
        for head in range(2):
            for k in range(2):
                part = jnp.sum(grad_mixed[head] * maps[k], axis=0, keepdims=True)
                for b in range(qi + 1):
                    sums[head][k] = sums[head][k] + part[:, b * LANES : (b + 1) * LANES]
        for k in range(2):
            grad_w = mix_ref[0, k] * grad_mixed[0] + mix_ref[1, k] * grad_mixed[1]
            inner = jnp.sum(grad_w * maps[k], axis=1, keepdims=True)
            conv_grad[k, rows, :width] = maps[k] * (grad_w - inner)
    for head in range(2):
        for k in range(2):
            small_ref[2 + 2 * head + k : 3 + 2 * head + k, :] = sums[head][k]
        cols = slice(head * LANES, (head + 1) * LANES)
        for kb in range(blocks):
            first = kb * LANES
            mixed = (
                mix_ref[head, 0] * weights_ref[0, first:, first : first + LANES]
                + mix_ref[head, 1] * weights_ref[1, first:, first : first + LANES]
            ).astype(jnp.bfloat16)
            out_ref[first : first + LANES, (4 + head) * LANES : (5 + head) * LANES] = lax.dot_general(
                mixed, grad_att[first:, cols], (((0,), (0,)), ((), ())), preferred_element_type=jnp.float32
            )

    def one_head(head, carry):
        lane = pl.multiple_of(head * LANES, LANES)
        lane_k = pl.multiple_of((head + 2) * LANES, LANES)
        keys_pad[EDGE : EDGE + seq_len, :] = proj_ref[:, pl.ds(lane_k, LANES)]
        for qi in range(blocks):
            first = qi * LANES
            width = (qi + 2) * LANES
            scores = masked_scores(
                proj_ref[first : first + LANES, pl.ds(lane, LANES)],
                keys_pad[:width, :],
                since_ref[first : first + LANES, :],
                first,
            )
            s_low[TOP + first : TOP + first + LANES, :width] = scores.astype(jnp.bfloat16)
            reach = min(width, seq_len)
            for tap in range(taps_q):
                moved = conv_grad[head, first + tap : first + tap + LANES, :reach]
                if tap > 0:
                    limit = since_pad[first + tap : first + tap + LANES, :]
                    limit = jnp.concatenate([limit] * (reach // LANES), 1)
                    moved = jnp.where(limit >= tap, moved, 0.0)
                shifted[tap, TOP + first : TOP + first + LANES, LANES : LANES + reach] = moved.astype(jnp.bfloat16)
        for m in range(blocks + 1):
            first = max(m - 1, 0) * LANES
            left = jnp.concatenate(
                [shifted[tap, TOP + first :, m * LANES : (m + 2) * LANES] for tap in range(taps_q)], 1
            )
            grad = jnp.dot(left, taps_ref[head], preferred_element_type=jnp.float32)
            rows = first + lax.broadcasted_iota(jnp.int32, grad.shape, 0)
            back = rows + EDGE - m * LANES - lax.broadcasted_iota(jnp.int32, grad.shape, 1)
            keep = (back >= 0) & (back <= since_ref[first:, :])
            s_grad[first:, m * LANES : (m + 1) * LANES] = jnp.where(keep, grad, 0.0).astype(jnp.bfloat16)
        total = jnp.zeros((2 * LANES, taps_q * LANES), jnp.float32)
        for m in range(blocks):
            first = m * LANES
            right = jnp.concatenate(
                [shifted[tap, first:, (m + 1) * LANES : (m + 2) * LANES] for tap in range(taps_q)], 1
            )
            total = total + lax.dot_general(
                s_low[first:, first : first + 2 * LANES], right, (((0,), (0,)), ((), ())),
                preferred_element_type=jnp.float32,
            )
        ridge = lax.broadcasted_iota(jnp.int32, (2 * LANES, LANES), 1) - lax.broadcasted_iota(
            jnp.int32, (2 * LANES, LANES), 0
        )
        for tap_k in range(taps_k):
            on = ridge == tap_k - EDGE - half
            for tap in range(taps_q):
                line = jnp.where(on, total[:, tap * LANES : (tap + 1) * LANES], 0.0)
                tap_ref[head, tap * taps_k + tap_k : tap * taps_k + tap_k + 1, :] = jnp.sum(line, axis=0, keepdims=True)
        for qi in range(blocks):
            first = qi * LANES
            width = (qi + 2) * LANES
            grad_q = jnp.dot(
                s_grad[first : first + LANES, :width], keys_pad[:width, :], preferred_element_type=jnp.float32
            )
            out_ref[first : first + LANES, pl.ds(lane, LANES)] = grad_q * scaling
        for kb in range(blocks):
            first = kb * LANES
            grad_k = lax.dot_general(
                s_grad[first:, first + EDGE : first + EDGE + LANES],
                proj_ref[first:, pl.ds(lane, LANES)],
                (((0,), (0,)), ((), ())),
                preferred_element_type=jnp.float32,
            )
            out_ref[first : first + LANES, pl.ds(lane_k, LANES)] = grad_k * scaling
        return carry

    lax.fori_loop(0, 2, one_head, 0)
    for at, first in ((own_at, 0), (other_at, half_len)):
        pieces = [out_ref[pl.ds(at, half_len), head * LANES : (head + 1) * LANES] for head in range(6)]
        joined = join_heads(pieces, head_size).astype(jnp.bfloat16)
        joined_grad_ref[first : first + half_len, :] = joined
        grad_in = lax.dot_general(
            joined, joined_ref[...], (((1,), (1,)), ((), ())), preferred_element_type=jnp.float32
        )
        if first:
            theirs_ref[...] = grad_in.astype(jnp.bfloat16)
        else:
            mine_ref[...] = grad_in.astype(jnp.bfloat16)


def attend_row_back(
    row, core, own, other, out_weight, joined, saved, since, mix, taps_backward, gain_pad, taps_q, taps_k, head_size
):
    projected, att, weights = saved
    seq_len = projected.shape[1]
    width = own.shape[1]
    full = seq_len + 2 * EDGE
    vmem = pl.BlockSpec(memory_space=pltpu.VMEM)
    smem = pl.BlockSpec(memory_space=pltpu.SMEM)
    anywhere = pl.BlockSpec(memory_space=pl.ANY)
    return pl.pallas_call(
        functools.partial(backward_kernel, taps_q, taps_k, head_size, head_size ** (-0.5), row),
        out_shape=(
            jax.ShapeDtypeStruct((seq_len, joined.shape[1]), jnp.bfloat16),
            jax.ShapeDtypeStruct((seq_len // 2, width), jnp.bfloat16),
            jax.ShapeDtypeStruct((seq_len // 2, width), jnp.bfloat16),
            jax.ShapeDtypeStruct((8, LANES), jnp.float32),
            jax.ShapeDtypeStruct((2, taps_q * taps_k, LANES), jnp.float32),
        ),
        in_specs=[smem, smem] + [vmem] * 6 + [anywhere] * 4,
        out_specs=(vmem,) * 5,
        scratch_shapes=[
            pltpu.VMEM((full, LANES), jnp.bfloat16),
            pltpu.VMEM((seq_len, 2 * LANES), jnp.bfloat16),
            pltpu.VMEM((2, seq_len + 8, seq_len), jnp.float32),
            pltpu.VMEM((taps_q, TOP + seq_len, seq_len + 2 * LANES), jnp.bfloat16),
            pltpu.VMEM((TOP + seq_len, full), jnp.bfloat16),
            pltpu.VMEM((seq_len, full), jnp.bfloat16),
            pltpu.VMEM((seq_len + 8, LANES), jnp.int32),
            pltpu.VMEM((seq_len, 2 * LANES), jnp.float32),
            pltpu.VMEM((seq_len, 6 * LANES), jnp.float32),
            pltpu.VMEM(projected.shape[1:], jnp.bfloat16),
            pltpu.VMEM(since.shape[1:], jnp.int32),
            pltpu.VMEM(att.shape[1:], jnp.float32),
            pltpu.VMEM(weights.shape[1:], jnp.float32),
            pltpu.SemaphoreType.DMA((4,)),
        ],
        compiler_params=pltpu.CompilerParams(vmem_limit_bytes=48 * 1024 * 1024),
        cost_estimate=cost(14),
        name="attend_row_back",
    )(core, mix, own, other, out_weight, joined, taps_backward, gain_pad, projected, since, att, weights)


def split_kernel(wide, feed_ref, gate_ref, down_ref):
    cols = down_ref.shape[0]
    chunk = cols // wide
    blocks = down_ref.shape[1] // cols
    gate_ref[...] = feed_ref[:, : 2 * cols]
    for z in range(wide):
        for b in range(blocks):
            first = (z * blocks + b) * chunk
            down_ref[z * chunk : (z + 1) * chunk, b * cols : (b + 1) * cols] = feed_ref[first : first + chunk, 2 * cols :]


def split_feed(feed, wide):
    vmem = pl.BlockSpec(memory_space=pltpu.VMEM)
    rows, cols = feed.shape[0], feed.shape[1] // 3
    return pl.pallas_call(
        functools.partial(split_kernel, wide),
        out_shape=(
            jax.ShapeDtypeStruct((rows, 2 * cols), jnp.bfloat16), jax.ShapeDtypeStruct((cols, rows), jnp.bfloat16),
        ),
        in_specs=[vmem],
        out_specs=(vmem,) * 2,
        compiler_params=pltpu.CompilerParams(vmem_limit_bytes=24 * 1024 * 1024),
        cost_estimate=LIGHT,
        name="split_feed",
    )(feed)


def feed_kernel(own_ref, other_ref, cot_own_ref, cot_other_ref, gate_ref, down_ref,
                hidden_ref, grads_ref, ffn_mine_ref, ffn_theirs_ref, back_mine_ref, back_theirs_ref):
    half_len = own_ref.shape[0]
    cols = down_ref.shape[0]
    for first, ref, cot_ref in ((0, own_ref, cot_own_ref), (half_len, other_ref, cot_other_ref)):
        rows = slice(first, first + half_len)
        both = jnp.dot(ref[...], gate_ref[...], preferred_element_type=jnp.float32)
        gating, upward = both[:, :cols], both[:, cols:]
        grad = lax.dot_general(
            cot_ref[...], down_ref[...], (((1,), (1,)), ((), ())), preferred_element_type=jnp.float32
        )
        sig = 1.0 / (1.0 + jnp.exp(-gating))
        silu = gating * sig
        hidden = (silu * upward).astype(jnp.bfloat16)
        hidden_ref[rows, :] = hidden
        grads_ref[rows, :cols] = (grad * upward * (sig * (1.0 + gating * (1.0 - sig)))).astype(jnp.bfloat16)
        grads_ref[rows, cols:] = (grad * silu).astype(jnp.bfloat16)
        back = lax.dot_general(
            grads_ref[rows, :], gate_ref[...], (((1,), (1,)), ((), ())), preferred_element_type=jnp.float32
        )
        ffn = jnp.dot(hidden, down_ref[...], preferred_element_type=jnp.float32)
        if first:
            back_theirs_ref[...] = back.astype(jnp.bfloat16)
            ffn_theirs_ref[...] = ffn.astype(jnp.bfloat16)
        else:
            back_mine_ref[...] = back.astype(jnp.bfloat16)
            ffn_mine_ref[...] = ffn.astype(jnp.bfloat16)


def feed_row(own, other, cot_own, cot_other, gate, down):
    half_len, width = own.shape
    cols = down.shape[0]
    vmem = pl.BlockSpec(memory_space=pltpu.VMEM)
    return pl.pallas_call(
        feed_kernel,
        out_shape=(
            jax.ShapeDtypeStruct((2 * half_len, cols), jnp.bfloat16),
            jax.ShapeDtypeStruct((2 * half_len, 2 * cols), jnp.bfloat16),
            jax.ShapeDtypeStruct((half_len, width), jnp.bfloat16),
            jax.ShapeDtypeStruct((half_len, width), jnp.bfloat16),
            jax.ShapeDtypeStruct((half_len, width), jnp.bfloat16),
            jax.ShapeDtypeStruct((half_len, width), jnp.bfloat16),
        ),
        in_specs=[vmem] * 6,
        out_specs=(vmem,) * 6,
        compiler_params=pltpu.CompilerParams(vmem_limit_bytes=48 * 1024 * 1024),
        cost_estimate=cost(8),
        name="feed_row",
    )(own, other, cot_own, cot_other, gate, down)


def feed_grad_kernel(counts, *refs):
    lefts, grads, hiddens, cots = (
        jnp.concatenate([ref[...] for ref in refs[sum(counts[:i]) : sum(counts[: i + 1])]], 0) for i in range(4)
    )
    out_ref = refs[-1]
    chunk = hiddens.shape[1]
    cols = out_ref.shape[1] - grads.shape[1]
    out_ref[:, : grads.shape[1]] = lax.dot_general(
        lefts, grads, (((0,), (0,)), ((), ())), preferred_element_type=jnp.float32
    ).astype(jnp.bfloat16)
    down = lax.dot_general(hiddens, cots, (((0,), (0,)), ((), ())), preferred_element_type=jnp.float32)
    for b in range(down.shape[1] // cols):
        out_ref[b * chunk : (b + 1) * chunk, grads.shape[1] :] = down[:, b * cols : (b + 1) * cols].astype(jnp.bfloat16)


def feed_grad(lefts, grads, hiddens, cots, wide):
    width = lefts[0].shape[1]
    cols = hiddens[0].shape[1]
    block, chunk = width // wide, cols // wide
    if block % LANES or chunk % LANES:
        gate = lax.dot_general(
            jnp.concatenate(lefts, 0), jnp.concatenate(grads, 0), (((0,), (0,)), ((), ())),
            preferred_element_type=jnp.float32,
        )
        down = lax.dot_general(
            jnp.concatenate(hiddens, 0), jnp.concatenate(cots, 0), (((0,), (0,)), ((), ())),
            preferred_element_type=jnp.float32,
        )
        down = jnp.swapaxes(down.reshape(wide, chunk, width // cols, cols), 1, 2).reshape(width, cols)
        return jnp.concatenate([gate, down], 1).astype(jnp.bfloat16)
    count = sum(a.shape[0] for a in lefts)
    cols_out = grads[0].shape[1] + cols
    return pl.pallas_call(
        functools.partial(feed_grad_kernel, (len(lefts), len(grads), len(hiddens), len(cots))),
        out_shape=jax.ShapeDtypeStruct((width, cols_out), jnp.bfloat16),
        grid=(wide,),
        in_specs=[pl.BlockSpec((a.shape[0], block), lambda s: (0, s)) for a in lefts]
        + [pl.BlockSpec(a.shape, lambda s: (0, 0)) for a in grads]
        + [pl.BlockSpec((a.shape[0], chunk), lambda s: (0, s)) for a in hiddens]
        + [pl.BlockSpec(a.shape, lambda s: (0, 0)) for a in cots],
        out_specs=pl.BlockSpec((block, cols_out), lambda s: (s, 0)),
        compiler_params=pltpu.CompilerParams(vmem_limit_bytes=ROOM),
        cost_estimate=cost(17),
        name="feed_grad",
    )(*lefts, *grads, *hiddens, *cots)


def weight_kernel(lefts, *refs):
    left = jnp.concatenate([ref[...] for ref in refs[:lefts]], 0)
    right = jnp.concatenate([ref[...] for ref in refs[lefts:-1]], 0)
    refs[-1][...] = lax.dot_general(
        left, right, (((0,), (0,)), ((), ())), preferred_element_type=jnp.float32
    ).astype(jnp.bfloat16)


def small_weight_grad(lefts, rights, name):
    vmem = pl.BlockSpec(memory_space=pltpu.VMEM)
    return pl.pallas_call(
        functools.partial(weight_kernel, len(lefts)),
        out_shape=jax.ShapeDtypeStruct((lefts[0].shape[1], rights[0].shape[1]), jnp.bfloat16),
        in_specs=[vmem] * (len(lefts) + len(rights)),
        out_specs=vmem,
        compiler_params=pltpu.CompilerParams(vmem_limit_bytes=32 * 1024 * 1024),
        cost_estimate=cost(3),
        name=name,
    )(*lefts, *rights)


def weight_grad(lefts, rights, block, name):
    rows_out, cols_out = lefts[0].shape[1] // block * block, rights[0].shape[1]
    count = sum(a.shape[0] for a in lefts)
    return pl.pallas_call(
        functools.partial(weight_kernel, len(lefts)),
        out_shape=jax.ShapeDtypeStruct((rows_out, cols_out), jnp.bfloat16),
        grid=(rows_out // block,),
        in_specs=[pl.BlockSpec((a.shape[0], block), lambda s: (0, s)) for a in lefts]
        + [pl.BlockSpec(a.shape, lambda s: (0, 0)) for a in rights],
        out_specs=pl.BlockSpec((block, cols_out), lambda s: (s, 0)),
        compiler_params=pltpu.CompilerParams(vmem_limit_bytes=ROOM),
        cost_estimate=cost(8),
        name=name,
    )(*lefts, *rights)


def halves_kernel(mine_ref, came_ref, low_ref, high_ref):
    cut = low_ref.shape[0]
    low_ref[...] = (mine_ref[:cut, :].astype(jnp.float32) + came_ref[:cut, :].astype(jnp.float32)).astype(jnp.bfloat16)
    high_ref[...] = (mine_ref[cut:, :].astype(jnp.float32) + came_ref[cut:, :].astype(jnp.float32)).astype(jnp.bfloat16)


def sum_halves(mine, came):
    half = jax.ShapeDtypeStruct((mine.shape[0] // 2, mine.shape[1]), jnp.bfloat16)
    vmem = pl.BlockSpec(memory_space=pltpu.VMEM)
    return pl.pallas_call(
        halves_kernel, out_shape=(half, half), in_specs=[vmem] * 2, out_specs=(vmem,) * 2,
        compiler_params=pltpu.CompilerParams(vmem_limit_bytes=4 * 1024 * 1024), cost_estimate=LIGHT, name="sum_halves",
    )(mine, came)


def sum_kernel(second, mine_ref, came_ref, extra_ref, out_ref):
    cut = extra_ref.shape[0]
    rows, rest = (slice(cut, 2 * cut), slice(0, cut)) if second else (slice(0, cut), slice(cut, 2 * cut))
    total = mine_ref[rows, :].astype(jnp.float32) + came_ref[rows, :].astype(jnp.float32) + extra_ref[...].astype(jnp.float32)
    out_ref[rows, :] = total.astype(jnp.bfloat16)
    out_ref[rest, :] = (mine_ref[rest, :].astype(jnp.float32) + came_ref[rest, :].astype(jnp.float32)).astype(jnp.bfloat16)


def low_sum(mine, came, extra, second):
    vmem = pl.BlockSpec(memory_space=pltpu.VMEM)
    return pl.pallas_call(
        functools.partial(sum_kernel, second), out_shape=jax.ShapeDtypeStruct(mine.shape, jnp.bfloat16),
        in_specs=[vmem] * 3, out_specs=vmem,
        compiler_params=pltpu.CompilerParams(vmem_limit_bytes=4 * 1024 * 1024), cost_estimate=LIGHT, name="low_sum",
    )(mine, came, extra)


def pair_kernel(mine_ref, came_ref, out_ref):
    out_ref[...] = (mine_ref[...].astype(jnp.float32) + came_ref[...].astype(jnp.float32)).astype(jnp.bfloat16)


def pair_sum(mine, came):
    vmem = pl.BlockSpec(memory_space=pltpu.VMEM)
    return pl.pallas_call(
        pair_kernel, out_shape=jax.ShapeDtypeStruct(mine.shape, jnp.bfloat16), in_specs=[vmem] * 2, out_specs=vmem,
        compiler_params=pltpu.CompilerParams(vmem_limit_bytes=4 * 1024 * 1024), cost_estimate=LIGHT, name="pair_sum",
    )(mine, came)


def place_out_kernel(place_ref, *refs):
    out_ref = refs[-1]
    out_ref[...] = jnp.zeros_like(out_ref)
    for step, ref in enumerate(refs[:-1]):
        chunk = jnp.bitwise_xor(place_ref[0], step)
        rows = ref.shape[0]
        at = pl.multiple_of(lax.div(chunk, 2) * LANES + lax.rem(chunk, 2) * rows, 16)
        out_ref[pl.ds(at, rows), :] = ref[...]


def place_out(place, pieces):
    vmem = pl.BlockSpec(memory_space=pltpu.VMEM)
    return pl.pallas_call(
        place_out_kernel,
        out_shape=jax.ShapeDtypeStruct((2 * LANES, pieces[0].shape[1]), jnp.bfloat16),
        in_specs=[pl.BlockSpec(memory_space=pltpu.SMEM)] + [vmem] * len(pieces),
        out_specs=vmem,
        compiler_params=pltpu.CompilerParams(vmem_limit_bytes=16 * 1024 * 1024),
        cost_estimate=LIGHT,
        name="place_out",
    )(place, *pieces)


def branch_kernel(grouped_ref, out_ref, *refs):
    weight = out_ref[...]
    for row in range(grouped_ref.shape[0]):
        mine_ref, theirs_ref = refs[2 * row : 2 * row + 2]
        half_len = mine_ref.shape[0]
        mine_ref[...] = jnp.dot(grouped_ref[row, :half_len, :], weight, preferred_element_type=jnp.float32).astype(
            jnp.bfloat16
        )
        theirs_ref[...] = jnp.dot(grouped_ref[row, half_len:, :], weight, preferred_element_type=jnp.float32).astype(
            jnp.bfloat16
        )


def branch_rows_of(grouped, out_own):
    vmem = pl.BlockSpec(memory_space=pltpu.VMEM)
    rows, half_len, width = grouped.shape[0], grouped.shape[1] // 2, out_own.shape[1]
    flat = pl.pallas_call(
        branch_kernel,
        out_shape=(
            jax.ShapeDtypeStruct((half_len, width), jnp.bfloat16),
        ) * (2 * rows),
        in_specs=[vmem] * 2,
        out_specs=(vmem,) * (2 * rows),
        compiler_params=pltpu.CompilerParams(vmem_limit_bytes=32 * 1024 * 1024),
        cost_estimate=LIGHT,
        name="branch",
    )(grouped, out_own)
    return flat[0::2], flat[1::2]


def pick_kernel(place_ref, *refs):
    ins, outs = refs[:4], refs[4:]
    for step, out in enumerate(outs):
        behind = jnp.bitwise_and(place_ref[2] - jnp.bitwise_xor(place_ref[0], step), 3)
        for k, ref in enumerate(ins):

            @pl.when(behind == k)
            def _():
                out[...] = ref[...]


def pick_out(place, pieces):
    vmem = pl.BlockSpec(memory_space=pltpu.VMEM)
    return pl.pallas_call(
        pick_kernel,
        out_shape=(jax.ShapeDtypeStruct(pieces[0].shape, pieces[0].dtype),) * 4,
        in_specs=[pl.BlockSpec(memory_space=pltpu.SMEM)] + [vmem] * 4,
        out_specs=(vmem,) * 4,
        compiler_params=pltpu.CompilerParams(vmem_limit_bytes=16 * 1024 * 1024),
        cost_estimate=LIGHT,
        name="pick_out",
    )(place, *pieces)


def place_quarters_kernel(place_ref, own_ref, other_ref, out_ref):
    chips, rows = own_ref.shape[:2]
    for k in range(chips):
        for e, ref in enumerate((own_ref, other_ref)):
            core = jnp.bitwise_xor(place_ref[1], e)
            at = pl.multiple_of((core * chips + jnp.bitwise_xor(place_ref[0], k)) * rows, rows)
            out_ref[pl.ds(at, rows), :] = ref[k].astype(jnp.float32)


def place_quarters(place, own, other):
    vmem = pl.BlockSpec(memory_space=pltpu.VMEM)
    chips, rows, cols = own.shape
    return pl.pallas_call(
        place_quarters_kernel,
        out_shape=jax.ShapeDtypeStruct((2 * chips * rows, cols), jnp.float32),
        in_specs=[pl.BlockSpec(memory_space=pltpu.SMEM)] + [vmem] * 2,
        out_specs=vmem,
        compiler_params=pltpu.CompilerParams(vmem_limit_bytes=16 * 1024 * 1024),
        cost_estimate=LIGHT,
        name="place_quarters",
    )(place, own, other)


from jax.sharding import PartitionSpec as P

PLANE = ("narrow", "seq")
SWAP = [(0, 1), (1, 0)]


def seq_swap(array):
    return lax.ppermute(array, "seq", SWAP)


def x_swap(array):
    return lax.ppermute(array, "narrow", [(0, 1), (1, 0), (2, 3), (3, 2)])


def y_swap(array):
    return lax.ppermute(array, "narrow", [(0, 2), (2, 0), (1, 3), (3, 1)])


def diagonal_swap(array):
    return lax.ppermute(array, "narrow", [(i, i ^ 3) for i in range(4)])


def gather_plane(own):
    half = own.shape[0] // 2
    from_x = x_swap(own)
    from_y = y_swap(own)
    corner = jnp.concatenate([y_swap(from_x[:half]), x_swap(from_y[half:])], 0)
    return [(a, seq_swap(a)) for a in (own, from_x, from_y, corner)]


def after(array, *others):
    return lax.optimization_barrier((array, *others))[0] if others else array


class Steps:
    def __init__(self):
        self.ended = ()

    def hold(self, array):
        return after(array, *self.ended)

    def end(self, *arrays):
        self.ended = arrays


def half_rows(array, second):
    cut = array.shape[0] // 2
    return array[cut:] if second else array[:cut]


def whole_sum(mine, came, from_x, from_y):
    return mine.astype(jnp.float32) + came.astype(jnp.float32) + from_x.astype(jnp.float32) + from_y.astype(jnp.float32)


def wide_shift(array, by):
    count = lax.axis_size("wide")
    return lax.ppermute(array, "wide", [(i, (i + by) % count) for i in range(count)])


def wide_block(blocks, step):
    count = lax.axis_size("wide")
    at = (lax.axis_index("wide") - step) % count
    return lax.dynamic_index_in_dim(blocks, at, 0, keepdims=False)


def wide_stack(pieces):
    whole = jnp.zeros((len(pieces),) + pieces[0].shape, pieces[0].dtype)
    for step, piece in enumerate(pieces):
        whole = lax.dynamic_update_index_in_dim(whole, piece, (lax.axis_index("wide") - step) % len(pieces), 0)
    return whole


def gather_wide(piece):
    return lax.all_gather(piece, "wide", axis=0, tiled=True)


def scatter_wide(whole):
    return lax.psum_scatter(whole, "wide", scatter_dimension=0, tiled=True)


def exchange_plane(blocks):
    line = lax.axis_index("narrow")

    def block(k):
        return lax.dynamic_index_in_dim(blocks, line ^ k, 0, keepdims=False)

    return [block(0), x_swap(block(1)), y_swap(block(2)), diagonal_swap(block(3))]


def in_place(pieces):
    line = lax.axis_index("narrow")
    whole = jnp.zeros((4,) + pieces[0].shape, pieces[0].dtype)
    for k in range(4):
        whole = lax.dynamic_update_index_in_dim(whole, pieces[k], line ^ k, 0)
    return whole


def pad_heads(array, head_size):
    heads = array.shape[1] // head_size
    split = array.reshape(array.shape[0], heads, head_size)
    return jnp.pad(split, ((0, 0), (0, 0), (0, LANES - head_size))).reshape(array.shape[0], heads * LANES)


def times(left, right):
    return jnp.dot(left, right, preferred_element_type=jnp.float32)


def norm_scale(values):
    return lax.rsqrt(jnp.mean(values * values, axis=-1, keepdims=True) + 1e-06)


def norm_back(values, scale, gain, grad):
    lift = grad * gain
    along = jnp.mean(lift * values, axis=-1, keepdims=True)
    return scale * lift - values * (scale * scale * scale * along), jnp.sum(grad * values * scale, axis=0)


def on_device(
    inputs,
    doc_start,
    norm_gain,
    qkv_weight,
    logit_kernel,
    head_mix,
    group_gain,
    out_weight,
    feed_gain,
    gate_up,
    down_weight,
    cotangent,
):
    tokens_dev, width = inputs.shape
    head_count, taps_q, taps_k = logit_kernel.shape
    head_size = width // head_count
    group_cols = 2 * head_size
    cores = lax.axis_size(PLANE)
    wide = lax.axis_size("wide")
    line = lax.axis_index("narrow")
    part = lax.axis_index(PLANE)
    chunk = gate_up.shape[1] // (2 * wide * cores)
    scaling = head_size ** (-0.5)

    core = lax.axis_index("seq").astype(jnp.int32).reshape(1)
    place = jnp.stack([line, lax.axis_index("seq"), lax.axis_index("wide")]).astype(jnp.int32)

    joined_piece = jnp.concatenate(
        [
            lax.dynamic_slice_in_dim(qkv_weight, s * width + part * group_cols, group_cols, 1)
            for s in range(3)
        ]
        + [jnp.zeros((qkv_weight.shape[0], -3 * group_cols % LANES), qkv_weight.dtype)],
        1,
    )
    joined = gather_wide(joined_piece)
    inputs, doc_start, out_weight = lax.optimization_barrier((inputs, doc_start, out_weight, joined_piece))[:3]

    flow = Steps()
    hold = flow.hold
    feed_cols = wide * chunk
    first_pos = lax.axis_index(("narrow", "wide", "seq")) * tokens_dev

    out_rows = group_cols // 4
    ring = wide == 4

    inputs_f = inputs.astype(jnp.float32)
    scale_in = norm_scale(inputs_f)
    since = first_pos + jnp.arange(tokens_dev, dtype=jnp.int32) - doc_start
    high = since // 256
    lane = jnp.arange(LANES, dtype=jnp.int32)[None, :]
    extra = jnp.where(lane == 0, high[:, None], jnp.where(lane == 1, (since - 256 * high)[:, None], 0))
    normed = jnp.concatenate(
        [(inputs_f * scale_in * norm_gain).astype(jnp.bfloat16), extra.astype(jnp.bfloat16)], 1
    )
    out_pieces = [lax.dynamic_slice_in_dim(out_weight, (lax.axis_index("seq") * 4 + line) * out_rows, out_rows, 0)]

    def out_step():
        if ring:
            out_pieces.append(wide_shift(hold(out_pieces[-1]), 1))

    out_step()
    flow.end(normed, out_pieces[-1])

    normed_x, normed_y, normed_o = x_swap(hold(normed)), y_swap(hold(normed)), seq_swap(hold(normed))
    out_step()
    kernels = lax.dynamic_slice_in_dim(logit_kernel, 2 * part, 2, 0)
    mix = lax.dynamic_slice_in_dim(head_mix, 2 * part, 2, 0)
    taps_forward, taps_backward = tap_bands(hold(kernels), scaling)
    gain_pad = pad_heads(lax.dynamic_slice_in_dim(group_gain, part * group_cols, group_cols, 0)[None], head_size)
    gate_piece = jnp.concatenate(
        [
            lax.dynamic_slice_in_dim(hold(gate_up), (s * cores + part) * chunk, chunk, 1)
            for s in range(2 * wide)
        ],
        1,
    )
    down_piece = lax.dynamic_slice_in_dim(hold(down_weight), part * chunk, chunk, 0)
    down_piece = jnp.concatenate(
        [down_piece[:, at : at + feed_cols] for at in range(0, width, feed_cols)], 0
    )
    feed_piece = jnp.concatenate([gate_piece, down_piece], 1)
    flow.end(normed_x, normed_y, normed_o, taps_forward, feed_piece, out_pieces[-1])

    low, high = half_rows(normed_x, False), half_rows(normed_y, True)
    flow.end(low, high, *flow.ended)
    corner_low, corner_high = y_swap(hold(low)), x_swap(hold(high))
    cot_x, cot_y = x_swap(hold(cotangent)), y_swap(hold(cotangent))
    out_step()
    flow.end(corner_low, corner_high, out_pieces[-1])

    normed_c = jnp.concatenate([corner_low, corner_high], 0)
    normed_xo, normed_yo, normed_co = seq_swap(normed_x), seq_swap(normed_y), seq_swap(hold(normed_c))
    normed_rows = [(normed, normed_o), (normed_x, normed_xo), (normed_y, normed_yo), (normed_c, normed_co)]
    if ring:
        out_picked = pick_out(hold(place), out_pieces)
        flow.end(normed_co, normed_xo, normed_yo, joined, *out_picked)
    else:
        flow.end(normed_co, normed_xo, normed_yo, joined)

    feed_own = gather_wide(hold(feed_piece))
    if ring:
        out_picked = [hold(a) for a in out_picked]
        out_pieces = [
            out_picked[0], x_swap(out_picked[1]), y_swap(out_picked[2]), diagonal_swap(out_picked[3])
        ]
    projected, attended, grouped, weights, since_rows = attend_rows(
        hold(core), [a for k in normed_rows for a in k], mix, joined, taps_forward, gain_pad, taps_q,
        head_size,
    )
    flow.end(grouped, cot_x, cot_y, *out_pieces)
    if ring:
        out_own = place_out(hold(place), out_pieces)
    else:
        out_own = lax.dynamic_slice_in_dim(gather_wide(hold(out_weight)), part * group_cols, group_cols, 0)
        out_own = jnp.pad(
            out_own.reshape(2, head_size, width), ((0, 0), (0, LANES - head_size), (0, 0))
        ).reshape(2 * LANES, width)
    branch_mine, branch_theirs = branch_rows_of(grouped, out_own)
    flow.end(*branch_mine, *branch_theirs)
    came_3, came_1, came_2 = (seq_swap(hold(branch_theirs[k])) for k in (3, 1, 2))
    flow.end(came_3, came_1, came_2)
    low, high = sum_halves(branch_mine[3], hold(came_3))
    flow.end(low, high)
    to_y, to_x = x_swap(hold(low)), y_swap(hold(high))
    came_0, cot_o = seq_swap(hold(branch_theirs[0])), seq_swap(hold(cotangent))
    flow.end(came_0, to_x, to_y, cot_o)
    low_x = low_sum(branch_mine[1], came_1, hold(to_x), True)
    low_y = low_sum(branch_mine[2], came_2, hold(to_y), False)
    flow.end(low_x, low_y)
    cot_xo, cot_yo = seq_swap(hold(cot_x)), seq_swap(hold(cot_y))
    branch_x, branch_y = x_swap(hold(low_x)), y_swap(hold(low_y))
    cot_halves = half_rows(hold(cot_x), False), half_rows(hold(cot_y), True)
    flow.end(branch_x, branch_y, cot_xo, cot_yo, feed_own, *cot_halves)
    residual = inputs_f + whole_sum(branch_mine[0], came_0, branch_x, branch_y)
    scale_mid = norm_scale(residual)
    normed_ffn = (residual * scale_mid * feed_gain).astype(jnp.bfloat16)
    flow.end(normed_ffn, *flow.ended)

    ffn_x, ffn_y, ffn_o = x_swap(hold(normed_ffn)), y_swap(hold(normed_ffn)), seq_swap(hold(normed_ffn))
    flow.end(ffn_o)
    hidden_rows, gate_grads, feed_out = [None] * 4, [None] * 4, [None] * 4
    ffn_rows = [(normed_ffn, ffn_o), None, None, None]
    cotangent_rows = [(cotangent, cot_o), (cot_x, cot_xo), (cot_y, cot_yo), None]

    gate_own, down_own = split_feed(hold(feed_own), wide)

    def feed(k):
        hidden_rows[k], gate_grads[k], *feed_out[k] = feed_row(
            hold(ffn_rows[k][0]), ffn_rows[k][1], *cotangent_rows[k], gate_own, down_own
        )

    feed(0)
    flow.end(hidden_rows[0], ffn_x, ffn_y)
    ffn_xo, ffn_yo = seq_swap(hold(ffn_x)), seq_swap(hold(ffn_y))
    ffn_rows[1], ffn_rows[2] = (ffn_x, ffn_xo), (ffn_y, ffn_yo)
    flow.end(ffn_xo, ffn_yo)
    cot_low, cot_high = y_swap(hold(cot_halves[0])), x_swap(hold(cot_halves[1]))
    low, high = half_rows(hold(ffn_x), False), half_rows(hold(ffn_y), True)
    back_came = [None] * 4
    feed(1)
    flow.end(hidden_rows[1], cot_low, cot_high, low, high)
    cot_c = jnp.concatenate([cot_low, cot_high], 0)
    flow.end(low, high, cot_c)
    corner_low, corner_high = y_swap(hold(low)), x_swap(hold(high))
    cot_co = seq_swap(hold(cot_c))
    back_came[1] = seq_swap(hold(feed_out[1][3]))
    feed(2)
    flow.end(hidden_rows[2], corner_low, corner_high, cot_co, back_came[1])
    back_came[2] = seq_swap(hold(feed_out[2][3]))
    ffn_c = jnp.concatenate([corner_low, corner_high], 0)
    ffn_co = seq_swap(ffn_c)
    low_x = pair_sum(feed_out[1][2], hold(back_came[1]))
    low_y = pair_sum(feed_out[2][2], back_came[2])
    ffn_rows[3], cotangent_rows[3] = (ffn_c, ffn_co), (cot_c, cot_co)
    flow.end(ffn_co, low_x, low_y)
    back_x, back_y = x_swap(hold(low_x)), y_swap(hold(low_y))
    feed(3)
    flow.end(hidden_rows[3], back_x, back_y)
    back_came[3], back_came[0] = seq_swap(hold(feed_out[3][3])), seq_swap(hold(feed_out[0][3]))
    flow.end(back_came[3], back_came[0])
    low = pair_sum(feed_out[3][2], hold(back_came[3]))
    flow.end(low)
    back_d = diagonal_swap(hold(low))
    feed_grad_own = feed_grad(
        [hold(a) for k in ffn_rows for a in k], gate_grads, hidden_rows, [a for k in cotangent_rows for a in k], wide
    )
    flow.end(back_d, feed_grad_own)
    shard_feed = scatter_wide(hold(feed_grad_own))
    feed_came = [seq_swap(hold(feed_out[k][1])) for k in range(4)]
    grad_ffn = whole_sum(feed_out[0][2], back_came[0], back_x, back_y) + hold(back_d).astype(jnp.float32)
    norm_part, grad_feed = norm_back(residual, scale_mid, feed_gain, grad_ffn)
    grad_residual = norm_part + cotangent.astype(jnp.float32)
    grad_branch = grad_residual.astype(jnp.bfloat16)
    flow.end(grad_branch, *feed_came)

    gb_x, gb_y, gb_o = x_swap(hold(grad_branch)), y_swap(hold(grad_branch)), seq_swap(hold(grad_branch))
    low, high = sum_halves(feed_out[3][0], hold(feed_came[3]))
    flow.end(gb_o, low, high)
    branch_rows = [(grad_branch, gb_o), None, None, None]
    grad_joined, normed_mine, normed_theirs, smalls, tap_sums = ([None] * 4 for _ in range(5))

    def attend_back(k):
        grad_joined[k], normed_mine[k], normed_theirs[k], smalls[k], tap_sums[k] = attend_row_back(
            k, hold(core), *branch_rows[k], out_own, joined, (projected, attended, weights), since_rows, mix,
            taps_backward, gain_pad, taps_q, taps_k, head_size,
        )

    attend_back(0)
    flow.end(grad_joined[0], gb_x, gb_y)
    gb_xo, gb_yo = seq_swap(hold(gb_x)), seq_swap(hold(gb_y))
    branch_rows[1], branch_rows[2] = (gb_x, gb_xo), (gb_y, gb_yo)
    flow.end(gb_xo, gb_yo)
    corner_low, corner_high = y_swap(hold(half_rows(gb_x, False))), x_swap(hold(half_rows(gb_y, True)))
    to_y, to_x = x_swap(hold(low)), y_swap(hold(high))
    attend_back(1)
    flow.end(grad_joined[1], corner_low, corner_high, to_x, to_y)
    low_x = low_sum(feed_out[1][0], feed_came[1], hold(to_x), True)
    low_y = low_sum(feed_out[2][0], feed_came[2], hold(to_y), False)
    gb_c = jnp.concatenate([corner_low, corner_high], 0)
    flow.end(low_x, low_y, gb_c)
    gb_co = seq_swap(hold(gb_c))
    flow.end(low_x, low_y, gb_co)
    feed_main_x, feed_main_y = x_swap(hold(low_x)), y_swap(hold(low_y))
    branch_rows[3] = (gb_c, gb_co)
    normed_came = [None] * 4
    normed_came[1] = seq_swap(hold(normed_theirs[1]))
    attend_back(2)
    grad_out_own = small_weight_grad([grouped.reshape(-1, 2 * LANES)], [hold(a) for k in branch_rows for a in k], "out_grad")
    flow.end(grad_joined[2], normed_came[1], grad_out_own, feed_main_x, feed_main_y)
    normed_came[2] = seq_swap(hold(normed_theirs[2]))
    low_x = pair_sum(normed_mine[1], hold(normed_came[1]))
    grad_out_own = hold(grad_out_own).reshape(2, LANES, width)[:, :head_size].reshape(2 * head_size, width)
    flow.end(normed_came[2], low_x, grad_out_own)
    low_y = pair_sum(normed_mine[2], hold(normed_came[2]))
    flow.end(low_x, low_y)
    grad_x, grad_y = x_swap(hold(low_x)), y_swap(hold(low_y))
    out_terms = hold(grad_out_own)
    if ring:
        out_terms = in_place(exchange_plane(out_terms.reshape(4, out_rows, width)))
    attend_back(3)
    flow.end(grad_joined[3], grad_x, grad_y, out_terms)

    normed_came[3], normed_came[0] = seq_swap(hold(normed_theirs[3])), seq_swap(hold(normed_theirs[0]))
    flow.end(normed_came[3], normed_came[0])
    low = pair_sum(normed_mine[3], hold(normed_came[3]))
    flow.end(low)
    grad_d = diagonal_swap(hold(low))
    out_came = []
    if ring:
        out_came = [wide_shift(hold(wide_block(out_terms, -step)), step) for step in range(1, 4)]
    joined_grad_own = weight_grad(
        [hold(a) for k in normed_rows for a in k], grad_joined, 2 * LANES, "joined_grad"
    )
    flow.end(grad_d, joined_grad_own, *out_came)
    shard_joined = scatter_wide(hold(joined_grad_own))
    feed_x, feed_y, feed_o = x_swap(hold(shard_feed)), y_swap(hold(shard_feed)), seq_swap(hold(shard_feed))
    grad_normed = whole_sum(normed_mine[0], normed_came[0], grad_x, grad_y) + hold(grad_d).astype(jnp.float32)
    norm_part, grad_norm = norm_back(inputs_f, scale_in, norm_gain, grad_normed)
    grad_input = norm_part + grad_residual
    small = hold(smalls[0] + smalls[1] + smalls[2] + smalls[3])
    taps = jnp.sum(tap_sums[0] + tap_sums[1] + tap_sums[2] + tap_sums[3], axis=2) * scaling

    def placed(array, total):
        array = array.reshape(-1)
        return lax.dynamic_update_slice(jnp.zeros((total,), jnp.float32), array, (part * array.shape[0],))

    pieces = [
        grad_feed,
        placed(small[:2, :head_size], width),
        placed(hold(taps), head_count * taps_q * taps_k),
        placed(jnp.sum(small[2:6], axis=1), 2 * head_count),
    ]
    lengths = [a.shape[0] for a in pieces]
    fill = -(sum(lengths) + width) % (8 * LANES)
    packed = jnp.concatenate(pieces + [jnp.zeros((fill,), jnp.float32)]).reshape(-1, LANES)
    packed = jnp.concatenate([packed, grad_norm.reshape(-1, LANES)], 0)
    packed = packed + seq_swap(packed)
    if wide & (wide - 1):
        packed = lax.psum(packed, "wide")
    else:
        for hop in [1 << i for i in range(16) if 1 << i < wide]:
            packed = packed + lax.ppermute(packed, "wide", [(i, i ^ hop) for i in range(wide)])
    packed = packed + x_swap(packed)
    flow.end(packed, feed_x, feed_y, feed_o)
    shard_out = out_x = out_y = grad_out_own
    if ring:
        out_sum = wide_block(out_terms, 0).astype(jnp.float32) + sum(hold(a).astype(jnp.float32) for a in out_came)
        shard_out = out_sum.astype(jnp.bfloat16)
    packed = packed + y_swap(hold(packed))
    feed_low, feed_high = y_swap(hold(half_rows(feed_x, False))), x_swap(hold(half_rows(feed_y, True)))
    feed_xo, feed_yo = seq_swap(hold(feed_x)), seq_swap(hold(feed_y))
    block_out = (residual + whole_sum(feed_out[0][0], hold(feed_came[0]), feed_main_x, feed_main_y)).astype(jnp.bfloat16)
    flow.end(feed_low, feed_high, feed_xo, feed_yo, packed, shard_joined, block_out, shard_out)

    joined_x, joined_y, joined_o = x_swap(hold(shard_joined)), y_swap(hold(shard_joined)), seq_swap(hold(shard_joined))
    feed_c = jnp.concatenate([feed_low, feed_high], 0)
    feed_co = seq_swap(hold(feed_c))
    if ring:
        out_x, out_y = x_swap(hold(shard_out)), y_swap(hold(shard_out))
        grad_gate, grad_down = place_feed(
            place, [hold(shard_feed), feed_o, feed_x, feed_xo, feed_y, feed_yo, feed_c, feed_co], chunk
        )
    else:
        every = lax.all_gather(shard_feed, PLANE, axis=0)
        split = every[:, :, : 2 * feed_cols].reshape(cores, shard_feed.shape[0], 2 * wide, chunk)
        grad_gate = jnp.moveaxis(split, 0, 2).reshape(shard_feed.shape[0], -1).astype(jnp.float32)
        split = every[:, :, 2 * feed_cols :].reshape(cores, width // feed_cols, chunk, feed_cols)
        grad_down = jnp.swapaxes(split, 1, 2).reshape(cores * chunk, width).astype(jnp.float32)
        grad_out = scatter_wide(lax.all_gather(grad_out_own, PLANE, axis=0, tiled=True)).astype(jnp.float32)
    flow.end(joined_x, joined_y, joined_o, packed, grad_gate, out_x, out_y)
    joined_low, joined_high = y_swap(hold(half_rows(joined_x, False))), x_swap(hold(half_rows(joined_y, True)))
    if ring:
        out_c = y_swap(hold(out_x))
    joined_xo, joined_yo = seq_swap(hold(joined_x)), seq_swap(hold(joined_y))
    joined_rows = [(shard_joined, joined_o), (joined_x, joined_xo), (joined_y, joined_yo)]
    whole_columns = 2 * group_cols % LANES == 0
    if whole_columns:
        grad_qkv = place_columns(hold(place), [a for k in joined_rows for a in k], 3, group_cols, 4)
        flow.end(joined_low, joined_high, grad_qkv, *([out_c] if ring else []))
    else:
        flow.end(joined_low, joined_high)
    joined_c = jnp.concatenate([joined_low, joined_high], 0)
    joined_co = seq_swap(hold(joined_c))
    if ring:
        quarters = jnp.stack([shard_out, out_x, out_y, out_c])
        grad_out = place_quarters(place, quarters, seq_swap(hold(quarters)))
    if whole_columns:
        grad_qkv = add_columns(place, joined_c, joined_co, grad_qkv, 3, group_cols, 4, 3)
    else:
        every = lax.all_gather(shard_joined, PLANE, axis=0)[:, :, : 3 * group_cols]
        split = every.reshape(cores, shard_joined.shape[0], 3, group_cols)
        grad_qkv = jnp.moveaxis(split, 0, 2).reshape(shard_joined.shape[0], -1).astype(jnp.float32)
    packed = packed.reshape(-1)
    grad_norm = packed[-width:]
    parts = []
    for length in lengths:
        parts.append(packed[:length])
        packed = packed[length:]
    grad_feed, grad_group, grad_kernel, grad_mix = parts
    return (
        block_out,
        grad_input,
        grad_norm,
        grad_qkv,
        grad_kernel.reshape(head_count, taps_q, taps_k),
        grad_mix.reshape(head_count, 2),
        grad_group,
        grad_out,
        grad_feed,
        grad_gate,
        grad_down,
    )


def solution(mesh):
    tokens = P(("narrow", "wide", "seq"), None)
    rows = P("wide", None)
    return jax.shard_map(
        on_device,
        mesh=mesh,
        in_specs=(tokens, P(("narrow", "wide", "seq")), P(), rows, P(), P(), P(), rows, P(), rows, rows, tokens),
        out_specs=(tokens, tokens, P(), rows, P(), P(), P(), rows, P(), rows, rows),
        check_vma=False,
    )
```
